32 devices in a mesh: dp: 4 (over z), ctx: 2 (over y), tp: 4 (over x, core).
Axes of the slice: x: 2, y: 2, z: 4, core: 2. Of those that a mesh axis runs over, the one named last changes fastest.
Arguments:
- hidden_states: bfloat16 [8, 1024, 1024], P('dp', 'ctx'), may hold values from -30 to 30
- out_grad: bfloat16 [8, 1024, 1024], P('dp', 'ctx'), may hold values from -6 to 6
- w_query: bfloat16 [1024, 1024], P('dp', 'tp'), may hold values from -0.1875 to 0.1875
- w_key: bfloat16 [1024, 512], P('dp', 'tp'), may hold values from -0.1875 to 0.1875
- w_value: bfloat16 [1024, 512], P('dp', 'tp'), may hold values from -0.1875 to 0.1875
- w_out: bfloat16 [1024, 1024], P('tp', 'dp'), may hold values from -0.75 to 0.75
- w_gate: bfloat16 [1024, 4608], P('dp', 'tp'), may hold values from -0.1875 to 0.1875
- w_up: bfloat16 [1024, 4608], P('dp', 'tp'), may hold values from -0.1875 to 0.1875
- w_down: bfloat16 [4608, 1024], P('tp', 'dp'), may hold values from -0.09375 to 0.09375
- attn_gain: bfloat16 [1024], P('dp'), may hold values from 0.25 to 1.75
- ffn_gain: bfloat16 [1024], P('dp'), may hold values from 0.25 to 1.75
- query_gain: bfloat16 [64], P('dp'), may hold values from 0.25 to 1.75
- key_gain: bfloat16 [64], P('dp'), may hold values from 0.25 to 1.75
- segment_ids: int32 [8, 1024], P('dp', 'ctx'), may hold values from 0 to 17, as said below
- valid_mask: int32 [8, 1024], P('dp', 'ctx'), may hold values from 0 to 1, as said below
- positions: int32 [8, 1024], P('dp', 'ctx'), may hold values from 0 to 2047, as said below
Outputs:
- result: float32 [8, 1024, 1024], P('dp', ('ctx', 'tp'))
- grad_hidden: float32 [8, 1024, 1024], P('dp', ('ctx', 'tp'))
- grad_w_query: float32 [1024, 1024], P('dp', 'tp')
- grad_w_key: float32 [1024, 512], P('dp', 'tp')
- grad_w_value: float32 [1024, 512], P('dp', 'tp')
- grad_w_out: float32 [1024, 1024], P('tp', 'dp')
- grad_w_gate: float32 [1024, 4608], P('dp', 'tp')
- grad_w_up: float32 [1024, 4608], P('dp', 'tp')
- grad_w_down: float32 [4608, 1024], P('tp', 'dp')
- grad_attn_gain: float32 [1024], P('dp')
- grad_ffn_gain: float32 [1024], P('dp')
- grad_query_gain: float32 [64], P('dp')
- grad_key_gain: float32 [64], P('dp')
- statistics: float32 [4], replicated
The draws below stay inside these ranges and needn't reach their ends.
Inputs may be any that keep to these rules, and one draw needn't show every extreme that they name: `segment_ids`: within each sequence the ids never fall; its last 1 to 128 positions are padding with id 2 * 8 + 1; one document of every sequence covers positions 256 to 768. `valid_mask`: 1 exactly where segment_ids is not the padding id. Within a document consecutive tokens have consecutive positions; every sequence's first document starts at 0; the last token of every sequence has position 2047.
All inputs are finite; a program needn't handle non-finite values.
Results may differ from the reference program's by a relative error of at most 0.02.
Values may be sent and summed in bfloat16 or wider, within the bound.
A program may use at most 128 MiB of HBM per device.

```python
import jax
import jax.numpy as jnp
from jax import lax

D = 1024
HEADS = 16
KV_HEADS = 8
HEAD_DIM = 64
FF = 4608
SEQ_LEN = 1024
CUTS = 8
SEQS = 8


def documents(key):
    key_pad, key_left, key_right, key_offset = jax.random.split(key, 4)
    quarter = SEQ_LEN // 4
    padding = jax.random.randint(key_pad, (SEQS, 1), 1, SEQ_LEN // 8 + 1)
    left_cuts = jax.random.randint(key_left, (SEQS, CUTS), 1, quarter)
    right_cuts = jax.random.randint(key_right, (SEQS, CUTS), 3 * quarter + 1, SEQ_LEN - SEQ_LEN // 8)
    cut_points = jnp.concatenate([left_cuts, right_cuts], axis=1)
    places = jnp.arange(SEQ_LEN, dtype=jnp.int32)
    passed = places[None, :, None] >= cut_points[:, None, :]
    segment = jnp.sum(passed.astype(jnp.int32), axis=-1)
    starts = jnp.max(jnp.where(passed, cut_points[:, None, :], 0), axis=-1)
    valid_rows = (places[None, :] < SEQ_LEN - padding).astype(jnp.int32)
    segment = jnp.where(valid_rows == 1, segment, 2 * CUTS + 1).astype(jnp.int32)
    last_start = jnp.max(cut_points, axis=1)
    offsets = jax.random.randint(key_offset, (SEQS, 2 * CUTS + 2), 0, SEQ_LEN)
    offsets = offsets.at[:, 0].set(0)
    offsets = offsets.at[:, 2 * CUTS + 1].set(SEQ_LEN + last_start)
    shifted = jnp.take_along_axis(offsets, segment, axis=1)
    return (segment, valid_rows, (places[None, :] - starts + shifted).astype(jnp.int32))


def draw_segment_ids(key, part):
    shared = documents(key)
    return shared[0]


def draw_valid_mask(key, part):
    shared = documents(key)
    return shared[1]


def draw_positions(key, part):
    shared = documents(key)
    return shared[2]


def draw_hidden_states(key, part):
    key = jax.random.fold_in(key, 4)
    total_rows = SEQS * SEQ_LEN
    fraction = jnp.arange(total_rows, dtype=jnp.float32) / (total_rows - 1)
    base = jax.random.truncated_normal(key, -5.0, 5.0, (total_rows, D), jnp.float32)
    scale = 3.0 ** fraction
    return (base * scale[:, None]).reshape(SEQS, SEQ_LEN, D).astype(jnp.bfloat16)


def shard_levels(key, extent, cuts, least, largest):
    def one(position, parts):
        steps = jax.random.uniform(jax.random.fold_in(jax.random.fold_in(key, 6), position), (parts,), jnp.float32, least / len(cuts), largest / len(cuts))
        return jnp.repeat(jnp.exp(steps), extent[position] // parts).reshape((-1,) + (1,) * (len(extent) - position - 1))

    level = one(*cuts[0])
    for cut in cuts[1:]:
        level = level * one(*cut)
    return level


def bell_draw(stream_key, shape, width, most, cuts=(), held_as=jnp.bfloat16):
    result = jax.random.normal(stream_key, shape, jnp.float32) * width
    if len(cuts) > 0:
        result = shard_levels(stream_key, shape, cuts, -0.22, 0.18) * result
    return jnp.clip(result, min=-most, max=most).astype(held_as)


def setup_inputs(seed: int = 0) -> dict:
    splits = jax.random.split(jax.random.key(seed), 17)
    return {
        "hidden_states": draw_hidden_states(jax.random.fold_in(splits[16], 71), 0),
        "out_grad": bell_draw(splits[1], (SEQS, SEQ_LEN, D), 1.0, 6.0, ((0, 4), (1, 2))),
        "w_query": bell_draw(splits[2], (D, HEADS * HEAD_DIM), D ** -0.5, 0.1875, ((0, 4), (1, 4))),
        "w_key": bell_draw(splits[3], (D, KV_HEADS * HEAD_DIM), D ** -0.5, 0.1875, ((0, 4), (1, 4))),
        "w_value": bell_draw(splits[4], (D, KV_HEADS * HEAD_DIM), D ** -0.5, 0.1875, ((0, 4), (1, 4))),
        "w_out": bell_draw(splits[5], (HEADS * HEAD_DIM, D), (HEADS * HEAD_DIM // 16) ** -0.5, 0.75, ((0, 4), (1, 4))),
        "w_gate": bell_draw(splits[6], (D, FF), D ** -0.5, 0.1875, ((0, 4), (1, 4))),
        "w_up": bell_draw(splits[7], (D, FF), D ** -0.5, 0.1875, ((0, 4), (1, 4))),
        "w_down": bell_draw(splits[8], (FF, D), FF ** -0.5, 0.09375, ((0, 4), (1, 4))),
        "attn_gain": jnp.clip(1.0 + 0.15 * jax.random.normal(splits[9], (D,), jnp.float32), 0.25, 1.75).astype(jnp.bfloat16),
        "ffn_gain": jnp.clip(1.0 + 0.15 * jax.random.normal(splits[10], (D,), jnp.float32), 0.25, 1.75).astype(jnp.bfloat16),
        "query_gain": jnp.clip(1.0 + 0.15 * jax.random.normal(splits[11], (HEAD_DIM,), jnp.float32), 0.25, 1.75).astype(jnp.bfloat16),
        "key_gain": jnp.clip(1.0 + 0.15 * jax.random.normal(splits[12], (HEAD_DIM,), jnp.float32), 0.25, 1.75).astype(jnp.bfloat16),
        "segment_ids": draw_segment_ids(jax.random.fold_in(splits[16], 71), 0),
        "valid_mask": draw_valid_mask(jax.random.fold_in(splits[16], 71), 0),
        "positions": draw_positions(jax.random.fold_in(splits[16], 71), 0),
    }


EPSILON = 1e-05
ROPE_BASE = 1000000.0
PRECISE = lax.Precision.HIGHEST

@jax.custom_vjp
def low(v):
    return lax.optimization_barrier(v.astype(jnp.bfloat16)).astype(jnp.float32)

@jax.custom_vjp
def low_back(v):
    return v

def low_keep(v):
    return (low(v), None)

def low_pass(kept, grad):
    return (grad,)

def back_keep(v):
    return (v, None)

def back_low(kept, grad):
    return (low(grad),)
low.defvjp(low_keep, low_pass)
low_back.defvjp(back_keep, back_low)

def rms_scale(value, gain):
    return value * lax.rsqrt(lax.optimization_barrier(jnp.mean(value * value, axis=-1, keepdims=True)) + EPSILON) * gain

def rotate(value, places):
    half = value.shape[-1] // 2
    freq = ROPE_BASE ** (-(jnp.arange(half, dtype=jnp.float32) * 2.0) / value.shape[-1])
    angle = places.astype(jnp.float32)[:, None] * freq[None, :]
    cosine = jnp.cos(angle)[:, None, :]
    sine = jnp.sin(angle)[:, None, :]
    first = value[..., :half]
    second = value[..., half:]
    return jnp.concatenate([first * cosine - second * sine, second * cosine + first * sine], axis=-1)

def matmul(left, right):
    return jnp.dot(left, right, precision=PRECISE, preferred_element_type=jnp.float32)

def block(hidden, w_query, w_key, w_value, w_out, w_gate, w_up, w_down, attn_gain, ffn_gain, query_gain, key_gain, seg_row, valid_row, place_row):
    length = hidden.shape[0]
    normed = low(rms_scale(hidden, attn_gain))
    queries = low_back(matmul(normed, w_query)).reshape(length, HEADS, HEAD_DIM)
    keys_raw = low_back(matmul(normed, w_key)).reshape(length, KV_HEADS, HEAD_DIM)
    values = low_back(low(matmul(normed, w_value))).reshape(length, KV_HEADS, HEAD_DIM)
    query_rot = low(rotate(rms_scale(queries, query_gain), place_row)).reshape(length, KV_HEADS, HEADS // KV_HEADS, HEAD_DIM)
    key_rot = low(rotate(rms_scale(keys_raw, key_gain), place_row))
    scores = jnp.einsum('qhgd,khd->hgqk', query_rot, key_rot, precision=PRECISE) * HEAD_DIM ** (-0.5)
    scores = low_back(scores)
    index = jnp.arange(length)
    allowed = (seg_row[:, None] == seg_row[None, :]) & (index[None, :] <= index[:, None]) & ((valid_row[None, :] == 1) | (index[None, :] == index[:, None]))
    scores = jnp.where(allowed, scores, -1e+30)
    highest = lax.optimization_barrier(jnp.max(scores, axis=-1, keepdims=True))
    expo = jnp.exp(scores - highest)
    probs = low(expo / lax.optimization_barrier(jnp.sum(expo, axis=-1, keepdims=True)))
    output = jnp.einsum('hgqk,khd->qhgd', probs, values, precision=PRECISE).reshape(length, HEADS * HEAD_DIM)
    output = low_back(low(output))
    attn = low_back(matmul(output, w_out))
    middle = hidden + attn
    normed_mid = low(rms_scale(middle, ffn_gain))
    gate = low_back(matmul(normed_mid, w_gate))
    upward = low_back(matmul(normed_mid, w_up))
    inner = low(gate * jax.nn.sigmoid(gate) * upward)
    mlp = low_back(matmul(inner, w_down))
    return (middle + mlp, (attn, middle, mlp))

def reference(hidden_states, out_grad, w_query, w_key, w_value, w_out, w_gate, w_up, w_down, attn_gain, ffn_gain, query_gain, key_gain, segment_ids, valid_mask, positions):
    weights = (w_query.astype(jnp.float32), w_key.astype(jnp.float32), w_value.astype(jnp.float32), w_out.astype(jnp.float32), w_gate.astype(jnp.float32), w_up.astype(jnp.float32), w_down.astype(jnp.float32), attn_gain.astype(jnp.float32), ffn_gain.astype(jnp.float32), query_gain.astype(jnp.float32), key_gain.astype(jnp.float32))

    def one_sequence(carry, item):
        hidden_bf, grad_bf, seg_row, valid_row, place_row = item
        hidden = hidden_bf.astype(jnp.float32)

        def forward(hidden_in, *params):
            return block(hidden_in, *params, seg_row, valid_row, place_row)
        output, pull_back, extras = jax.vjp(forward, hidden, *weights, has_aux=True)
        attn, middle, mlp = extras
        grads = pull_back(grad_bf.astype(jnp.float32))
        keep = valid_row.astype(jnp.float32)[:, None]
        squares = jnp.stack([jnp.sum(keep * hidden * hidden), jnp.sum(keep * attn * attn), jnp.sum(keep * middle * middle), jnp.sum(keep * mlp * mlp)])
        summed = tuple((total + piece for total, piece in zip(carry[0], grads[1:])))
        return ((summed, carry[1] + squares, carry[2] + jnp.sum(valid_row.astype(jnp.float32))), (output, grads[0]))
    start = (tuple((jnp.zeros(w.shape, jnp.float32) for w in weights)), jnp.zeros((4,), jnp.float32), jnp.zeros((), jnp.float32))
    (wgrads, squares, count), (outputs, grad_inputs) = lax.scan(one_sequence, start, (hidden_states, out_grad, segment_ids, valid_mask, positions))
    statistics = jnp.sqrt(squares / (count * D))
    return (outputs, grad_inputs, wgrads[0], wgrads[1], wgrads[2], wgrads[3], wgrads[4], wgrads[5], wgrads[6], wgrads[7], wgrads[8], wgrads[9], wgrads[10], statistics)
```

```python
import jax
import jax.numpy as jnp
from jax import lax
from jax.sharding import PartitionSpec as P

EPSILON = 1e-05
ROPE_BASE = 1000000.0
F32 = jnp.float32
BF16 = jnp.bfloat16


def norm_rows(value):
    factor = lax.rsqrt(jnp.mean(value * value, axis=-1, keepdims=True) + EPSILON)
    return (value * factor, factor)


def norm_back(incoming, normed_hat, factor, gain):
    grad_hat = incoming * gain
    return factor * (
        grad_hat - normed_hat * jnp.mean(grad_hat * normed_hat, axis=-1, keepdims=True)
    )


def rope_tables(places, half):
    freq = ROPE_BASE ** (-(jnp.arange(half, dtype=F32) * 2.0) / (2 * half))
    angle = places.astype(F32)[:, None] * freq[None, :]
    return (jnp.cos(angle)[:, None, :], jnp.sin(angle)[:, None, :])


def rotate(value, cosine, sine, direction):
    half = value.shape[-1] // 2
    first = value[..., :half]
    second = value[..., half:]
    return jnp.concatenate(
        [first * cosine - direction * second * sine, second * cosine + direction * first * sine],
        axis=-1,
    )


def product(left, right):
    return jnp.dot(left, right, preferred_element_type=F32)


def product_tn(left, right):
    return lax.dot_general(left, right, (((0,), (0,)), ((), ())), preferred_element_type=F32)


def product_nt(left, right):
    return lax.dot_general(left, right, (((1,), (1,)), ((), ())), preferred_element_type=F32)


def shift_send(value, axis, step):
    size = lax.axis_size(axis)
    return lax.ppermute(value, axis, [(i, (i + step) % size) for i in range(size)])


def put(buffer, piece, *starts):
    return lax.dynamic_update_slice(buffer, piece, tuple(starts) + (0,) * (buffer.ndim - len(starts)))


def take(value, index, axis):
    return lax.dynamic_index_in_dim(value, index, axis, keepdims=False)


def gather_weight(shard):
    parts, halves = lax.axis_size("dp"), lax.axis_size("ctx")
    me, side = lax.axis_index("dp"), lax.axis_index("ctx")
    rows, width = shard.shape
    split = shard.reshape(halves, rows // halves, width)
    mine = take(split, side, 0)
    whole = jnp.zeros((parts, halves, rows // halves, width), shard.dtype)
    whole = put(whole, split[None], me)
    for step in range(1, parts):
        piece = shift_send(mine, "dp", step)
        owner = (me - step) % parts
        whole = put(whole, piece[None, None], owner, side)
        for turn in range(1, halves):
            other = shift_send(piece, "ctx", turn)
            whole = put(whole, other[None, None], owner, (side - turn) % halves)
    return whole.reshape(parts * rows, width)


def scatter_weight(grad):
    parts, halves = lax.axis_size("dp"), lax.axis_size("ctx")
    me, side = lax.axis_index("dp"), lax.axis_index("ctx")
    rows, width = grad.shape
    rows = rows // (parts * halves)
    low = grad.astype(BF16).reshape(parts, halves, rows, width)
    total = take(low, side, 1).astype(F32)
    for turn in range(1, halves):
        total += shift_send(take(low, (side + turn) % halves, 1), "ctx", turn).astype(F32)
    low = total.astype(BF16)
    mine = take(low, me, 0).astype(F32)
    for step in range(1, parts):
        mine += shift_send(take(low, (me + step) % parts, 0), "dp", step).astype(F32)
    mine = mine.astype(BF16)
    whole = jnp.zeros((halves, rows, width), BF16)
    whole = put(whole, mine[None], side)
    for turn in range(1, halves):
        whole = put(whole, shift_send(mine, "ctx", turn)[None], (side - turn) % halves)
    return whole.reshape(halves * rows, width).astype(F32)


def tp_pairs(size):
    return [(i, i ^ 1) for i in range(size)]


def tp_chip(size, step):
    return [(i, (i + 2 * step) % size) for i in range(size)]


def tp_scatter(value):
    size, me = lax.axis_size("tp"), lax.axis_index("tp")
    seqs, tokens, width = value.shape
    core, chip, chips = me % 2, me // 2, size // 2
    low = value.astype(BF16).reshape(seqs, chips, 2, tokens // size, width)
    total = take(low, core, 2).astype(F32) + lax.ppermute(
        take(low, 1 - core, 2), "tp", tp_pairs(size)
    ).astype(F32)
    low = total.astype(BF16)
    mine = take(low, chip, 1).astype(F32)
    for step in range(1, chips):
        piece = take(low, (chip + step) % chips, 1)
        mine += lax.ppermute(piece, "tp", tp_chip(size, step)).astype(F32)
    return mine


def tp_gather(value):
    size, me = lax.axis_size("tp"), lax.axis_index("tp")
    seqs, share, width = value.shape
    core, chip, chips = me % 2, me // 2, size // 2
    whole = jnp.zeros((seqs, chips, 2, share, width), value.dtype)
    pair = jnp.zeros((seqs, chips, share, width), value.dtype)
    pair = put(pair, value[:, None], 0, chip)
    for step in range(1, chips):
        piece = lax.ppermute(value, "tp", tp_chip(size, step))
        pair = put(pair, piece[:, None], 0, (chip - step) % chips)
    other = lax.ppermute(pair, "tp", tp_pairs(size))
    whole = put(whole, pair[:, :, None], 0, 0, core)
    whole = put(whole, other[:, :, None], 0, 0, 1 - core)
    return whole.reshape(seqs, size * share, width)


def tiles_of(width):
    return 3 if width % 3 == 0 else 1


def per_device(
    hidden_states,
    out_grad,
    w_query,
    w_key,
    w_value,
    w_out,
    w_gate,
    w_up,
    w_down,
    attn_gain,
    ffn_gain,
    query_gain,
    key_gain,
    segment_ids,
    valid_mask,
    positions,
):
    seqs, local_len, width = hidden_states.shape
    rows = seqs * local_len
    share_len = local_len // lax.axis_size("tp")
    share_start = lax.axis_index("tp") * share_len
    nq, nk = w_query.shape[1], w_key.shape[1]
    hidden_units = w_gate.shape[1]
    tiles = tiles_of(hidden_units)
    tile = hidden_units // tiles

    gains = lax.all_gather(
        jnp.concatenate([attn_gain, ffn_gain, query_gain, key_gain]), "dp", axis=0
    ).astype(F32)
    marks = []
    start = 0
    for gain in (attn_gain, ffn_gain, query_gain, key_gain):
        marks.append(gains[:, start : start + gain.shape[0]].reshape(-1))
        start += gain.shape[0]
    gain_attn, gain_ffn, gain_query, gain_key = marks

    mat_attn = gather_weight(jnp.concatenate([w_query, w_key, w_value, w_out.T], axis=1))
    mat_ffn = []
    for i in range(tiles):
        cut = slice(i * tile, (i + 1) * tile)
        mat_ffn.append(
            gather_weight(jnp.concatenate([w_gate[:, cut], w_up[:, cut], w_down[cut].T], axis=1))
        )
    mat_qkv, mat_out_t = mat_attn[:, : nq + 2 * nk], mat_attn[:, nq + 2 * nk :]

    head_dim = gain_query.shape[0]
    q_heads, kv_heads = nq // head_dim, nk // head_dim
    group = q_heads // kv_heads
    scale_factor = head_dim ** (-0.5)

    def share_rows(value):
        return lax.dynamic_slice_in_dim(value, share_start, share_len, 1)

    hidden = hidden_states.astype(F32).reshape(rows, width)
    hidden_hat, hidden_factor = norm_rows(hidden)
    normed = (hidden_hat * gain_attn).astype(BF16)
    qkv = product(normed, mat_qkv)
    query_pre = qkv[:, :nq].reshape(rows, q_heads, head_dim)
    key_pre = qkv[:, nq : nq + nk].reshape(rows, kv_heads, head_dim)
    value_low = qkv[:, nq + nk :].astype(BF16)
    cosine, sine = rope_tables(positions.reshape(rows), head_dim // 2)
    query_hat, query_factor = norm_rows(query_pre)
    query_rot = rotate(query_hat * gain_query, cosine, sine, 1.0).astype(BF16)
    key_hat, key_factor = norm_rows(key_pre)
    key_rot = rotate(key_hat * gain_key, cosine, sine, 1.0).astype(BF16)
    halves, side = lax.axis_size("ctx"), lax.axis_index("ctx")
    full_len = halves * local_len

    def ctx_gather(value):
        whole = jnp.zeros((seqs, halves) + value.shape[1:], value.dtype)
        whole = put(whole, value[:, None], 0, side)
        for turn in range(1, halves):
            whole = put(whole, shift_send(value, "ctx", turn)[:, None], 0, (side - turn) % halves)
        return whole.reshape((seqs, full_len) + value.shape[2:])

    kv_low = jnp.concatenate([key_rot.reshape(rows, nk), value_low], axis=1)
    all_kv = ctx_gather(kv_low.reshape(seqs, local_len, 2 * nk))
    all_keys, all_values = all_kv[..., :nk], all_kv[..., nk:]
    key_facts = ctx_gather(jnp.stack([segment_ids, valid_mask], axis=-1))
    key_segments, key_valid = key_facts[..., 0], key_facts[..., 1]
    query_index = side * local_len + jnp.arange(local_len)
    key_index = jnp.arange(full_len)
    queries = query_rot.reshape(seqs, local_len, kv_heads, group, head_dim)

    def allowed_of(query_seg, key_seg, key_flag):
        same = query_seg[:, None] == key_seg[None, :]
        causal = key_index[None, :] <= query_index[:, None]
        itself = key_index[None, :] == query_index[:, None]
        return same & causal & ((key_flag[None, :] == 1) | itself)

    def masked_scores(query_blk, key_blk, query_seg, key_seg, key_flag):
        scores = (
            jnp.einsum("qhgd,khd->hgqk", query_blk, key_blk, preferred_element_type=F32)
            * scale_factor
        )
        return jnp.where(allowed_of(query_seg, key_seg, key_flag)[None, None], scores, -1e30)

    def attend(item):
        query_blk, key_flat, value_flat, query_seg, key_seg, key_flag = item
        key_blk = key_flat.reshape(full_len, kv_heads, head_dim)
        value_blk = value_flat.reshape(full_len, kv_heads, head_dim)
        scores = masked_scores(query_blk, key_blk, query_seg, key_seg, key_flag)
        highest = jnp.max(scores, axis=-1, keepdims=True)
        expo = jnp.exp(scores - highest)
        totals = jnp.sum(expo, axis=-1, keepdims=True)
        probs_low = (expo / totals).astype(BF16)
        output = jnp.einsum("hgqk,khd->qhgd", probs_low, value_blk, preferred_element_type=F32)
        return (
            output.astype(BF16).reshape(local_len, q_heads * head_dim),
            highest[..., 0] + jnp.log(totals[..., 0]),
        )

    attn_out, log_totals = lax.map(
        attend, (queries, all_keys, all_values, segment_ids, key_segments, key_valid)
    )
    attn_out = attn_out.reshape(rows, q_heads * head_dim)
    attn_part = product_nt(attn_out, mat_out_t).reshape(seqs, local_len, width)
    attn_s = tp_scatter(attn_part)
    hidden_s = share_rows(hidden_states).astype(F32)
    middle_s = hidden_s + attn_s
    mid_hat_s, mid_factor_s = norm_rows(middle_s)
    normed_mid = tp_gather((mid_hat_s * gain_ffn).astype(BF16)).reshape(rows, width)

    grad_low = out_grad.reshape(rows, width)
    mlp_part = jnp.zeros((rows, width), F32)
    back_part = jnp.zeros((rows, width), F32)
    ffn_grads = []
    for mat in mat_ffn:
        both, mat_down_t = mat[:, : 2 * tile], mat[:, 2 * tile :]
        pre = product(normed_mid, both)
        gate, upward = pre[:, :tile], pre[:, tile:]
        sigmoid_gate = jax.nn.sigmoid(gate)
        inner = (gate * sigmoid_gate * upward).astype(BF16)
        grad_inner = product(grad_low, mat_down_t)
        grad_gate = (
            grad_inner * upward * sigmoid_gate * (1.0 + gate * (1.0 - sigmoid_gate))
        ).astype(BF16)
        grad_upward = (grad_inner * gate * sigmoid_gate).astype(BF16)
        mlp_part += product_nt(inner, mat_down_t)
        grad_both = jnp.concatenate([grad_gate, grad_upward], axis=1)
        back_part += product_nt(grad_both, both)
        ffn_grads.append(
            scatter_weight(
                jnp.concatenate(
                    [product_tn(normed_mid, grad_both), product_tn(grad_low, inner)], axis=1
                )
            )
        )
    grad_nm_s = tp_scatter(back_part.reshape(seqs, local_len, width))
    grad_out_s = share_rows(out_grad).astype(F32)
    grad_middle_s = grad_out_s + norm_back(grad_nm_s, mid_hat_s, mid_factor_s, gain_ffn)
    grad_attn_low = tp_gather(grad_middle_s.astype(BF16)).reshape(rows, width)
    ffn_part = jnp.sum(grad_nm_s * mid_hat_s, axis=(0, 1))
    mlp_s = tp_scatter(mlp_part.reshape(seqs, local_len, width))
    result_s = middle_s + mlp_s
    keep_s = share_rows(valid_mask[..., None]).astype(F32)
    squares = jnp.stack(
        [
            jnp.sum(keep_s * hidden_s * hidden_s),
            jnp.sum(keep_s * attn_s * attn_s),
            jnp.sum(keep_s * middle_s * middle_s),
            jnp.sum(keep_s * mlp_s * mlp_s),
        ]
    )
    grad_wout_t = product_tn(grad_attn_low, attn_out)
    grad_attn_out = (
        product(grad_attn_low, mat_out_t)
        .astype(BF16)
        .reshape(seqs, local_len, kv_heads, group, head_dim)
    )

    def attend_back(item):
        query_blk, key_flat, value_flat, query_seg, key_seg, key_flag, log_total, grad_blk = item
        key_blk = key_flat.reshape(full_len, kv_heads, head_dim)
        value_blk = value_flat.reshape(full_len, kv_heads, head_dim)
        scores = masked_scores(query_blk, key_blk, query_seg, key_seg, key_flag)
        probs = jnp.exp(scores - log_total[..., None])
        probs_low = probs.astype(BF16)
        grad_value = jnp.einsum(
            "hgqk,qhgd->khd", probs_low, grad_blk, preferred_element_type=F32
        )
        grad_probs = jnp.einsum(
            "qhgd,khd->hgqk", grad_blk, value_blk, preferred_element_type=F32
        )
        row_dot = jnp.sum(probs * grad_probs, axis=-1, keepdims=True)
        grad_scores = (probs * (grad_probs - row_dot)).astype(BF16)
        grad_query = (
            jnp.einsum("hgqk,khd->qhgd", grad_scores, key_blk, preferred_element_type=F32)
            * scale_factor
        )
        grad_key = (
            jnp.einsum("hgqk,qhgd->khd", grad_scores, query_blk, preferred_element_type=F32)
            * scale_factor
        )
        return (
            grad_query,
            grad_key.reshape(full_len, kv_heads * head_dim),
            grad_value.reshape(full_len, kv_heads * head_dim),
        )

    grad_queries, grad_keys_all, grad_values_all = lax.map(
        attend_back,
        (
            queries,
            all_keys,
            all_values,
            segment_ids,
            key_segments,
            key_valid,
            log_totals,
            grad_attn_out,
        ),
    )
    grad_kv_all = (
        jnp.concatenate([grad_keys_all, grad_values_all], axis=-1)
        .astype(BF16)
        .reshape(seqs, halves, local_len, 2 * nk)
    )
    grad_kv = take(grad_kv_all, side, 1).astype(F32)
    for turn in range(1, halves):
        piece = take(grad_kv_all, (side + turn) % halves, 1)
        grad_kv += shift_send(piece, "ctx", turn).astype(F32)
    grad_keys, grad_values = grad_kv[..., :nk], grad_kv[..., nk:]
    grad_query_norm = rotate(grad_queries.reshape(rows, q_heads, head_dim), cosine, sine, -1.0)
    grad_key_norm = rotate(grad_keys.reshape(rows, kv_heads, head_dim), cosine, sine, -1.0)
    grad_gq_part = jnp.sum(grad_query_norm * query_hat, axis=(0, 1))
    grad_gk_part = jnp.sum(grad_key_norm * key_hat, axis=(0, 1))
    grad_query_low = (
        norm_back(grad_query_norm, query_hat, query_factor, gain_query)
        .astype(BF16)
        .reshape(rows, nq)
    )
    grad_key_low = (
        norm_back(grad_key_norm, key_hat, key_factor, gain_key).astype(BF16).reshape(rows, nk)
    )
    grad_value_low = grad_values.astype(BF16).reshape(rows, nk)
    grad_qkv = jnp.concatenate([grad_query_low, grad_key_low, grad_value_low], axis=1)
    attn_grads = scatter_weight(
        jnp.concatenate([product_tn(normed, grad_qkv), grad_wout_t], axis=1)
    )
    grad_normed_s = tp_scatter(product_nt(grad_qkv, mat_qkv).reshape(seqs, local_len, width))
    hidden_hat_s, hidden_factor_s = norm_rows(hidden_s)
    attn_g_part = jnp.sum(grad_normed_s * hidden_hat_s, axis=(0, 1))
    grad_hidden_s = grad_middle_s + norm_back(
        grad_normed_s, hidden_hat_s, hidden_factor_s, gain_attn
    )
    packed = jnp.concatenate(
        [
            attn_g_part,
            ffn_part,
            grad_gq_part,
            grad_gk_part,
            squares,
            jnp.sum(keep_s)[None],
        ]
    )
    packed = lax.psum(packed, ("dp", "ctx", "tp"))
    grad_attn_full, grad_ffn_full = packed[:width], packed[width : 2 * width]
    rest = packed[2 * width :]
    grad_gq_full, grad_gk_full = rest[:head_dim], rest[head_dim : 2 * head_dim]
    square_sums, count = rest[2 * head_dim : 2 * head_dim + 4], rest[2 * head_dim + 4]
    statistics = jnp.sqrt(square_sums / (count * width))
    owner = lax.axis_index("dp")

    def own(value, like):
        size = like.shape[0]
        return lax.dynamic_slice_in_dim(value, owner * size, size, 0)

    return (
        result_s,
        grad_hidden_s,
        attn_grads[:, :nq],
        attn_grads[:, nq : nq + nk],
        attn_grads[:, nq + nk : nq + 2 * nk],
        attn_grads[:, nq + 2 * nk :].T,
        jnp.concatenate([g[:, :tile] for g in ffn_grads], axis=1),
        jnp.concatenate([g[:, tile : 2 * tile] for g in ffn_grads], axis=1),
        jnp.concatenate([g[:, 2 * tile :].T for g in ffn_grads], axis=0),
        own(grad_attn_full, attn_gain),
        own(grad_ffn_full, ffn_gain),
        own(grad_gq_full, query_gain),
        own(grad_gk_full, key_gain),
        statistics,
    )


def solution(mesh):
    return jax.shard_map(
        per_device,
        mesh=mesh,
        in_specs=(
            P("dp", "ctx", None),
            P("dp", "ctx", None),
            P("dp", "tp"),
            P("dp", "tp"),
            P("dp", "tp"),
            P("tp", "dp"),
            P("dp", "tp"),
            P("dp", "tp"),
            P("tp", "dp"),
            P("dp"),
            P("dp"),
            P("dp"),
            P("dp"),
            P("dp", "ctx"),
            P("dp", "ctx"),
            P("dp", "ctx"),
        ),
        out_specs=(
            P("dp", ("ctx", "tp"), None),
            P("dp", ("ctx", "tp"), None),
            P("dp", "tp"),
            P("dp", "tp"),
            P("dp", "tp"),
            P("tp", "dp"),
            P("dp", "tp"),
            P("dp", "tp"),
            P("tp", "dp"),
            P("dp"),
            P("dp"),
            P("dp"),
            P("dp"),
            P(),
        ),
        check_vma=False,
    )
```

```python
import functools

import jax
import jax.numpy as jnp
from jax import lax
from jax.experimental import pallas as pl
from jax.experimental.pallas import tpu as pltpu
from jax.sharding import PartitionSpec as P

EPSILON = 1e-05
ROPE_BASE = 1000000.0
F32 = jnp.float32
BF16 = jnp.bfloat16
MESH = pl.DeviceIdType.MESH
NEGATIVE = -1e30


def dot(left, right):
    return jnp.dot(left, right, preferred_element_type=F32)


def dot_nt(left, right):
    return lax.dot_general(left, right, (((1,), (1,)), ((), ())), preferred_element_type=F32)


def each(count, body):
    def step(i, carry):
        body(i)
        return carry

    lax.fori_loop(0, count, step, 0)


def aligned(index, unit):
    return pl.multiple_of(index * unit, unit)


def mean_square(value):
    return jnp.mean(value * value, axis=-1, keepdims=True)


def swap_halves(value):
    half = value.shape[-1] // 2
    return jnp.concatenate([value[:, half:], value[:, :half]], axis=1)


def fold_lanes(value):
    total = jnp.sum(value, axis=0, keepdims=True)
    out = total[:, :128]
    for i in range(1, value.shape[1] // 128):
        out += total[:, i * 128 : (i + 1) * 128]
    return out


class Copy:
    def __init__(self, src, dst, sems, index, device):
        self.copy = pltpu.make_async_remote_copy(
            src_ref=src,
            dst_ref=dst,
            send_sem=sems[0].at[index],
            recv_sem=sems[1].at[index],
            device_id=device,
            device_id_type=MESH,
        )

    def start(self):
        self.copy.start()

    def wait_send(self):
        self.copy.wait_send()

    def wait_recv(self):
        self.copy.wait_recv()


def block_kernel(cfg, names, *refs):
    r = dict(zip(names, refs))
    seqs, local, width, head = cfg["seqs"], cfg["local"], cfg["width"], cfg["head"]
    dp, ctx, tp = cfg["dp"], cfg["ctx"], cfg["tp"]
    qh, kh, nt, ft = cfg["qh"], cfg["kh"], cfg["nt"], cfg["ft"]
    nq, nk = qh * head, kh * head
    nqkv = nq + 2 * nk
    group = qh // kh
    chips = tp // 2
    rows = seqs * local
    share = local // tp
    dd = width // dp
    hd = dd // ctx
    me, side, lane = lax.axis_index("dp"), lax.axis_index("ctx"), lax.axis_index("tp")
    core, chip = lax.rem(lane, 2), lax.div(lane, 2)
    other_core = lane + 1 - 2 * core
    peer = 1 - side
    rb = min(256, local)
    qb = min(256, local)
    tb = min(128, local)
    scale = head**-0.5

    def sems(name):
        return (r[name + "_s"], r[name + "_r"])

    def dp_at(step):
        return lax.rem(me + step, dp)

    def chip_lane(step):
        return lax.rem(chip + step, chips) * 2 + core

    barrier = pltpu.get_barrier_semaphore()
    greet = [{"dp": dp_at(s)} for s in range(1, dp)] + [{"ctx": peer}, {"tp": other_core}]
    greet += [{"tp": chip_lane(s)} for s in range(1, chips)]
    for device in greet:
        pl.semaphore_signal(barrier, inc=1, device_id=device, device_id_type=MESH)
    pl.semaphore_wait(barrier, len(greet))

    shards = [r["w_qkv"], r["w_o"]] + [r["w_f"].at[t] for t in range(nt)]
    whole = [r["mat_q"], r["mat_o"]] + [r["mat_f"].at[t] for t in range(nt)]

    def my_rows(owner, which):
        return pl.ds(pl.multiple_of(owner * dd + which * hd, hd), hd)

    def ag_z(c, step):
        return Copy(
            shards[c].at[pl.ds(aligned(side, hd), hd)],
            whole[c].at[my_rows(me, side)],
            sems("agz"),
            (c, step - 1),
            {"dp": dp_at(step)},
        )

    def ag_y(c, step):
        owner = lax.rem(me - step + dp, dp)
        area = whole[c].at[my_rows(owner, side)]
        return Copy(area, area, sems("agy"), (c, step - 1), {"ctx": peer})

    def own_copy(c):
        return pltpu.make_async_copy(
            shards[c], whole[c].at[pl.ds(aligned(me, dd), dd)], r["own_sem"].at[c]
        )

    def ag_start(c):
        for step in range(1, dp):
            ag_z(c, step).start()

    def ag_pass(c):
        for step in range(1, dp):
            ag_z(c, step).wait_recv()
            ag_y(c, step).start()

    def ag_end(c):
        own_copy(c).wait()
        for step in range(1, dp):
            ag_y(c, step).wait_recv()
            ag_y(c, step).wait_send()
            ag_z(c, step).wait_send()

    gain_buf = r["gain_buf"]

    def gain_copy(step):
        return Copy(
            r["gains"], gain_buf.at[me], sems("gain"), step - 1, {"dp": dp_at(step)}
        )

    def code_copy():
        return Copy(r["codes"], r["code_peer"], sems("code"), 0, {"ctx": peer})

    for step in range(1, dp):
        gain_copy(step).start()
    code_copy().start()
    ag_start(0)
    ag_start(1)
    for c in range(nt + 2):
        own_copy(c).start()

    x, dy, hn, hn_t, dr_t = r["x"], r["dy"], r["hn"], r["hn_t"], r["dr_t"]

    def transpose_into(source, target, first, count):
        def one(i):
            at = pl.ds(pl.multiple_of(first + i * tb, tb), tb)
            target[:, at] = source[at, :].astype(F32).T.astype(BF16)

        each(count, one)

    transpose_into(dy, dr_t, 0, rows // tb)

    def code_columns(source, which):
        for s in range(seqs):
            row = jnp.broadcast_to(source[s], (128, local))
            r["key_code"][which, s] = row.T

    code_columns(r["codes"], 0)
    gain_buf[pl.ds(me, 1)] = r["gains"][...][None]
    for step in range(1, dp):
        gain_copy(step).wait_recv()
        gain_copy(step).wait_send()
    piece = head // dp
    for d in range(dp):
        r["gain_w"][0:2, d * dd : (d + 1) * dd] = gain_buf[d, 0:2, :]
        r["gain_h"][0:2, d * piece : (d + 1) * piece] = gain_buf[d, 2:4, :piece]

    def normed_into(target, first, count):
        def one(i):
            at = pl.ds(pl.multiple_of(first + i * tb, tb), tb)
            value = x[at, :].astype(F32)
            value = value * lax.rsqrt(mean_square(value) + EPSILON)
            target[at, :] = (value * r["gain_w"][0:1, :]).astype(BF16)

        each(count, one)

    normed_into(hn, 0, rows // tb)
    code_copy().wait_recv()
    code_copy().wait_send()
    code_columns(r["code_peer"], 1)
    ag_pass(0)
    ag_start(2)
    ag_end(0)

    mat_q, mat_o, raw, tab = r["mat_q"], r["mat_o"], r["raw"], r["tab"]
    q_pad, kv, kv_t = r["q_pad"], r["kv"], r["kv_t"]

    def project(s):
        def one(i):
            at = pl.ds(pl.multiple_of(s * local + i * rb, rb), rb)
            inner = pl.ds(aligned(i, rb), rb)
            both = dot(hn[at, :], mat_q[...])
            raw[at, :] = both[:, : nq + nk]
            cosine, sine = tab[at, :head], tab[at, head : 2 * head]

            def turned(start, which):
                value = both[:, start : start + head]
                value = value * lax.rsqrt(mean_square(value) + EPSILON)
                value = value * r["gain_h"][which : which + 1, :]
                return value * cosine + swap_halves(value) * sine

            for h in range(qh):
                value = turned(h * head, 0) * scale
                q_pad[s * qh + h, inner, :] = jnp.concatenate(
                    [value, jnp.zeros_like(value)], axis=1
                ).astype(BF16)
            for h in range(kh):
                value = turned(nq + h * head, 1)
                low = both[:, nq + nk + h * head : nq + nk + (h + 1) * head]
                kv[s * kh + h, 0, inner, :] = jnp.concatenate([value, low], axis=1).astype(BF16)

        each(local // rb, one)

    def kv_copy(s):
        return Copy(
            kv.at[pl.ds(s * kh, kh), 0],
            kv.at[pl.ds(s * kh, kh), 1],
            sems("kv"),
            s,
            {"ctx": peer},
        )

    def kv_transpose(s, which):
        for h in range(kh):
            kv_t[s * kh + h, which] = kv[s * kh + h, which].astype(F32).T.astype(BF16)

    for s in range(seqs):
        project(s)

        @pl.when(side == 0)
        def _():
            kv_copy(s).start()

        kv_transpose(s, 0)
    ag_pass(1)
    ag_start(3) if nt > 1 else None

    o_t, lse = r["o_t"], r["lse"]

    def masked(s, j, index, with_peer):
        last = (j + 1) * qb
        head_kv = s * kh + index // group
        here = q_pad[s * qh + index, j * qb : last, :]
        query = r["codes"][s][:, j * qb : last]

        def spread(code):
            return jnp.concatenate([code] * (qb // 128), axis=1)

        own = dot_nt(kv[head_kv, 0, :last, :], here)
        key_at = lax.broadcasted_iota(jnp.int32, (last, qb), 0)
        query_at = lax.broadcasted_iota(jnp.int32, (last, qb), 1) + j * qb
        allowed = (spread(r["key_code"][0, s, :last, :]) == query) & (key_at <= query_at)
        own = jnp.where(allowed, own, NEGATIVE)
        parts = [(own, 0, last)]
        if with_peer:
            far = dot_nt(kv[head_kv, 1], here)
            far = jnp.where(spread(r["key_code"][1, s]) == query, far, NEGATIVE)
            parts.append((far, 1, local))
        return parts, head_kv, here

    def attend(s, first, count, with_peer):
        def one(i):
            index = first + i
            for j in range(local // qb):
                parts, head_kv, _ = masked(s, j, index, with_peer)
                highest = functools.reduce(
                    jnp.maximum, [jnp.max(p[0], axis=0, keepdims=True) for p in parts]
                )
                expo = [jnp.exp(p[0] - highest) for p in parts]
                total = sum(jnp.sum(e, axis=0, keepdims=True) for e in expo)
                factor = 1.0 / total
                out = jnp.zeros((2 * head, qb), F32)
                for (_, which, size), e in zip(parts, expo):
                    out += dot(kv_t[head_kv, which, :, :size], (e * factor).astype(BF16))
                at = pl.ds(pl.multiple_of(index * head, head), head)
                o_t[s, at, j * qb : (j + 1) * qb] = out[head:, :].astype(BF16)
                lse[s * qh + index, :, j * qb : (j + 1) * qb] = highest + jnp.log(total)

        each(count, one)

    def attend_any(s, first, count):
        @pl.when(side == 0)
        def _():
            attend(s, first, count, False)

        @pl.when(side != 0)
        def _():
            attend(s, first, count, True)

    def kv_arrive(s):
        @pl.when(side == 0)
        def _():
            kv_copy(s).wait_send()

        @pl.when(side != 0)
        def _():
            kv_copy(s).wait_recv()
            kv_transpose(s, 1)

    part, near, pair, far = r["part"], r["near"], r["pair"], r["far"]

    def pool(use):
        return 1 if use == 3 else 0

    def token_rows(s, which_chip, which_core):
        start = s * local + (which_chip * 2 + which_core) * share
        return pl.ds(pl.multiple_of(start, share), share)

    def sum1(use, s, c):
        return Copy(
            part.at[token_rows(s, c, 1 - core)],
            near.at[pool(use), s, c],
            sems("sum1"),
            (use, s * chips + c),
            {"tp": other_core},
        )

    def sum1_start(use, s):
        for c in range(chips):
            sum1(use, s, c).start()

    def sum2(use, s, step):
        return Copy(
            pair.at[s, lax.rem(chip + step, chips)],
            far.at[pool(use), s, step - 1],
            sems("sum2"),
            (use, s * max(chips - 1, 1) + step - 1),
            {"tp": chip_lane(step)},
        )

    def sum2_start(use, s):
        for c in range(chips):
            sum1(use, s, c).wait_recv()
        for c in range(chips):
            mine = part[token_rows(s, c, core), :].astype(F32)
            pair[s, c] = (mine + near[pool(use), s, c].astype(F32)).astype(BF16)
        for step in range(1, chips):
            sum2(use, s, step).start()

    def sum_end(use, s):
        for step in range(1, chips):
            sum2(use, s, step).wait_recv()
        total = part[token_rows(s, chip, core), :].astype(F32)
        total += near[pool(use), s, chip].astype(F32)
        for step in range(1, chips):
            total += far[pool(use), s, step - 1].astype(F32)
        for c in range(chips):
            sum1(use, s, c).wait_send()
        for step in range(1, chips):
            sum2(use, s, step).wait_send()
        return total

    def spread1(use, s, step):
        area = hn.at[token_rows(s, chip, core)]
        index = (use, s * max(chips - 1, 1) + step - 1)
        return Copy(area, area, sems("spread1"), index, {"tp": chip_lane(step)})

    def spread1_start(use, s, value):
        hn[token_rows(s, chip, core), :] = value
        for step in range(1, chips):
            spread1(use, s, step).start()

    def spread2(use, s, c):
        area = hn.at[token_rows(s, c, core)]
        return Copy(area, area, sems("spread2"), (use, s * chips + c), {"tp": other_core})

    def spread2_start(use, s):
        for step in range(1, chips):
            spread1(use, s, step).wait_recv()
        for c in range(chips):
            spread2(use, s, c).start()

    def spread_end(use, s):
        for c in range(chips):
            spread2(use, s, c).wait_recv()
            spread2(use, s, c).wait_send()
        for step in range(1, chips):
            spread1(use, s, step).wait_send()

    def out_project(s):
        def one(i):
            at = pl.ds(pl.multiple_of(s * local + i * rb, rb), rb)
            inner = pl.ds(aligned(i, rb), rb)
            o_rows = o_t[s, :, inner].astype(F32).T.astype(BF16)
            part[at, :] = dot_nt(o_rows, mat_o[...]).astype(BF16)

        each(local // rb, one)

    small, keep, grad_hidden = r["small"], r["keep"], r["grad_hidden"]
    mid = r["result"]
    small[...] = jnp.zeros_like(small)

    def share_at(s):
        return pl.ds(s * share, share)

    def middle(s):
        attn = sum_end(0, s)
        value = x[token_rows(s, chip, core), :].astype(F32)
        weight = keep[share_at(s), 0:1]
        small[4:5, 0:128] += fold_lanes(weight * value * value)
        small[4:5, 128:256] += fold_lanes(weight * attn * attn)
        value = value + attn
        mid[share_at(s), :] = value
        small[4:5, 256:384] += fold_lanes(weight * value * value)
        value = value * lax.rsqrt(mean_square(value) + EPSILON)
        spread1_start(0, s, (value * r["gain_w"][1:2, :]).astype(BF16))

    ag_end(1)
    kv_arrive(0)
    attend_any(0, 0, qh)
    out_project(0)
    sum1_start(0, 0)
    kv_arrive(1)
    attend_any(1, 0, qh // 2)
    sum2_start(0, 0)
    attend_any(1, qh // 2, qh - qh // 2)
    out_project(1)
    sum1_start(0, 1)
    ag_pass(2)
    if nt > 2:
        ag_start(4)
    middle(0)
    sum2_start(0, 1)
    spread2_start(0, 0)
    middle(1)
    spread_end(0, 0)
    transpose_into(hn, hn_t, 0, local // tb)
    ag_end(2)

    mat_f, units, acc_m, acc_h = r["mat_f"], r["units"], r["acc_m"], r["acc_h"]

    def ffn_rows(t, s):
        def one(i):
            at = pl.ds(pl.multiple_of(s * local + i * rb, rb), rb)
            both = dot(hn[at, :], mat_f[t, :, : 2 * ft])
            gate, upward = both[:, :ft], both[:, ft:]
            sigmoid = 1.0 / (1.0 + jnp.exp(-gate))
            grad_inner = dot(dy[at, :], mat_f[t, :, 2 * ft :])
            silu = gate * sigmoid
            grad_up = (grad_inner * silu).astype(BF16)
            grad_gate = (
                grad_inner * upward * sigmoid * (1.0 + gate * (1.0 - sigmoid))
            ).astype(BF16)
            inner = (silu * upward).astype(BF16)
            grads = jnp.concatenate([grad_gate, grad_up], axis=1)
            units[at, : 2 * ft] = grads
            units[at, 2 * ft :] = inner
            back = dot_nt(grads, mat_f[t, :, : 2 * ft])
            ahead = dot_nt(inner, mat_f[t, :, 2 * ft :])
            if t == 0:
                acc_h[at, :] = back
                acc_m[at, :] = ahead
            else:
                acc_h[at, :] += back
                acc_m[at, :] += ahead

        each(local // rb, one)

    def ffn_weights(t):
        def one(i):
            at = pl.ds(aligned(i, rb), rb)
            mat_f[t, at, : 2 * ft] = dot(hn_t[at, :], units[:, : 2 * ft]).astype(BF16)
            mat_f[t, at, 2 * ft :] = dot(dr_t[at, :], units[:, 2 * ft :]).astype(BF16)

        each(width // rb, one)

    grads = [r["grad_q"], mat_o] + [mat_f.at[t] for t in range(nt)]
    y_in = [r["y_q"], r["y_o"]] + [r["y_f"].at[t] for t in range(nt)]
    z_in = [r["z_q"], r["z_o"]] + [r["z_f"].at[t] for t in range(nt)]
    fin = [r["fin_q"], r["fin_o"]] + [r["fin_f"].at[t] for t in range(nt)]

    def rs_y(c, p):
        return Copy(
            grads[c].at[my_rows(p, peer)], y_in[c].at[p], sems("rsy"), (c, p), {"ctx": peer}
        )

    def rs_z(c, step):
        return Copy(
            y_in[c].at[dp_at(step)],
            z_in[c].at[step - 1],
            sems("rsz"),
            (c, step - 1),
            {"dp": dp_at(step)},
        )

    def rs_f(c):
        area = fin[c].at[pl.ds(aligned(side, hd), hd)]
        return Copy(area, area, sems("rsf"), c, {"ctx": peer})

    def rs_start(c):
        for step in list(range(1, dp)) + [0]:
            rs_y(c, dp_at(step)).start()

    def rs_mid(c):
        for step in list(range(1, dp)) + [0]:
            p = dp_at(step)
            rs_y(c, p).wait_recv()
            mine = grads[c][my_rows(p, side), :].astype(F32)
            y_in[c][p] = (mine + y_in[c][p].astype(F32)).astype(BF16)
            if step:
                rs_z(c, step).start()

    def rs_fin(c):
        total = y_in[c][me].astype(F32)
        for step in range(1, dp):
            rs_z(c, step).wait_recv()
            total += z_in[c][step - 1].astype(F32)
        fin[c][pl.ds(aligned(side, hd), hd), :] = total.astype(BF16)
        rs_f(c).start()

    def rs_end(c):
        for p in range(dp):
            rs_y(c, p).wait_send()
        for step in range(1, dp):
            rs_z(c, step).wait_send()
        rs_f(c).wait_recv()
        rs_f(c).wait_send()

    def acc_low(source, target, s):
        def one(i):
            at = pl.ds(pl.multiple_of(s * local + i * tb, tb), tb)
            target[at, :] = source[at, :].astype(BF16)

        each(local // tb, one)

    for t in range(nt):
        ffn_rows(t, 0)
        if t == 0:
            spread2_start(0, 1)
            spread_end(0, 1)
            transpose_into(hn, hn_t, local, local // tb)
            if nt > 1:
                ag_pass(3)
        if t == nt - 1:
            acc_low(acc_h, part, 0)
            sum1_start(1, 0)
        ffn_rows(t, 1)
        if t == nt - 1:
            acc_low(acc_h, part, 1)
            sum1_start(1, 1)
            sum2_start(1, 0)
        ffn_weights(t)
        rs_start(2 + t)
        if t + 1 < nt:
            if t + 2 < nt:
                ag_pass(2 + t + 2)
            ag_end(2 + t + 1)

    def middle_back(s):
        incoming = sum_end(1, s)
        value = mid[share_at(s), :]
        factor = lax.rsqrt(mean_square(value) + EPSILON)
        hat = value * factor
        small[1:2, :] += jnp.sum(incoming * hat, axis=0, keepdims=True)
        grad_hat = incoming * r["gain_w"][1:2, :]
        back = factor * (grad_hat - hat * jnp.mean(grad_hat * hat, axis=-1, keepdims=True))
        total = dy[token_rows(s, chip, core), :].astype(F32) + back
        grad_hidden[share_at(s), :] = total
        spread1_start(1, s, total.astype(BF16))

    sum2_start(1, 1)
    middle_back(0)
    middle_back(1)
    for s in range(seqs):
        acc_low(acc_m, part, s)
        sum1_start(3, s)
    rs_mid(2)
    spread2_start(1, 0)
    spread2_start(1, 1)

    def again(first, count):
        def one(i):
            at = pl.ds(pl.multiple_of(first + i * tb, tb), tb)
            value = x[at, :].astype(F32)
            value = value * lax.rsqrt(mean_square(value) + EPSILON)
            value = (value * r["gain_w"][0:1, :]).astype(BF16).astype(F32)
            hn_t[:, at] = value.T.astype(BF16)

        each(count, one)

    again(0, rows // tb)
    for s in range(seqs):
        sum2_start(3, s)

    g_kv, gq_t = r["g_kv"], r["gq_t"]

    def out_back(s):
        def one(i):
            at = pl.ds(pl.multiple_of(s * local + i * rb, rb), rb)
            value = dot(hn[at, :], mat_o[...])
            for h in range(qh):
                piece = value[:, h * head : (h + 1) * head]
                start = nqkv + h * 2 * head
                units[at, start : start + 2 * head] = jnp.concatenate(
                    [jnp.zeros_like(piece), piece], axis=1
                ).astype(BF16)

        each(local // rb, one)

    def attend_back(s, with_peer):
        for h in range(kh):
            g_kv[s * kh + h] = jnp.zeros_like(g_kv[s * kh + h])

        def one(index):
            for j in range(local // qb):
                parts, head_kv, here = masked(s, j, index, with_peer)
                at = slice(j * qb, (j + 1) * qb)
                token = slice(s * local + j * qb, s * local + (j + 1) * qb)
                lanes = pl.ds(pl.multiple_of(nqkv + index * 2 * head, 128), 2 * head)
                go = units[token, lanes]
                logs = lse[s * qh + index, :, at]
                probs = [jnp.exp(p[0] - logs) for p in parts]
                grad_probs = [dot_nt(kv[head_kv, w, :size, :], go) for _, w, size in parts]
                row_dot = sum(
                    jnp.sum(p * g, axis=0, keepdims=True) for p, g in zip(probs, grad_probs)
                )
                out = jnp.zeros((2 * head, qb), F32)
                for (_, w, size), p, g in zip(parts, probs, grad_probs):
                    gs = (p * (g - row_dot)).astype(BF16)
                    out += dot(kv_t[head_kv, w, :, :size], gs)
                    g_kv[head_kv, w, :size, :] += dot(gs, here) + dot(p.astype(BF16), go)
                spot = pl.ds(pl.multiple_of(index * head, head), head)
                gq_t[s, spot, at] = out[:head, :] * scale

        each(qh, one)

    def back_copy(s):
        return Copy(
            r["g_kv_low"].at[pl.ds(s * kh, kh)],
            r["g_kv_in"].at[pl.ds(s * kh, kh)],
            sems("gkv"),
            s,
            {"ctx": peer},
        )

    def attend_back_any(s):
        @pl.when(side == 0)
        def _():
            attend_back(s, False)

        @pl.when(side != 0)
        def _():
            attend_back(s, True)
            for h in range(kh):
                r["g_kv_low"][s * kh + h] = g_kv[s * kh + h, 1].astype(BF16)
            back_copy(s).start()

    def kv_back_arrive(s):
        @pl.when(side == 0)
        def _():
            back_copy(s).wait_recv()
            for h in range(kh):
                g_kv[s * kh + h, 0] += r["g_kv_in"][s * kh + h].astype(F32)

        @pl.when(side != 0)
        def _():
            back_copy(s).wait_send()

    def project_back(s):
        def one(i):
            at = pl.ds(pl.multiple_of(s * local + i * rb, rb), rb)
            inner = pl.ds(aligned(i, rb), rb)
            cosine, sine = tab[at, :head], tab[at, head : 2 * head]
            gq = gq_t[s, :, inner].T

            def back(value, start, which):
                value = value * cosine - swap_halves(value) * sine
                plain = raw[at, start : start + head]
                factor = lax.rsqrt(mean_square(plain) + EPSILON)
                hat = plain * factor
                small[2 + which : 3 + which, :head] += jnp.sum(
                    value * hat, axis=0, keepdims=True
                )
                grad_hat = value * r["gain_h"][which : which + 1, :]
                return factor * (
                    grad_hat - hat * jnp.mean(grad_hat * hat, axis=-1, keepdims=True)
                )

            pieces = [
                back(gq[:, h * head : (h + 1) * head], h * head, 0) for h in range(qh)
            ]
            both = [g_kv[s * kh + h, 0, inner, :] for h in range(kh)]
            pieces += [back(b[:, :head], nq + h * head, 1) for h, b in enumerate(both)]
            pieces += [b[:, head:] for b in both]
            low = jnp.concatenate(pieces, axis=1).astype(BF16)
            units[at, :nqkv] = low
            part[at, :] = dot_nt(low, mat_q[...]).astype(BF16)

        each(local // rb, one)

    def out_weights():
        for i in range(width // rb):
            total = sum(
                dot(o_t[s], hn[s * local : (s + 1) * local, i * rb : (i + 1) * rb])
                for s in range(seqs)
            )
            r["grad_o"][i * rb : (i + 1) * rb, :] = total.T.astype(BF16)

    def qkv_weights():
        def one(i):
            at = pl.ds(aligned(i, rb), rb)
            r["grad_q"][at, :] = dot(hn_t[at, :], units[:, :nqkv]).astype(BF16)

        each(width // rb, one)

    grads[1] = r["grad_o"]

    spread_end(1, 0)
    out_back(0)
    attend_back_any(0)
    spread_end(1, 1)
    rs_fin(2)
    if nt > 1:
        rs_mid(3)
    out_back(1)
    out_weights()
    rs_start(1)
    attend_back_any(1)

    def mlp_end(s):
        mlp = sum_end(3, s)
        weight = keep[share_at(s), 0:1]
        small[4:5, 384:512] += fold_lanes(weight * mlp * mlp)
        small[4:5, 512:640] += jnp.sum(keep[share_at(s), :], axis=0, keepdims=True)
        mid[share_at(s), :] += mlp

    kv_back_arrive(0)
    for s in range(seqs):
        mlp_end(s)
    project_back(0)
    sum1_start(2, 0)
    if nt > 2:
        rs_mid(4)
    kv_back_arrive(1)
    project_back(1)
    sum1_start(2, 1)
    sum2_start(2, 0)
    qkv_weights()
    rs_start(0)
    sum2_start(2, 1)
    rs_mid(1)
    if nt > 1:
        rs_fin(3)

    def first_back(s):
        incoming = sum_end(2, s)
        value = x[token_rows(s, chip, core), :].astype(F32)
        factor = lax.rsqrt(mean_square(value) + EPSILON)
        hat = value * factor
        small[0:1, :] += jnp.sum(incoming * hat, axis=0, keepdims=True)
        grad_hat = incoming * r["gain_w"][0:1, :]
        back = factor * (grad_hat - hat * jnp.mean(grad_hat * hat, axis=-1, keepdims=True))
        grad_hidden[share_at(s), :] += back

    first_back(0)
    first_back(1)

    small_in = r["small_in"]

    def small_round(start, copies, order):
        for c in copies:
            c.start()
        for c in copies:
            c.wait_recv()
            c.wait_send()
        total = None
        for o in order:
            term = small_in[start + o]
            total = term if total is None else total + term
        small[...] = total

    small_in[pl.ds(core, 1)] = small[...][None]
    small_round(
        0, [Copy(small, small_in.at[core], sems("small"), 0, {"tp": other_core})], range(2)
    )
    small_in[pl.ds(2 + side, 1)] = small[...][None]
    small_round(2, [Copy(small, small_in.at[2 + side], sems("small"), 1, {"ctx": peer})], range(2))
    small_in[pl.ds(4 + chip, 1)] = small[...][None]
    small_round(
        4,
        [
            Copy(small, small_in.at[4 + chip], sems("small"), 1 + s, {"tp": chip_lane(s)})
            for s in range(1, chips)
        ],
        range(chips),
    )
    rs_mid(0)
    if nt > 2:
        rs_fin(4)
    rs_fin(1)
    small_in[pl.ds(4 + chips + me, 1)] = small[...][None]
    small_round(
        4 + chips,
        [
            Copy(small, small_in.at[4 + chips + me], sems("small"), chips + s, {"dp": dp_at(s)})
            for s in range(1, dp)
        ],
        range(dp),
    )
    r["small_out"][...] = small[...]
    rs_fin(0)
    for c in list(range(2, nt + 2)) + [1, 0]:
        rs_end(c)


def per_device(
    sizes,
    hidden_states,
    out_grad,
    w_query,
    w_key,
    w_value,
    w_out,
    w_gate,
    w_up,
    w_down,
    attn_gain,
    ffn_gain,
    query_gain,
    key_gain,
    segment_ids,
    valid_mask,
    positions,
):
    seqs, local, width = hidden_states.shape
    dp, ctx, tp = sizes
    rows = seqs * local
    head = query_gain.shape[0] * dp
    nq, nk, units = w_query.shape[1], w_key.shape[1], w_gate.shape[1]
    nqkv = nq + 2 * nk
    nt = 3 if units % 3 == 0 else 1
    ft = units // nt
    dd = width // dp
    hd = dd // ctx
    share = local // tp
    chips = tp // 2
    qh, kh = nq // head, nk // head
    cfg = dict(
        seqs=seqs, local=local, width=width, head=head, dp=dp, ctx=ctx, tp=tp,
        qh=qh, kh=kh, nt=nt, ft=ft,
    )
    me, side, lane = lax.axis_index("dp"), lax.axis_index("ctx"), lax.axis_index("tp")

    w_qkv = jnp.concatenate([w_query, w_key, w_value], axis=1)
    w_f = jnp.stack(
        [
            jnp.concatenate(
                [
                    w_gate[:, i * ft : (i + 1) * ft],
                    w_up[:, i * ft : (i + 1) * ft],
                    w_down[i * ft : (i + 1) * ft].T,
                ],
                axis=1,
            )
            for i in range(nt)
        ]
    )

    def wide(value):
        return jnp.pad(value.astype(F32), (0, dd - value.shape[0]))[None]

    gains = jnp.concatenate(
        [wide(attn_gain), wide(ffn_gain), wide(query_gain), wide(key_gain), jnp.zeros((4, dd), F32)]
    )
    token = side * local + jnp.arange(local)
    codes = jnp.where(valid_mask == 1, segment_ids, 100000 + token[None, :]).astype(F32)
    codes = codes.reshape(seqs, 1, local)
    keep = lax.dynamic_slice_in_dim(valid_mask, lane * share, share, 1).astype(F32)
    keep = jnp.broadcast_to(keep.reshape(seqs * share, 1), (seqs * share, 128))
    half = head // 2
    freq = ROPE_BASE ** (-(jnp.arange(half, dtype=F32) * 2.0) / head)
    angle = positions.reshape(rows, 1).astype(F32) * freq[None, :]
    cosine, sine = jnp.cos(angle), jnp.sin(angle)
    tab = jnp.concatenate([cosine, cosine, -sine, sine], axis=1)

    inputs = [
        ("x", hidden_states.reshape(rows, width), True),
        ("dy", out_grad.reshape(rows, width), True),
        ("w_qkv", w_qkv, False),
        ("w_o", w_out.T, False),
        ("w_f", w_f, False),
        ("gains", gains, True),
        ("codes", codes, True),
        ("keep", keep, True),
        ("tab", tab, True),
    ]
    outputs = [
        ("result", (seqs * share, width), F32),
        ("grad_hidden", (seqs * share, width), F32),
        ("fin_q", (dd, nqkv), BF16),
        ("fin_o", (dd, nq), BF16),
        ("fin_f", (nt, dd, 3 * ft), BF16),
        ("small_out", (8, width), F32),
    ]
    scratch = [
        ("mat_q", (width, nqkv), BF16),
        ("mat_o", (width, nq), BF16),
        ("mat_f", (nt, width, 3 * ft), BF16),
        ("gain_buf", (dp, 8, dd), F32),
        ("gain_w", (8, width), F32),
        ("gain_h", (8, head), F32),
        ("code_peer", (seqs, 1, local), F32),
        ("key_code", (ctx, seqs, local, 128), F32),
        ("hn", (rows, width), BF16),
        ("hn_t", (width, rows), BF16),
        ("dr_t", (width, rows), BF16),
        ("raw", (rows, nq + nk), F32),
        ("q_pad", (seqs * qh, local, 2 * head), BF16),
        ("kv", (seqs * kh, ctx, local, 2 * head), BF16),
        ("kv_t", (seqs * kh, ctx, 2 * head, local), BF16),
        ("g_kv", (seqs * kh, ctx, local, 2 * head), F32),
        ("g_kv_low", (seqs * kh, local, 2 * head), BF16),
        ("g_kv_in", (seqs * kh, local, 2 * head), BF16),
        ("o_t", (seqs, nq, local), BF16),
        ("gq_t", (seqs, nq, local), F32),
        ("lse", (seqs * qh, 1, local), F32),
        ("part", (rows, width), BF16),
        ("near", (2, seqs, chips, share, width), BF16),
        ("pair", (seqs, chips, share, width), BF16),
        ("far", (2, seqs, max(chips - 1, 1), share, width), BF16),
        ("small", (8, width), F32),
        ("small_in", (4 + chips + dp, 8, width), F32),
        ("units", (rows, 3 * ft), BF16),
        ("acc_m", (rows, width), F32),
        ("acc_h", (rows, width), F32),
        ("grad_q", (width, nqkv), BF16),
        ("grad_o", (width, nq), BF16),
        ("y_q", (dp, hd, nqkv), BF16),
        ("y_o", (dp, hd, nq), BF16),
        ("y_f", (nt, dp, hd, 3 * ft), BF16),
        ("z_q", (dp - 1, hd, nqkv), BF16),
        ("z_o", (dp - 1, hd, nq), BF16),
        ("z_f", (nt, dp - 1, hd, 3 * ft), BF16),
    ]
    semaphores = [("own_sem", (nt + 2,))]
    for name, shape in (
        ("agz", (nt + 2, dp - 1)),
        ("agy", (nt + 2, dp - 1)),
        ("gain", (dp - 1,)),
        ("code", (1,)),
        ("kv", (seqs,)),
        ("gkv", (seqs,)),
        ("sum1", (4, seqs * chips)),
        ("sum2", (4, seqs * max(chips - 1, 1))),
        ("spread1", (2, seqs * max(chips - 1, 1))),
        ("spread2", (2, seqs * chips)),
        ("rsy", (nt + 2, dp)),
        ("rsz", (nt + 2, dp - 1)),
        ("rsf", (nt + 2,)),
        ("small", (chips + dp,)),
    ):
        semaphores += [(name + "_s", shape), (name + "_r", shape)]
    names = [n for n, *_ in inputs] + [n for n, *_ in outputs]
    names += [n for n, *_ in scratch] + [n for n, *_ in semaphores]
    vmem = pl.BlockSpec(memory_space=pltpu.VMEM)
    out = pl.pallas_call(
        functools.partial(block_kernel, cfg, names),
        out_shape=[jax.ShapeDtypeStruct(s, d) for _, s, d in outputs],
        in_specs=[vmem if v else pl.BlockSpec(memory_space=pl.ANY) for *_, v in inputs],
        out_specs=[vmem] * len(outputs),
        scratch_shapes=[pltpu.VMEM(s, d) for _, s, d in scratch]
        + [pltpu.SemaphoreType.DMA(s) for _, s in semaphores],
        compiler_params=pltpu.CompilerParams(
            collective_id=0, has_side_effects=True, vmem_limit_bytes=VMEM_LIMIT
        ),
        name="block",
    )(*[v for _, v, _ in inputs])
    result, grad_hidden, fin_q, fin_o, fin_f, small = out

    squares = small[4, :640].reshape(5, 128)
    sums = jnp.sum(squares[:4], axis=1)
    statistics = jnp.sqrt(sums / (squares[4, 0] * width))

    def own(row, size):
        return lax.dynamic_slice_in_dim(small[row], me * size, size, 0)

    fin_f = fin_f.astype(F32)
    return (
        result.reshape(seqs, share, width),
        grad_hidden.reshape(seqs, share, width),
        fin_q[:, :nq].astype(F32),
        fin_q[:, nq : nq + nk].astype(F32),
        fin_q[:, nq + nk :].astype(F32),
        fin_o.T.astype(F32),
        jnp.concatenate([fin_f[i, :, :ft] for i in range(nt)], axis=1),
        jnp.concatenate([fin_f[i, :, ft : 2 * ft] for i in range(nt)], axis=1),
        jnp.concatenate([fin_f[i, :, 2 * ft :].T for i in range(nt)], axis=0),
        own(0, attn_gain.shape[0]),
        own(1, ffn_gain.shape[0]),
        own(2, query_gain.shape[0]),
        own(3, key_gain.shape[0]),
        statistics,
    )


VMEM_LIMIT = 63 * 2**20


def solution(mesh):
    sizes = tuple(mesh.shape[a] for a in ("dp", "ctx", "tp"))
    return jax.shard_map(
        functools.partial(per_device, sizes),
        mesh=mesh,
        in_specs=(
            P("dp", "ctx", None),
            P("dp", "ctx", None),
            P("dp", "tp"),
            P("dp", "tp"),
            P("dp", "tp"),
            P("tp", "dp"),
            P("dp", "tp"),
            P("dp", "tp"),
            P("tp", "dp"),
            P("dp"),
            P("dp"),
            P("dp"),
            P("dp"),
            P("dp", "ctx"),
            P("dp", "ctx"),
            P("dp", "ctx"),
        ),
        out_specs=(
            P("dp", ("ctx", "tp"), None),
            P("dp", ("ctx", "tp"), None),
            P("dp", "tp"),
            P("dp", "tp"),
            P("dp", "tp"),
            P("tp", "dp"),
            P("dp", "tp"),
            P("dp", "tp"),
            P("tp", "dp"),
            P("dp"),
            P("dp"),
            P("dp"),
            P("dp"),
            P(),
        ),
        check_vma=False,
    )
```

```python
import functools
import types

import jax
import jax.numpy as jnp
import numpy as np
from jax import lax
from jax.experimental import pallas as pl
from jax.experimental.pallas import tpu as pltpu
from jax.sharding import PartitionSpec as P

EPSILON = 1e-05
ROPE_BASE = 1000000.0
F32 = jnp.float32
BF16 = jnp.bfloat16
MESH = pl.DeviceIdType.MESH
NEGATIVE = -1e30
PADDING = 50000.0


def dot(left, right):
    return jnp.dot(left, right, preferred_element_type=F32)


def dot_nt(left, right):
    return lax.dot_general(left, right, (((1,), (1,)), ((), ())), preferred_element_type=F32)


def each(count, body):
    def step(i, carry):
        body(i)
        return carry

    lax.fori_loop(0, count, step, 0)


def aligned(index, unit):
    return pl.multiple_of(index * unit, unit)


def mean_square(value):
    return jnp.mean(value * value, axis=-1, keepdims=True)


def swap_halves(value, head):
    half = head // 2
    size = value.shape[1]
    if size % 128 == 0:
        at = lax.broadcasted_iota(jnp.int32, (1, size), 1)
        first = lax.rem(at, head) < half
        return jnp.where(first, pltpu.roll(value, size - half, 1), pltpu.roll(value, half, 1))
    pieces = []
    for start in range(0, size, head):
        pieces += [value[:, start + half : start + head], value[:, start : start + half]]
    return jnp.concatenate(pieces, axis=1)


def spread_means(value, head):
    size = value.shape[1]
    row = lax.div(lax.broadcasted_iota(jnp.int32, (size, size), 0), head)
    column = lax.div(lax.broadcasted_iota(jnp.int32, (size, size), 1), head)
    block = jnp.where(row == column, 1.0 / head, 0.0).astype(BF16)
    high = value.astype(BF16)
    rest = (value - high.astype(F32)).astype(BF16)
    return dot(high, block) + dot(rest, block)


def widen(value, count):
    size = value.shape[1]
    if count <= size:
        return value[:, :count]
    return jnp.concatenate([value] * -(-count // size), axis=1)[:, :count]


def fold_lanes(value):
    total = jnp.sum(value, axis=0, keepdims=True)
    out = total[:, :128]
    for i in range(1, value.shape[1] // 128):
        out += total[:, i * 128 : (i + 1) * 128]
    return out


class Copy:
    def __init__(self, src, dst, sems, index, device, send=None):
        send = sems[0].at[index] if send is None else send
        self.copy = pltpu.make_async_remote_copy(
            src_ref=src,
            dst_ref=dst,
            send_sem=send,
            recv_sem=sems[1].at[index],
            device_id=device,
            device_id_type=MESH,
        )

    def start(self):
        self.copy.start()

    def wait_send(self):
        self.copy.wait_send()

    def wait_recv(self):
        self.copy.wait_recv()


def block_kernel(cfg, r, two):
    seqs, local, width, head = cfg.seqs, cfg.local, cfg.width, cfg.head
    dp, ctx, tp = cfg.dp, cfg.ctx, cfg.tp
    qh, kh, nt, ft = cfg.qh, cfg.kh, cfg.nt, cfg.ft
    nq, nk = qh * head, kh * head
    nqkv = nq + 2 * nk
    group = qh // kh
    chips = tp // 2
    rows = seqs * local
    share = local // tp
    dd = width // dp
    hd = dd // ctx
    me, side, lane = lax.axis_index("dp"), lax.axis_index("ctx"), lax.axis_index("tp")
    core, chip = lax.rem(lane, 2), lax.div(lane, 2)
    other_core = lane + 1 - 2 * core
    peer = 1 - side
    rb = min(256, local)
    qb = min(256, local)
    tb = min(128, local)
    scale = head**-0.5

    def dp_at(step):
        return lax.rem(me + step, dp)

    def chip_lane(step):
        return lax.rem(chip + step, chips) * 2 + core

    barrier = pltpu.get_barrier_semaphore()
    greet = [{"dp": dp_at(s)} for s in range(1, dp)] + [{"ctx": peer}, {"tp": other_core}]
    greet += [{"tp": chip_lane(s)} for s in range(1, chips)]
    for device in greet:
        pl.semaphore_signal(barrier, inc=1, device_id=device, device_id_type=MESH)
    pl.semaphore_wait(barrier, len(greet))

    whole = [r.mat_q, r.mat_o] + [r.mat_f.at[t] for t in range(nt)]

    def my_rows(owner, which):
        return pl.ds(pl.multiple_of(owner * dd + which * hd, hd), hd)

    def ag_z(c, step):
        return Copy(
            whole[c].at[my_rows(me, side)],
            whole[c].at[my_rows(me, side)],
            two.agz,
            (c, step - 1),
            {"dp": dp_at(step)},
        )

    def ag_y(c, step):
        owner = lax.rem(me - step + dp, dp)
        area = whole[c].at[my_rows(owner, side)]
        return Copy(area, area, two.agy, (c, step - 1), {"ctx": peer})

    relayed = tuple(range(nt + 2)) if dp > 2 else ()
    hops = [dp - 2, 2] if dp > 2 else []
    order = sorted(range(1, dp), key=lambda step: (step not in hops, step))

    def ag_far(c, step):
        owner, target = (0, dp - 1) if step == dp - 2 else (dp - 1, 0)
        if dp == 4:
            owner = jnp.where(me == 1, dp - 1, 0)
            target = jnp.where(me == 1, 0, dp - 1)
        area = whole[c].at[my_rows(owner, side)]
        index = lax.rem(target - owner + dp, dp) - 1
        send = r.agfar.at[c]
        return Copy(area, area, two.agz, (c, index), {"dp": target}, send)

    def far_when(c, step, body):
        if c not in relayed:
            return
        if dp == 4:
            if step == 2:
                pl.when((me == 1) | (me == 2))(body)
        elif step == dp - 2:
            pl.when(me == dp - 2)(body)
        elif step == 2:
            pl.when(me == 1)(body)

    def near_when(c, step, body):
        if c in relayed and step == dp - 1:
            pl.when(me != 0)(body)
        elif c in relayed and step == 1:
            pl.when(me != dp - 1)(body)
        else:
            body()

    own_rows = pl.ds(aligned(me, dd), dd)

    def stage(c):
        if c == 1:
            return r.units.at[pl.ds(ft, nq), pl.ds(0, dd)]
        return r.units.at[pl.ds(0, ft), pl.ds((c - 2) * dd, dd)]

    def own_moves(c):
        if not cfg.plain:
            source = [r.w_qkv, r.w_o] + [r.w_f.at[t] for t in range(nt)]
            pairs_of = [(source[c], whole[c].at[own_rows])]
        elif c == 0:
            pairs_of, start = [], 0
            for source in (r.w_query, r.w_key, r.w_value):
                size = source.shape[1]
                pairs_of.append((source, r.mat_q.at[own_rows, pl.ds(start, size)]))
                start += size
        elif c == 1:
            pairs_of = [(r.w_out, stage(1))]
        else:
            t = c - 2
            at = pl.ds(t * ft, ft)
            pairs_of = [
                (r.w_gate.at[:, at], r.mat_f.at[t, own_rows, pl.ds(0, ft)]),
                (r.w_up.at[:, at], r.mat_f.at[t, own_rows, pl.ds(ft, ft)]),
                (r.w_down.at[at], stage(c)),
            ]
        return [
            pltpu.make_async_copy(source, target, r.own_sem.at[c, i])
            for i, (source, target) in enumerate(pairs_of)
        ]

    def own_start(c):
        for move in own_moves(c):
            move.start()

    def own_end(c):
        for move in own_moves(c):
            move.wait()
        if cfg.plain and c >= 1:
            block = stage(c)[...].astype(F32).T.astype(BF16)
            if c == 1:
                r.mat_o[own_rows, :] = block
            else:
                r.mat_f[c - 2, own_rows, 2 * ft :] = block

    def ag_start(c):
        if c >= nt + 2:
            return
        for step in order:
            near_when(c, step, lambda: ag_z(c, step).start())

    def ag_pass_one(c, step):
        ag_z(c, step).wait_recv()
        far_when(c, step, lambda: ag_far(c, step).start())
        ag_y(c, step).start()

    waiting = [(c, step) for c in range(nt + 2) for step in order]

    def serve(count):
        for _ in range(min(count, len(waiting))):
            ag_pass_one(*waiting.pop(0))

    def serve_all(c):
        while waiting and waiting[0][0] <= c:
            serve(1)

    def ag_end(c):
        serve_all(c)
        for step in order:
            ag_y(c, step).wait_recv()
            ag_y(c, step).wait_send()
            near_when(c, step, lambda: ag_z(c, step).wait_send())
            far_when(c, step, lambda: ag_far(c, step).wait_send())

    gain_buf = r.gain_buf

    def gain_copy(step):
        return Copy(
            r.gains, gain_buf.at[me], two.gain, step - 1, {"dp": dp_at(step)}
        )

    def code_copy():
        return Copy(r.facts, r.code_peer, two.code, 0, {"ctx": peer})

    for c in range(nt + 2):
        own_start(c)
    for step in range(1, dp):
        gain_copy(step).start()
    own_end(0)
    ag_start(0)
    code_copy().start()
    for c in range(1, nt + 2):
        own_end(c)

    x, dy, hn, hn_t, dr_t = r.x, r.dy, r.hn, r.hn_t, r.dr_t

    def transpose_into(source, target, first, count):
        def one(i):
            at = pl.ds(pl.multiple_of(first + i * tb, tb), tb)
            target[:, at] = source[at, :].astype(F32).T.astype(BF16)

        each(count, one)

    transpose_into(dy, dr_t, 0, rows // tb)

    def code_columns(source, which):
        for s in range(seqs):
            row = jnp.broadcast_to(source[s, 0:1, :], (128, local))
            r.key_code[which, s] = row.T

    code_columns(r.facts, 0)

    sign = lax.rem(lax.broadcasted_iota(jnp.int32, (1, 128), 1), head) < head // 2
    sign = jnp.where(sign, -1.0, 1.0).astype(F32)
    for s in range(seqs):
        for start in range(0, local, tb):
            place = jnp.broadcast_to(r.facts[s, 1:2, start : start + tb], (128, tb)).T
            angle = place * r.freq[...]
            at = pl.ds(s * local + start, tb)
            r.tab[at, :128] = jnp.cos(angle)
            r.tab[at, 128:] = jnp.sin(angle) * sign

    gain_buf[pl.ds(me, 1)] = r.gains[...][None]
    for step in range(1, dp):
        gain_copy(step).wait_recv()
        gain_copy(step).wait_send()
    piece = head // dp
    for d in range(dp):
        r.gain_w[0:2, d * dd : (d + 1) * dd] = gain_buf[d, 0:2, :]
        for h in range(qh):
            start = h * head + d * piece
            r.gain_h[0:1, start : start + piece] = gain_buf[d, 2:3, :piece]
        for h in range(kh):
            start = nq + h * head + d * piece
            r.gain_h[0:1, start : start + piece] = gain_buf[d, 3:4, :piece]

    def normed_into(target, first, count):
        def one(i):
            at = pl.ds(pl.multiple_of(first + i * tb, tb), tb)
            value = x[at, :].astype(F32)
            value = value * lax.rsqrt(mean_square(value) + EPSILON)
            target[at, :] = (value * r.gain_w[0:1, :]).astype(BF16)

        each(count, one)

    normed_into(hn, 0, rows // tb)
    code_copy().wait_recv()
    code_copy().wait_send()
    code_columns(r.code_peer, 1)
    serve_all(0)
    ag_start(1)
    ag_start(2)
    ag_end(0)

    mat_q, mat_o, raw, tab = r.mat_q, r.mat_o, r.raw, r.tab
    q_pad, kv, kv_t = r.q_pad, r.kv, r.kv_t

    nqk = nq + nk
    low_half = lax.broadcasted_iota(jnp.int32, (1, 2 * head), 1) < head

    def pairs(value, start, count):
        out = []
        for h in range(0, count, 2):
            if count == 1:
                here = value[:, start : start + head]
                both = jnp.concatenate([here, here], axis=1)
                out.append((both, both))
                continue
            here = value[:, start + h * head : start + (h + 2) * head]
            turned = pltpu.roll(here, head, 1)
            out += [(here, turned), (turned, here)]
        return out

    def project(s):
        def one(i):
            at = pl.ds(pl.multiple_of(s * local + i * rb, rb), rb)
            inner = pl.ds(aligned(i, rb), rb)
            both = dot(hn[at, :], mat_q[...])
            plain = both[:, :nqk]
            raw[at, :] = plain
            cosine = widen(tab[at, : 2 * head], nqk)
            sine = widen(tab[at, 2 * head :], nqk)
            value = plain * lax.rsqrt(spread_means(plain * plain, head) + EPSILON)
            value = value * r.gain_h[0:1, :]
            value = value * cosine + swap_halves(value, head) * sine
            for h, (low, _) in enumerate(pairs(value, 0, qh)):
                q_pad[s * qh + h, inner, :] = jnp.where(low_half, low * scale, 0.0).astype(BF16)
            keys = pairs(value, nq, kh)
            values = pairs(both, nqk, kh)
            for h in range(kh):
                kv[s * kh + h, 0, inner, :] = jnp.where(
                    low_half, keys[h][0], values[h][1]
                ).astype(BF16)

        each(local // rb, one)

    def kv_copy(s):
        return Copy(
            kv.at[pl.ds(s * kh, kh), 0],
            kv.at[pl.ds(s * kh, kh), 1],
            two.kv,
            s,
            {"ctx": peer},
        )

    def kv_transpose(s, which):
        for h in range(kh):
            kv_t[s * kh + h, which] = kv[s * kh + h, which].astype(F32).T.astype(BF16)

    for s in range(seqs):
        project(s)

        @pl.when(side == 0)
        def _():
            kv_copy(s).start()

        kv_transpose(s, 0)
        if s == 0:
            serve_all(1)
            ag_start(3)

    o_t, lse = r.o_t, r.lse

    def masked(s, j, index, with_peer):
        last = (j + 1) * qb
        head_kv = s * kh + index // group
        here = q_pad[s * qh + index, j * qb : last, :]
        query = r.facts[s, 0:1, j * qb : last]

        def spread(code):
            return jnp.concatenate([code] * (qb // 128), axis=1)

        own = dot_nt(kv[head_kv, 0, :last, :], here)
        key_at = lax.broadcasted_iota(jnp.int32, (last, qb), 0)
        query_at = lax.broadcasted_iota(jnp.int32, (last, qb), 1) + j * qb
        allowed = (spread(r.key_code[0, s, :last, :]) == query) & (key_at <= query_at)
        own = jnp.where(allowed, own, NEGATIVE)
        parts = [(own, 0, last)]
        if with_peer:
            far = dot_nt(kv[head_kv, 1], here)
            far = jnp.where(spread(r.key_code[1, s]) == query, far, NEGATIVE)
            parts.append((far, 1, local))
        return parts, head_kv, here

    def attend_one(s, index, with_peer):
        for j in range(local // qb):
            parts, head_kv, _ = masked(s, j, index, with_peer)
            highest = functools.reduce(
                jnp.maximum, [jnp.max(p[0], axis=0, keepdims=True) for p in parts]
            )
            expo = [jnp.exp(p[0] - highest) for p in parts]
            total = sum(jnp.sum(e, axis=0, keepdims=True) for e in expo)
            factor = 1.0 / total
            out = jnp.zeros((2 * head, qb), F32)
            for (_, which, size), e in zip(parts, expo):
                out += dot(kv_t[head_kv, which, :, :size], (e * factor).astype(BF16))
            at = pl.ds(pl.multiple_of(index * head, head), head)
            o_t[s, at, j * qb : (j + 1) * qb] = out[head:, :].astype(BF16)
            lse[s * qh + index, :, j * qb : (j + 1) * qb] = highest + jnp.log(total)

    def attend(s, first, count):
        def one(i):
            @pl.when(side == 0)
            def _():
                attend_one(s, first + i, False)

            @pl.when(side != 0)
            def _():
                attend_one(s, first + i, True)

        each(count, one)

    def kv_arrive(s):
        @pl.when(side == 0)
        def _():
            kv_copy(s).wait_send()

        @pl.when(side != 0)
        def _():
            kv_copy(s).wait_recv()
            kv_transpose(s, 1)

    part, near, pair, far = r.part, r.near, r.pair, r.far

    def pool(use):
        return 1 if use == 3 else 0

    def token_rows(s, which_chip, which_core):
        start = s * local + (which_chip * 2 + which_core) * share
        return pl.ds(pl.multiple_of(start, share), share)

    def sum1(use, s, c):
        return Copy(
            part.at[token_rows(s, c, 1 - core)],
            near.at[pool(use), s, c],
            two.sum1,
            (use, s * chips + c),
            {"tp": other_core},
        )

    def sum1_start(use, s):
        for c in range(chips):
            sum1(use, s, c).start()

    def sum2(use, s, step):
        return Copy(
            pair.at[s, lax.rem(chip + step, chips)],
            far.at[pool(use), s, step - 1],
            two.sum2,
            (use, s * max(chips - 1, 1) + step - 1),
            {"tp": chip_lane(step)},
        )

    def sum2_start(use, s):
        for c in range(chips):
            sum1(use, s, c).wait_recv()
        for c in range(chips):
            mine = part[token_rows(s, c, core), :].astype(F32)
            pair[s, c] = (mine + near[pool(use), s, c].astype(F32)).astype(BF16)
        for step in range(1, chips):
            sum2(use, s, step).start()

    def sum_end(use, s):
        for step in range(1, chips):
            sum2(use, s, step).wait_recv()
        total = part[token_rows(s, chip, core), :].astype(F32)
        total += near[pool(use), s, chip].astype(F32)
        for step in range(1, chips):
            total += far[pool(use), s, step - 1].astype(F32)
        for c in range(chips):
            sum1(use, s, c).wait_send()
        for step in range(1, chips):
            sum2(use, s, step).wait_send()
        return total

    def spread1(use, s, step):
        area = hn.at[token_rows(s, chip, core)]
        index = (use, s * max(chips - 1, 1) + step - 1)
        return Copy(area, area, two.spread1, index, {"tp": chip_lane(step)})

    def spread1_start(use, s, value):
        hn[token_rows(s, chip, core), :] = value
        for step in range(1, chips):
            spread1(use, s, step).start()

    def spread2(use, s, c):
        area = hn.at[token_rows(s, c, core)]
        return Copy(area, area, two.spread2, (use, s * chips + c), {"tp": other_core})

    def spread2_start(use, s):
        for step in range(1, chips):
            spread1(use, s, step).wait_recv()
        for c in range(chips):
            spread2(use, s, c).start()

    def spread_end(use, s):
        for c in range(chips):
            spread2(use, s, c).wait_recv()
            spread2(use, s, c).wait_send()
        for step in range(1, chips):
            spread1(use, s, step).wait_send()

    def out_project(s):
        def one(i):
            at = pl.ds(pl.multiple_of(s * local + i * rb, rb), rb)
            inner = pl.ds(aligned(i, rb), rb)
            o_rows = o_t[s, :, inner].astype(F32).T.astype(BF16)
            part[at, :] = dot_nt(o_rows, mat_o[...]).astype(BF16)

        each(local // rb, one)

    small, grad_hidden = r.small, r.grad_hidden
    mid = r.result
    small[...] = jnp.zeros_like(small)

    def share_at(s):
        return pl.ds(s * share, share)

    def keep_of(s):
        code = r.key_code[0, s, pl.ds(aligned(lane, share), share), :]
        return jnp.where(code < PADDING, 1.0, 0.0).astype(F32)

    def middle(s):
        attn = sum_end(0, s)
        value = x[token_rows(s, chip, core), :].astype(F32)
        weight = keep_of(s)[:, 0:1]
        small[4:5, 0:128] += fold_lanes(weight * value * value)
        small[4:5, 128:256] += fold_lanes(weight * attn * attn)
        value = value + attn
        mid[share_at(s), :] = value
        small[4:5, 256:384] += fold_lanes(weight * value * value)
        value = value * lax.rsqrt(mean_square(value) + EPSILON)
        spread1_start(0, s, (value * r.gain_w[1:2, :]).astype(BF16))

    half = qh // 2
    serve_all(2)
    kv_arrive(0)
    attend(0, 0, qh)
    ag_end(1)
    out_project(0)
    sum1_start(0, 0)
    ag_start(4)
    kv_arrive(1)
    attend(1, 0, half)
    sum2_start(0, 0)
    attend(1, half, qh - half)
    out_project(1)
    sum1_start(0, 1)
    middle(0)
    sum2_start(0, 1)
    serve_all(3)
    spread2_start(0, 0)
    middle(1)
    spread_end(0, 0)
    transpose_into(hn, hn_t, 0, local // tb)
    spread2_start(0, 1)
    ag_end(2)

    mat_f, units, acc_m, acc_h = r.mat_f, r.units, r.acc_m, r.acc_h

    def ffn_rows(t, s):
        def one(i):
            at = pl.ds(pl.multiple_of(s * local + i * rb, rb), rb)
            both = dot(hn[at, :], mat_f[t, :, : 2 * ft])
            gate, upward = both[:, :ft], both[:, ft:]
            sigmoid = 1.0 / (1.0 + jnp.exp(-gate))
            grad_inner = dot(dy[at, :], mat_f[t, :, 2 * ft :])
            silu = gate * sigmoid
            grad_up = (grad_inner * silu).astype(BF16)
            grad_gate = (
                grad_inner * upward * sigmoid * (1.0 + gate * (1.0 - sigmoid))
            ).astype(BF16)
            inner = (silu * upward).astype(BF16)
            grads = jnp.concatenate([grad_gate, grad_up], axis=1)
            units[at, : 2 * ft] = grads
            units[at, 2 * ft :] = inner
            back = dot_nt(grads, mat_f[t, :, : 2 * ft])
            ahead = dot_nt(inner, mat_f[t, :, 2 * ft :])
            if t > 0:
                back += acc_h[at, :]
                ahead += acc_m[at, :]
            if t < nt - 1:
                acc_h[at, :] = back
            else:
                part[at, :] = back.astype(BF16)
            acc_m[at, :] = ahead

        each(local // rb, one)

    def ffn_weights(t):
        def one(i):
            at = pl.ds(aligned(i, rb), rb)
            mat_f[t, at, : 2 * ft] = dot(hn_t[at, :], units[:, : 2 * ft]).astype(BF16)
            mat_f[t, at, 2 * ft :] = dot(dr_t[at, :], units[:, 2 * ft :]).astype(BF16)

        each(width // rb, one)

    folds = dp > 2
    grads = [r.grad_q, r.grad_o, None] + [mat_f.at[t] for t in range(1, nt)]
    y_in = [r.y_q, r.y_o, None] + [r.y_f.at[t] for t in range(nt - 1)]
    z_in = [r.z_q, r.z_o, None] + [r.z_f.at[t] for t in range(nt - 1)]
    fold = [None, None, r.fold_a] + [r.fold_f.at[t] for t in range(nt - 1)]
    fin = [r.fin_q, r.fin_o] + [r.fin_f.at[t] for t in range(nt)]

    def fold_of(c):
        return folds and fold[c] is not None

    def send_when(c, step, direct, other, defer):
        if not fold_of(c):
            direct()
            return
        away = []
        if step == dp - 1:
            pl.when(me == 0)(other)
            away.append(me == 0)
        if step == 1:
            pl.when(me == dp - 1)(other)
            away.append(me == dp - 1)
        if step == dp - 2:
            pl.when(me == 1)(defer)
            away.append(me == 1)
        if step == 2:
            pl.when(me == dp - 2)(defer)
            away.append(me == dp - 2)
        if not away:
            direct()
            return
        away = functools.reduce(jnp.logical_or, away)
        pl.when(jnp.logical_not(away))(direct)

    def fold_when(c, body):
        if not fold_of(c):
            return
        if dp == 4:
            pl.when((me == 1) | (me == 2))(lambda: body(2))
        else:
            pl.when(me == 1)(lambda: body(dp - 2))
            pl.when(me == dp - 2)(lambda: body(2))

    def end_when(c, body):
        if fold_of(c):
            pl.when(me == 0)(lambda: body(dp - 1))
            pl.when(me == dp - 1)(lambda: body(1))

    def taken(c, step, body):
        if fold_of(c) and step == dp - 1:
            pl.when(me != dp - 1)(body)
        elif fold_of(c) and step == 1:
            pl.when(me != 0)(body)
        else:
            body()

    def rs_y(c, p):
        return Copy(
            grads[c].at[my_rows(p, peer)], y_in[c].at[p], two.rsy, (c, p), {"ctx": peer}
        )

    def z_out(c, step):
        if c == 2:
            return mat_f.at[0, pl.ds(aligned(dp_at(step), dd), dd)]
        return y_in[c].at[dp_at(step)]

    def z_slot(c, step):
        return r.z_a.at[step - 1] if c == 2 else z_in[c].at[step - 1]

    def rs_z(c, step):
        return Copy(
            z_out(c, step), z_slot(c, step), two.rsz, (c, step - 1), {"dp": dp_at(step)}
        )

    def rs_fold(c, step):
        neighbour = 1 if step == dp - 1 else dp - 2
        return Copy(z_out(c, step), fold[c], two.rsn, c, {"dp": neighbour})

    def rs_f(c):
        area = fin[c].at[pl.ds(aligned(side, hd), hd)]
        return Copy(z_in[c].at[0], area, two.rsf, c, {"ctx": peer})

    def fin_copy(c):
        if c == 2:
            return pltpu.make_async_copy(r.z_a.at[1], fin[c], r.fin_sem.at[c])
        area = fin[c].at[pl.ds(aligned(side, hd), hd)]
        return pltpu.make_async_copy(z_in[c].at[0], area, r.fin_sem.at[c])

    def first_y():
        return Copy(r.z_a.at[0], r.y_a, two.firsty, 0, {"ctx": peer})

    steps = sorted(range(1, dp), key=lambda step: (step not in (1, dp - 1), step))

    def send_piece(c, step):
        send_when(
            c,
            step,
            lambda: rs_z(c, step).start(),
            lambda: rs_fold(c, step).start(),
            lambda: None,
        )

    def rs_start(c):
        if c == 2:
            for step in steps:
                send_piece(c, step)
            return
        for step in steps + [0]:
            rs_y(c, dp_at(step)).start()

    def rs_mid(c):
        for step in steps + [0]:
            p = dp_at(step)
            rs_y(c, p).wait_recv()
            mine = grads[c][my_rows(p, side), :].astype(F32)
            y_in[c][p] = (mine + y_in[c][p].astype(F32)).astype(BF16)
            if step:
                send_piece(c, step)

    def rs_join(c):
        def one(step):
            rs_fold(c, dp - 1).wait_recv()
            if c == 2:
                for start in range(0, dd, hd):
                    at = pl.ds(pl.multiple_of(dp_at(step) * dd + start, hd), hd)
                    both = mat_f[0, at, :].astype(F32) + fold[c][start : start + hd, :].astype(F32)
                    mat_f[0, at, :] = both.astype(BF16)
            else:
                both = y_in[c][dp_at(step)].astype(F32) + fold[c][...].astype(F32)
                y_in[c][dp_at(step)] = both.astype(BF16)
            rs_z(c, step).start()

        fold_when(c, one)

    def blank(c):
        def zero(step):
            slot = r.z_a if c == 2 else z_in[c]
            slot[step - 1] = jnp.zeros(slot.shape[1:], BF16)

        if fold_of(c):
            pl.when(me == 0)(lambda: zero(1))
            pl.when(me == dp - 1)(lambda: zero(dp - 1))

    def rs_fin(c):
        for step in range(1, dp):
            taken(c, step, lambda: rs_z(c, step).wait_recv())
        blank(c)
        if c == 2:
            for start in range(0, dd, hd):
                at = pl.ds(start, hd)
                mine = pl.ds(pl.multiple_of(me * dd + start, hd), hd)
                total = mat_f[0, mine, :].astype(F32)
                for step in range(1, dp):
                    total += r.z_a[step - 1, at, :].astype(F32)
                r.z_a[0, at, :] = total.astype(BF16)
            first_y().start()
            return
        total = y_in[c][me].astype(F32)
        for step in range(1, dp):
            total += z_in[c][step - 1].astype(F32)
        z_in[c][0] = total.astype(BF16)
        rs_f(c).start()
        fin_copy(c).start()

    def first_sum():
        first_y().wait_recv()
        for start in range(0, dd, hd):
            at = pl.ds(start, hd)
            total = r.z_a[0, at, :].astype(F32) + r.y_a[at, :].astype(F32)
            r.z_a[1, at, :] = total.astype(BF16)
        fin_copy(2).start()

    def rs_end(c):
        for step in range(1, dp):
            wait = lambda: rs_z(c, step).wait_send()
            send_when(c, step, wait, lambda: None, wait)
        end_when(c, lambda step: rs_fold(c, step).wait_send())
        if c == 2:
            first_y().wait_send()
        else:
            for p in range(dp):
                rs_y(c, p).wait_send()
            rs_f(c).wait_recv()
            rs_f(c).wait_send()
        fin_copy(c).wait()

    def acc_low(source, target, s):
        def one(i):
            at = pl.ds(pl.multiple_of(s * local + i * tb, tb), tb)
            target[at, :] = source[at, :].astype(BF16)

        each(local // tb, one)

    for t in range(nt):
        ffn_rows(t, 0)
        if t == 0:
            spread_end(0, 1)
            transpose_into(hn, hn_t, local, local // tb)
            serve(1)
        if t == nt - 1:
            sum1_start(1, 0)
        ffn_rows(t, 1)
        if t == 0:
            serve_all(nt + 1)
        if t == nt - 1:
            sum1_start(1, 1)
            sum2_start(1, 0)
        ffn_weights(t)
        rs_start(2 + t)
        if t + 1 < nt:
            ag_end(2 + t + 1)
        if t == 0:
            pass

    def middle_back(s):
        incoming = sum_end(1, s)
        value = mid[share_at(s), :]
        factor = lax.rsqrt(mean_square(value) + EPSILON)
        hat = value * factor
        small[1:2, :] += jnp.sum(incoming * hat, axis=0, keepdims=True)
        grad_hat = incoming * r.gain_w[1:2, :]
        back = factor * (grad_hat - hat * jnp.mean(grad_hat * hat, axis=-1, keepdims=True))
        total = dy[token_rows(s, chip, core), :].astype(F32) + back
        grad_hidden[share_at(s), :] = total
        spread1_start(1, s, total.astype(BF16))

    sum2_start(1, 1)
    middle_back(0)
    middle_back(1)
    for s in range(seqs):
        acc_low(acc_m, part, s)
        sum1_start(3, s)
    spread2_start(1, 0)

    def again(first, count):
        def one(i):
            at = pl.ds(pl.multiple_of(first + i * tb, tb), tb)
            value = x[at, :].astype(F32)
            value = value * lax.rsqrt(mean_square(value) + EPSILON)
            value = (value * r.gain_w[0:1, :]).astype(BF16).astype(F32)
            hn_t[:, at] = value.T.astype(BF16)

        each(count, one)

    rs_join(2)
    spread2_start(1, 1)
    for s in range(seqs):
        sum2_start(3, s)

    g_kv, gq_t = r.g_kv, r.gq_t

    def out_back(s):
        def one(i):
            at = pl.ds(pl.multiple_of(s * local + i * rb, rb), rb)
            value = dot(hn[at, :], mat_o[...])
            for h in range(qh):
                piece = value[:, h * head : (h + 1) * head]
                start = nqkv + h * 2 * head
                units[at, start : start + 2 * head] = jnp.concatenate(
                    [jnp.zeros_like(piece), piece], axis=1
                ).astype(BF16)

        each(local // rb, one)

    def attend_back(s, with_peer):
        for h in range(kh):
            g_kv[s * kh + h] = jnp.zeros_like(g_kv[s * kh + h])

        def one(index):
            for j in range(local // qb):
                parts, head_kv, here = masked(s, j, index, with_peer)
                at = slice(j * qb, (j + 1) * qb)
                token = slice(s * local + j * qb, s * local + (j + 1) * qb)
                lanes = pl.ds(pl.multiple_of(nqkv + index * 2 * head, 128), 2 * head)
                go = units[token, lanes]
                logs = lse[s * qh + index, :, at]
                probs = [jnp.exp(p[0] - logs) for p in parts]
                grad_probs = [dot_nt(kv[head_kv, w, :size, :], go) for _, w, size in parts]
                row_dot = sum(
                    jnp.sum(p * g, axis=0, keepdims=True) for p, g in zip(probs, grad_probs)
                )
                out = jnp.zeros((2 * head, qb), F32)
                for (_, w, size), p, g in zip(parts, probs, grad_probs):
                    gs = (p * (g - row_dot)).astype(BF16)
                    out += dot(kv_t[head_kv, w, :, :size], gs)
                    g_kv[head_kv, w, :size, :] += dot(gs, here) + dot(p.astype(BF16), go)
                spot = pl.ds(pl.multiple_of(index * head, head), head)
                gq_t[s, spot, at] = out[:head, :] * scale

        each(qh, one)

    def back_copy(s):
        return Copy(
            r.g_kv_low.at[pl.ds(s * kh, kh)],
            r.g_kv_in.at[pl.ds(s * kh, kh)],
            two.gkv,
            s,
            {"ctx": peer},
        )

    def attend_back_any(s):
        @pl.when(side == 0)
        def _():
            attend_back(s, False)

        @pl.when(side != 0)
        def _():
            attend_back(s, True)
            for h in range(kh):
                r.g_kv_low[s * kh + h] = g_kv[s * kh + h, 1].astype(BF16)
            back_copy(s).start()

    def kv_back_arrive(s):
        @pl.when(side == 0)
        def _():
            back_copy(s).wait_recv()
            for h in range(kh):
                g_kv[s * kh + h, 0] += r.g_kv_in[s * kh + h].astype(F32)

        @pl.when(side != 0)
        def _():
            back_copy(s).wait_send()

    def project_back(s):
        def one(i):
            at = pl.ds(pl.multiple_of(s * local + i * rb, rb), rb)
            inner = pl.ds(aligned(i, rb), rb)
            gkv = [g_kv[s * kh + h, 0, inner, :] for h in range(kh)]
            if kh == 1:
                g_key, g_value = gkv[0][:, :head], gkv[0][:, head:]
            else:
                keys, values = [], []
                for h in range(0, kh, 2):
                    keys.append(jnp.where(low_half, gkv[h], pltpu.roll(gkv[h + 1], head, 1)))
                    values.append(jnp.where(low_half, pltpu.roll(gkv[h], head, 1), gkv[h + 1]))
                g_key = jnp.concatenate(keys, axis=1)
                g_value = jnp.concatenate(values, axis=1)
            value = jnp.concatenate([gq_t[s, :, inner].T, g_key], axis=1)
            cosine = widen(tab[at, : 2 * head], nqk)
            sine = widen(tab[at, 2 * head :], nqk)
            value = value * cosine - swap_halves(value, head) * sine
            plain = raw[at, :]
            factor = lax.rsqrt(spread_means(plain * plain, head) + EPSILON)
            hat = plain * factor
            small[2:3, :nqk] += jnp.sum(value * hat, axis=0, keepdims=True)
            grad_hat = value * r.gain_h[0:1, :]
            value = factor * (grad_hat - hat * spread_means(grad_hat * hat, head))
            low = jnp.concatenate([value, g_value], axis=1).astype(BF16)
            units[at, :nqkv] = low
            part[at, :] = dot_nt(low, mat_q[...]).astype(BF16)

        each(local // rb, one)

    def out_weights():
        for i in range(width // rb):
            total = sum(
                dot(o_t[s], hn[s * local : (s + 1) * local, i * rb : (i + 1) * rb])
                for s in range(seqs)
            )
            r.grad_o[i * rb : (i + 1) * rb, :] = total.T.astype(BF16)

    def qkv_weights():
        def one(i):
            at = pl.ds(aligned(i, rb), rb)
            r.grad_q[at, :] = dot(hn_t[at, :], units[:, :nqkv]).astype(BF16)

        each(width // rb, one)

    spread_end(1, 0)
    out_back(0)
    attend_back_any(0)
    spread_end(1, 1)
    out_back(1)
    if nt > 1:
        rs_mid(3)
    rs_fin(2)
    again(0, rows // tb)
    attend_back_any(1)
    out_weights()
    rs_start(1)
    if nt > 1:
        rs_join(3)

    def mlp_end(s):
        mlp = sum_end(3, s)
        weight = keep_of(s)[:, 0:1]
        small[4:5, 384:512] += fold_lanes(weight * mlp * mlp)
        small[4:5, 512:640] += jnp.sum(keep_of(s), axis=0, keepdims=True)
        mid[share_at(s), :] += mlp

    for s in range(seqs):
        mlp_end(s)
    kv_back_arrive(0)
    project_back(0)
    sum1_start(2, 0)
    first_sum()
    if nt > 2:
        rs_mid(4)
    kv_back_arrive(1)
    project_back(1)
    sum1_start(2, 1)
    sum2_start(2, 0)
    qkv_weights()
    rs_start(0)
    sum2_start(2, 1)
    if nt > 1:
        rs_fin(3)
    rs_mid(1)

    def first_back(s):
        incoming = sum_end(2, s)
        value = x[token_rows(s, chip, core), :].astype(F32)
        factor = lax.rsqrt(mean_square(value) + EPSILON)
        hat = value * factor
        small[0:1, :] += jnp.sum(incoming * hat, axis=0, keepdims=True)
        grad_hat = incoming * r.gain_w[0:1, :]
        back = factor * (grad_hat - hat * jnp.mean(grad_hat * hat, axis=-1, keepdims=True))
        grad_hidden[share_at(s), :] += back

    first_back(0)
    if nt > 2:
        rs_join(4)
    first_back(1)
    rs_mid(0)

    small_in = r.small_in

    def small_round(start, copies, order):
        for c in copies:
            c.start()
        for c in copies:
            c.wait_recv()
            c.wait_send()
        total = None
        for o in order:
            term = small_in[start + o]
            total = term if total is None else total + term
        small[...] = total

    small_in[pl.ds(core, 1)] = small[...][None]
    small_round(
        0, [Copy(small, small_in.at[core], two.small, 0, {"tp": other_core})], range(2)
    )
    small_in[pl.ds(2 + side, 1)] = small[...][None]
    small_round(2, [Copy(small, small_in.at[2 + side], two.small, 1, {"ctx": peer})], range(2))
    small_in[pl.ds(4 + chip, 1)] = small[...][None]
    small_round(
        4,
        [
            Copy(small, small_in.at[4 + chip], two.small, 1 + s, {"tp": chip_lane(s)})
            for s in range(1, chips)
        ],
        range(chips),
    )
    rs_fin(1)
    if nt > 2:
        rs_fin(4)
    small_in[pl.ds(4 + chips + me, 1)] = small[...][None]
    small_round(
        4 + chips,
        [
            Copy(small, small_in.at[4 + chips + me], two.small, chips + s, {"dp": dp_at(s)})
            for s in range(1, dp)
        ],
        range(dp),
    )
    def mine_of(value, size):
        return sum(
            jnp.where(me == d, value[:, d * size : (d + 1) * size], 0.0) for d in range(dp)
        )

    r.own_attn[...] = mine_of(small[0:1, :], dd)
    r.own_ffn[...] = mine_of(small[1:2, :], dd)
    row = small[2:3, :nqk]
    over_q = sum(row[:, h * head : (h + 1) * head] for h in range(qh))
    over_k = sum(row[:, h * head : (h + 1) * head] for h in range(qh, qh + kh))
    r.own_query[...] = mine_of(over_q, piece)
    r.own_key[...] = mine_of(over_k, piece)
    totals = [
        jnp.sum(small[4:5, i * 128 : (i + 1) * 128], axis=1, keepdims=True) for i in range(4)
    ]
    count = small[4:5, 512:513] * width
    r.own_stat[...] = jnp.sqrt(jnp.concatenate(totals, axis=1) / count)
    rs_fin(0)
    for c in list(range(2, nt + 2)) + [1, 0]:
        rs_end(c)


def per_device(
    sizes,
    hidden_states,
    out_grad,
    w_query,
    w_key,
    w_value,
    w_out,
    w_gate,
    w_up,
    w_down,
    attn_gain,
    ffn_gain,
    query_gain,
    key_gain,
    segment_ids,
    valid_mask,
    positions,
):
    seqs, local, width = hidden_states.shape
    dp, ctx, tp = sizes
    rows = seqs * local
    head = query_gain.shape[0] * dp
    nq, nk, units = w_query.shape[1], w_key.shape[1], w_gate.shape[1]
    nqkv = nq + 2 * nk
    nt = 3 if units % 3 == 0 else 1
    ft = units // nt
    dd = width // dp
    hd = dd // ctx
    share = local // tp
    chips = tp // 2
    qh, kh = nq // head, nk // head
    plain = ft % 128 == 0 and dd % 128 == 0 and nk % 128 == 0
    cfg = types.SimpleNamespace(
        seqs=seqs, local=local, width=width, head=head, dp=dp, ctx=ctx, tp=tp,
        qh=qh, kh=kh, nt=nt, ft=ft, plain=plain,
    )
    side = lax.axis_index("ctx")

    def wide(value):
        return jnp.pad(value.astype(F32), (0, dd - value.shape[0]))[None]

    gains = jnp.concatenate(
        [wide(attn_gain), wide(ffn_gain), wide(query_gain), wide(key_gain), jnp.zeros((4, dd), F32)]
    )
    token = side * local + jnp.arange(local)
    codes = jnp.where(valid_mask == 1, segment_ids, 100000 + token[None, :])
    facts = jnp.stack([codes, positions], axis=1).astype(F32)
    half = head // 2
    freq = np.float32(ROPE_BASE) ** (-(np.arange(half, dtype=np.float32) * 2.0) / head)
    freq = jnp.asarray(np.tile(freq.astype(np.float32), 128 // half)[None])
    inputs = dict(
        x=(hidden_states.reshape(rows, width), True),
        dy=(out_grad.reshape(rows, width), True),
        gains=(gains, True),
        facts=(facts, True),
        freq=(freq, True),
    )
    if plain:
        inputs.update(
            w_query=(w_query, False),
            w_key=(w_key, False),
            w_value=(w_value, False),
            w_out=(w_out, False),
            w_gate=(w_gate, False),
            w_up=(w_up, False),
            w_down=(w_down, False),
        )
    else:
        tiles = []
        for i in range(nt):
            cut = slice(i * ft, (i + 1) * ft)
            tiles.append(jnp.concatenate([w_gate[:, cut], w_up[:, cut], w_down[cut].T], axis=1))
        inputs.update(
            w_qkv=(jnp.concatenate([w_query, w_key, w_value], axis=1), False),
            w_o=(w_out.T, False),
            w_f=(jnp.stack(tiles), False),
        )
    outputs = dict(
        result=((seqs * share, width), F32),
        grad_hidden=((seqs * share, width), F32),
        fin_q=((dd, nqkv), BF16),
        fin_o=((dd, nq), BF16),
        fin_f=((nt, dd, 3 * ft), BF16),
        own_attn=((1, dd), F32),
        own_ffn=((1, dd), F32),
        own_query=((1, head // dp), F32),
        own_key=((1, head // dp), F32),
        own_stat=((1, 4), F32),
    )
    scratch = dict(
        mat_q=((width, nqkv), BF16),
        mat_o=((width, nq), BF16),
        mat_f=((nt, width, 3 * ft), BF16),
        gain_buf=((dp, 8, dd), F32),
        gain_w=((8, width), F32),
        gain_h=((8, nq + nk), F32),
        code_peer=((seqs, 2, local), F32),
        tab=((rows, 256), F32),
        key_code=((ctx, seqs, local, 128), F32),
        hn=((rows, width), BF16),
        hn_t=((width, rows), BF16),
        dr_t=((width, rows), BF16),
        raw=((rows, nq + nk), F32),
        q_pad=((seqs * qh, local, 2 * head), BF16),
        kv=((seqs * kh, ctx, local, 2 * head), BF16),
        kv_t=((seqs * kh, ctx, 2 * head, local), BF16),
        g_kv=((seqs * kh, ctx, local, 2 * head), F32),
        g_kv_low=((seqs * kh, local, 2 * head), BF16),
        g_kv_in=((seqs * kh, local, 2 * head), BF16),
        o_t=((seqs, nq, local), BF16),
        gq_t=((seqs, nq, local), F32),
        lse=((seqs * qh, 1, local), F32),
        part=((rows, width), BF16),
        near=((2, seqs, chips, share, width), BF16),
        pair=((seqs, chips, share, width), BF16),
        far=((2, seqs, max(chips - 1, 1), share, width), BF16),
        small=((8, width), F32),
        small_in=((4 + chips + dp, 8, width), F32),
        units=((rows, 3 * ft), BF16),
        acc_m=((rows, width), F32),
        acc_h=((rows, width), F32),
        grad_q=((width, nqkv), BF16),
        grad_o=((width, nq), BF16),
        y_q=((dp, hd, nqkv), BF16),
        y_o=((dp, hd, nq), BF16),
        y_f=((nt - 1, dp, hd, 3 * ft), BF16),
        z_q=((dp - 1, hd, nqkv), BF16),
        z_o=((dp - 1, hd, nq), BF16),
        z_f=((nt - 1, dp - 1, hd, 3 * ft), BF16),
    )
    scratch.update(
        y_a=((dd, 3 * ft), BF16),
        z_a=((dp - 1, dd, 3 * ft), BF16),
        fold_a=((dd, 3 * ft), BF16),
        fold_f=((nt - 1, hd, 3 * ft), BF16),
    )
    pairs = dict(
        agz=(nt + 2, dp - 1),
        agy=(nt + 2, dp - 1),
        gain=(dp - 1,),
        code=(1,),
        kv=(seqs,),
        gkv=(seqs,),
        sum1=(4, seqs * chips),
        sum2=(4, seqs * max(chips - 1, 1)),
        spread1=(2, seqs * max(chips - 1, 1)),
        spread2=(2, seqs * chips),
        rsy=(nt + 2, dp),
        rsz=(nt + 2, dp - 1),
        rsf=(nt + 2,),
        small=(chips + dp,),
        rsn=(nt + 2,),
        firsty=(1,),
    )
    singles = dict(own_sem=(nt + 2, 3), agfar=(nt + 2,), fin_sem=(nt + 2,))
    shapes = list(singles.values()) + [v for v in pairs.values() for _ in range(2)]

    def kernel(*refs):
        refs = list(refs)
        r = types.SimpleNamespace()
        for name in list(inputs) + list(outputs) + list(scratch) + list(singles):
            setattr(r, name, refs.pop(0))
        two = types.SimpleNamespace()
        for name in pairs:
            setattr(two, name, (refs.pop(0), refs.pop(0)))
        block_kernel(cfg, r, two)

    vmem = pl.BlockSpec(memory_space=pltpu.VMEM)
    away = pl.BlockSpec(memory_space=pl.ANY)
    out = pl.pallas_call(
        kernel,
        out_shape=[jax.ShapeDtypeStruct(*v) for v in outputs.values()],
        in_specs=[vmem if v else away for _, v in inputs.values()],
        out_specs=[away if n.startswith("fin") else vmem for n in outputs],
        scratch_shapes=[pltpu.VMEM(*v) for v in scratch.values()]
        + [pltpu.SemaphoreType.DMA(v) for v in shapes],
        compiler_params=pltpu.CompilerParams(
            collective_id=0, has_side_effects=True, vmem_limit_bytes=VMEM_LIMIT
        ),
    )(*[v for v, _ in inputs.values()])
    result, grad_hidden, fin_q, fin_o, fin_f = out[:5]

    gates = [fin_f[i, :, :ft] for i in range(nt)]
    ups = [fin_f[i, :, ft : 2 * ft] for i in range(nt)]
    downs = [fin_f[i, :, 2 * ft :] for i in range(nt)]
    return (
        result.reshape(seqs, share, width),
        grad_hidden.reshape(seqs, share, width),
        fin_q[:, :nq].astype(F32),
        fin_q[:, nq : nq + nk].astype(F32),
        fin_q[:, nq + nk :].astype(F32),
        fin_o.T.astype(F32),
        jnp.concatenate(gates, axis=1).astype(F32),
        jnp.concatenate(ups, axis=1).astype(F32),
        jnp.concatenate([d.T for d in downs], axis=0).astype(F32),
        *[value.reshape(-1) for value in out[5:]],
    )


VMEM_LIMIT = 63 * 2**20


def solution(mesh):
    sizes = tuple(mesh.shape[a] for a in ("dp", "ctx", "tp"))
    return jax.shard_map(
        functools.partial(per_device, sizes),
        mesh=mesh,
        in_specs=(
            P("dp", "ctx", None),
            P("dp", "ctx", None),
            P("dp", "tp"),
            P("dp", "tp"),
            P("dp", "tp"),
            P("tp", "dp"),
            P("dp", "tp"),
            P("dp", "tp"),
            P("tp", "dp"),
            P("dp"),
            P("dp"),
            P("dp"),
            P("dp"),
            P("dp", "ctx"),
            P("dp", "ctx"),
            P("dp", "ctx"),
        ),
        out_specs=(
            P("dp", ("ctx", "tp"), None),
            P("dp", ("ctx", "tp"), None),
            P("dp", "tp"),
            P("dp", "tp"),
            P("dp", "tp"),
            P("tp", "dp"),
            P("dp", "tp"),
            P("dp", "tp"),
            P("tp", "dp"),
            P("dp"),
            P("dp"),
            P("dp"),
            P("dp"),
            P(),
        ),
        check_vma=False,
    )
```

```python
import functools
import types

import jax
import jax.numpy as jnp
import numpy as np
from jax import lax
from jax.experimental import pallas as pl
from jax.experimental.pallas import tpu as pltpu
from jax.sharding import PartitionSpec as P

EPSILON = 1e-05
ROPE_BASE = 1000000.0
F32 = jnp.float32
BF16 = jnp.bfloat16
MESH = pl.DeviceIdType.MESH
NEGATIVE = -1e30
PADDING = 50000.0


def dot(left, right):
    return jnp.dot(left, right, preferred_element_type=F32)


def dot_nt(left, right):
    return lax.dot_general(left, right, (((1,), (1,)), ((), ())), preferred_element_type=F32)


def each(count, body):
    def step(i, carry):
        body(i)
        return carry

    lax.fori_loop(0, count, step, 0)


def aligned(index, unit):
    return pl.multiple_of(index * unit, unit)


def mean_square(value):
    return jnp.mean(value * value, axis=-1, keepdims=True)


def swap_halves(value, head):
    half = head // 2
    size = value.shape[1]
    if size % 128 == 0:
        at = lax.broadcasted_iota(jnp.int32, (1, size), 1)
        first = lax.rem(at, head) < half
        return jnp.where(first, pltpu.roll(value, size - half, 1), pltpu.roll(value, half, 1))
    pieces = []
    for start in range(0, size, head):
        pieces += [value[:, start + half : start + head], value[:, start : start + half]]
    return jnp.concatenate(pieces, axis=1)


def spread_means(value, head):
    size = value.shape[1]
    row = lax.div(lax.broadcasted_iota(jnp.int32, (size, size), 0), head)
    column = lax.div(lax.broadcasted_iota(jnp.int32, (size, size), 1), head)
    block = jnp.where(row == column, 1.0 / head, 0.0).astype(BF16)
    high = value.astype(BF16)
    rest = (value - high.astype(F32)).astype(BF16)
    return dot(high, block) + dot(rest, block)


def widen(value, count):
    size = value.shape[1]
    if count <= size:
        return value[:, :count]
    return jnp.concatenate([value] * -(-count // size), axis=1)[:, :count]


def fold_lanes(value):
    total = jnp.sum(value, axis=0, keepdims=True)
    out = total[:, :128]
    for i in range(1, value.shape[1] // 128):
        out += total[:, i * 128 : (i + 1) * 128]
    return out


class Copy:
    def __init__(self, src, dst, sems, index, device, send=None):
        send = sems[0].at[index] if send is None else send
        self.copy = pltpu.make_async_remote_copy(
            src_ref=src,
            dst_ref=dst,
            send_sem=send,
            recv_sem=sems[1].at[index],
            device_id=device,
            device_id_type=MESH,
        )

    def start(self):
        self.copy.start()

    def wait_send(self):
        self.copy.wait_send()

    def wait_recv(self):
        self.copy.wait_recv()


def block_kernel(cfg, r, two):
    seqs, local, width, head = cfg.seqs, cfg.local, cfg.width, cfg.head
    dp, ctx, tp = cfg.dp, cfg.ctx, cfg.tp
    qh, kh, nt, ft = cfg.qh, cfg.kh, cfg.nt, cfg.ft
    nq, nk = qh * head, kh * head
    nqkv = nq + 2 * nk
    group = qh // kh
    chips = tp // 2
    rows = seqs * local
    share = local // tp
    dd = width // dp
    hd = dd // ctx
    me, side, lane = lax.axis_index("dp"), lax.axis_index("ctx"), lax.axis_index("tp")
    core, chip = lax.rem(lane, 2), lax.div(lane, 2)
    other_core = lane + 1 - 2 * core
    peer = 1 - side
    rb = min(256, local)
    qb = min(256, local)
    tb = min(128, local)
    scale = head**-0.5

    def dp_at(step):
        return lax.rem(me + step, dp)

    def chip_lane(step):
        return lax.rem(chip + step, chips) * 2 + core

    barrier = pltpu.get_barrier_semaphore()
    greet = [{"dp": dp_at(s)} for s in range(1, dp)] + [{"ctx": peer}, {"tp": other_core}]
    greet += [{"tp": chip_lane(s)} for s in range(1, chips)]
    for device in greet:
        pl.semaphore_signal(barrier, inc=1, device_id=device, device_id_type=MESH)
    pl.semaphore_wait(barrier, len(greet))

    whole = [r.mat_q, r.mat_o] + [r.mat_f.at[t] for t in range(nt)]

    def my_rows(owner, which):
        return pl.ds(pl.multiple_of(owner * dd + which * hd, hd), hd)

    solo = ()

    def ag_rows(c, owner):
        if c in solo:
            return pl.ds(aligned(owner, dd), dd)
        return my_rows(owner, side)

    def ag_z(c, step):
        return Copy(
            whole[c].at[ag_rows(c, me)],
            whole[c].at[ag_rows(c, me)],
            two.agz,
            (c, step - 1),
            {"dp": dp_at(step)},
        )

    def ag_y(c, step):
        owner = lax.rem(me - step + dp, dp)
        area = whole[c].at[my_rows(owner, side)]
        return Copy(area, area, two.agy, (c, step - 1), {"ctx": peer})

    relayed = (0,) + tuple(range(2, nt + 2)) if dp > 2 else ()
    hops = [dp - 2, 2] if dp > 2 else []
    order = sorted(range(1, dp), key=lambda step: (step not in hops, step))

    def ag_far(c, step):
        owner, target = (0, dp - 1) if step == dp - 2 else (dp - 1, 0)
        if dp == 4:
            owner = jnp.where(me == 1, dp - 1, 0)
            target = jnp.where(me == 1, 0, dp - 1)
        area = whole[c].at[ag_rows(c, owner)]
        index = lax.rem(target - owner + dp, dp) - 1
        send = r.agfar.at[c]
        return Copy(area, area, two.agz, (c, index), {"dp": target}, send)

    def far_when(c, step, body):
        if c not in relayed:
            return
        if dp == 4:
            if step == 2:
                pl.when((me == 1) | (me == 2))(body)
        elif step == dp - 2:
            pl.when(me == dp - 2)(body)
        elif step == 2:
            pl.when(me == 1)(body)

    def near_when(c, step, body):
        if c in relayed and step == dp - 1:
            pl.when(me != 0)(body)
        elif c in relayed and step == 1:
            pl.when(me != dp - 1)(body)
        else:
            body()

    own_rows = pl.ds(aligned(me, dd), dd)

    def stage(c):
        if c == 1:
            return r.units.at[pl.ds(ft, nq), pl.ds(0, dd)]
        return r.units.at[pl.ds(0, ft), pl.ds((c - 2) * dd, dd)]

    def own_moves(c):
        if not cfg.plain:
            source = [r.w_qkv, r.w_o] + [r.w_f.at[t] for t in range(nt)]
            pairs_of = [(source[c], whole[c].at[own_rows])]
        elif c == 0:
            pairs_of, start = [], 0
            for source in (r.w_query, r.w_key, r.w_value):
                size = source.shape[1]
                pairs_of.append((source, r.mat_q.at[own_rows, pl.ds(start, size)]))
                start += size
        elif c == 1:
            pairs_of = [(r.w_out, stage(1))]
        else:
            t = c - 2
            at = pl.ds(t * ft, ft)
            pairs_of = [
                (r.w_gate.at[:, at], r.mat_f.at[t, own_rows, pl.ds(0, ft)]),
                (r.w_up.at[:, at], r.mat_f.at[t, own_rows, pl.ds(ft, ft)]),
                (r.w_down.at[at], stage(c)),
            ]
        return [
            pltpu.make_async_copy(source, target, r.own_sem.at[c, i])
            for i, (source, target) in enumerate(pairs_of)
        ]

    def own_start(c):
        for move in own_moves(c):
            move.start()

    def own_end(c):
        for move in own_moves(c):
            move.wait()
        if cfg.plain and c >= 1:
            block = stage(c)[...].astype(F32).T.astype(BF16)
            if c == 1:
                r.mat_o[own_rows, :] = block
            else:
                r.mat_f[c - 2, own_rows, 2 * ft :] = block

    def ag_start(c, early=True, late=True):
        if c >= nt + 2:
            return
        for step in order:
            if not (early if step in hops else late):
                continue
            near_when(c, step, lambda: ag_z(c, step).start())

    def ag_pass_one(c, step):
        ag_z(c, step).wait_recv()
        far_when(c, step, lambda: ag_far(c, step).start())
        if c not in solo:
            ag_y(c, step).start()

    served = set()

    def serve(c, early=True, late=True):
        for step in order:
            if c < nt + 2 and (c, step) not in served and (early if step in hops else late):
                served.add((c, step))
                ag_pass_one(c, step)

    def ag_end(c):
        serve(c)
        for step in order:
            if c not in solo:
                ag_y(c, step).wait_recv()
                ag_y(c, step).wait_send()
            near_when(c, step, lambda: ag_z(c, step).wait_send())
            far_when(c, step, lambda: ag_far(c, step).wait_send())

    gain_buf = r.gain_buf

    def gain_copy(step):
        return Copy(
            r.gains, gain_buf.at[me], two.gain, step - 1, {"dp": dp_at(step)}
        )

    for s in range(seqs):
        token = lax.broadcasted_iota(jnp.int32, (1, local), 1) + side * local + 100000
        real = r.valid_mask[s : s + 1, :] == 1
        code = jnp.where(real, r.segment_ids[s : s + 1, :], token)
        r.facts[s, 0:1, :] = code.astype(F32)
        r.facts[s, 1:2, :] = r.positions[s : s + 1, :].astype(F32)

    def code_copy():
        return Copy(r.facts, r.code_peer, two.code, 0, {"ctx": peer})

    for c in range(nt + 2):
        own_start(c)
    for step in range(1, dp):
        gain_copy(step).start()
    own_end(0)
    ag_start(0)
    code_copy().start()
    for c in range(1, nt + 2):
        own_end(c)

    x, dy, hn, hn_t, dr_t = r.x, r.dy, r.hn, r.hn_t, r.dr_t

    def transpose_into(source, target, first, count):
        def one(i):
            at = pl.ds(pl.multiple_of(first + i * tb, tb), tb)
            target[:, at] = source[at, :].astype(F32).T.astype(BF16)

        each(count, one)

    def code_columns(source, which):
        for s in range(seqs):
            row = jnp.broadcast_to(source[s, 0:1, :], (128, local))
            r.key_code[which, s] = row.T

    code_columns(r.facts, 0)

    sign = lax.rem(lax.broadcasted_iota(jnp.int32, (1, 128), 1), head) < head // 2
    sign = jnp.where(sign, -1.0, 1.0).astype(F32)
    for s in range(seqs):
        for start in range(0, local, tb):
            place = jnp.broadcast_to(r.facts[s, 1:2, start : start + tb], (128, tb)).T
            angle = place * r.freq[...]
            at = pl.ds(s * local + start, tb)
            r.tab[at, :128] = jnp.cos(angle)
            r.tab[at, 128:] = jnp.sin(angle) * sign

    gain_buf[pl.ds(me, 1)] = r.gains[...][None]
    for step in range(1, dp):
        gain_copy(step).wait_recv()
        gain_copy(step).wait_send()
    piece = head // dp
    for d in range(dp):
        r.gain_w[0:1, d * dd : (d + 1) * dd] = gain_buf[d, :, :dd]
        r.gain_w[1:2, d * dd : (d + 1) * dd] = gain_buf[d, :, dd : 2 * dd]
        for h in range(qh):
            start = h * head + d * piece
            r.gain_h[0:1, start : start + piece] = gain_buf[d, :, 2 * dd : 2 * dd + piece]
        for h in range(kh):
            start = nq + h * head + d * piece
            r.gain_h[0:1, start : start + piece] = gain_buf[d, :, 2 * dd + piece : 2 * dd + 2 * piece]

    def normed_into(target, first, count):
        def one(i):
            at = pl.ds(pl.multiple_of(first + i * tb, tb), tb)
            value = x[at, :].astype(F32)
            value = value * lax.rsqrt(mean_square(value) + EPSILON)
            target[at, :] = (value * r.gain_w[0:1, :]).astype(BF16)

        each(count, one)

    normed_into(hn, 0, rows // tb // 2)
    serve(0, late=False)
    normed_into(hn, rows // 2, rows // tb // 2)
    code_copy().wait_recv()
    code_copy().wait_send()
    code_columns(r.code_peer, 1)
    ag_start(2, late=False)
    serve(0)
    ag_start(1)
    transpose_into(dy, dr_t, 0, rows // tb)
    ag_start(2, early=False)
    ag_end(0)

    mat_q, mat_o, raw, tab = r.mat_q, r.mat_o, r.raw, r.tab
    q_pad, kv, kv_t = r.q_pad, r.kv, r.kv_t

    nqk = nq + nk
    low_half = lax.broadcasted_iota(jnp.int32, (1, 2 * head), 1) < head

    def pairs(value, start, count):
        out = []
        for h in range(0, count, 2):
            if count == 1:
                here = value[:, start : start + head]
                both = jnp.concatenate([here, here], axis=1)
                out.append((both, both))
                continue
            here = value[:, start + h * head : start + (h + 2) * head]
            turned = pltpu.roll(here, head, 1)
            out += [(here, turned), (turned, here)]
        return out

    def project(s):
        def one(i):
            at = pl.ds(pl.multiple_of(s * local + i * rb, rb), rb)
            inner = pl.ds(aligned(i, rb), rb)
            both = dot(hn[at, :], mat_q[...])
            plain = both[:, :nqk]
            raw[at, :] = plain
            cosine = widen(tab[at, : 2 * head], nqk)
            sine = widen(tab[at, 2 * head :], nqk)
            value = plain * lax.rsqrt(spread_means(plain * plain, head) + EPSILON)
            value = value * r.gain_h[0:1, :]
            value = value * cosine + swap_halves(value, head) * sine
            for h, (low, _) in enumerate(pairs(value, 0, qh)):
                q_pad[s * qh + h, inner, :] = jnp.where(low_half, low * scale, 0.0).astype(BF16)
            keys = pairs(value, nq, kh)
            values = pairs(both, nqk, kh)
            for h in range(kh):
                kv[s * kh + h, 0, inner, :] = jnp.where(
                    low_half, keys[h][0], values[h][1]
                ).astype(BF16)

        each(local // rb, one)

    def kv_copy(s):
        return Copy(
            kv.at[pl.ds(s * kh, kh), 0],
            kv.at[pl.ds(s * kh, kh), 1],
            two.kv,
            s,
            {"ctx": peer},
        )

    def kv_transpose(s, which):
        for h in range(kh):
            kv_t[s * kh + h, which] = kv[s * kh + h, which].astype(F32).T.astype(BF16)

    for s in range(seqs):
        project(s)

        @pl.when(side == 0)
        def _():
            kv_copy(s).start()

        kv_transpose(s, 0)
        if s == 0:
            serve(2, late=False)
            serve(1)
            ag_start(3, late=False)

    o_t, lse = r.o_t, r.lse

    def masked(s, j, index, with_peer):
        last = (j + 1) * qb
        head_kv = s * kh + index // group
        here = q_pad[s * qh + index, j * qb : last, :]
        query = r.facts[s, 0:1, j * qb : last]

        def spread(code):
            return jnp.concatenate([code] * (qb // 128), axis=1)

        own = dot_nt(kv[head_kv, 0, :last, :], here)
        key_at = lax.broadcasted_iota(jnp.int32, (last, qb), 0)
        query_at = lax.broadcasted_iota(jnp.int32, (last, qb), 1) + j * qb
        allowed = (spread(r.key_code[0, s, :last, :]) == query) & (key_at <= query_at)
        own = jnp.where(allowed, own, NEGATIVE)
        parts = [(own, 0, last)]
        if with_peer:
            far = dot_nt(kv[head_kv, 1], here)
            far = jnp.where(spread(r.key_code[1, s]) == query, far, NEGATIVE)
            parts.append((far, 1, local))
        return parts, head_kv, here

    def attend_one(s, index, with_peer):
        for j in range(local // qb):
            parts, head_kv, _ = masked(s, j, index, with_peer)
            highest = functools.reduce(
                jnp.maximum, [jnp.max(p[0], axis=0, keepdims=True) for p in parts]
            )
            expo = [jnp.exp(p[0] - highest) for p in parts]
            total = sum(jnp.sum(e, axis=0, keepdims=True) for e in expo)
            factor = 1.0 / total
            out = jnp.zeros((2 * head, qb), F32)
            for (_, which, size), e in zip(parts, expo):
                out += dot(kv_t[head_kv, which, :, :size], (e * factor).astype(BF16))
            at = pl.ds(pl.multiple_of(index * head, head), head)
            o_t[s, at, j * qb : (j + 1) * qb] = out[head:, :].astype(BF16)
            lse[s * qh + index, :, j * qb : (j + 1) * qb] = highest + jnp.log(total)

    def attend(s, first, count):
        def one(i):
            @pl.when(side == 0)
            def _():
                attend_one(s, first + i, False)

            @pl.when(side != 0)
            def _():
                attend_one(s, first + i, True)

        each(count, one)

    def kv_arrive(s):
        @pl.when(side == 0)
        def _():
            kv_copy(s).wait_send()

        @pl.when(side != 0)
        def _():
            kv_copy(s).wait_recv()
            kv_transpose(s, 1)

    part, near, pair, far = r.part, r.near, r.pair, r.far

    def pool(use):
        return 1 if use == 3 else 0

    def token_rows(s, which_chip, which_core):
        start = s * local + (which_chip * 2 + which_core) * share
        return pl.ds(pl.multiple_of(start, share), share)

    def sum1(use, s, c):
        return Copy(
            part.at[token_rows(s, c, 1 - core)],
            near.at[pool(use), s, c],
            two.sum1,
            (use, s * chips + c),
            {"tp": other_core},
        )

    def sum1_start(use, s):
        for c in range(chips):
            sum1(use, s, c).start()

    def sum2(use, s, step):
        return Copy(
            pair.at[s, lax.rem(chip + step, chips)],
            far.at[pool(use), s, step - 1],
            two.sum2,
            (use, s * max(chips - 1, 1) + step - 1),
            {"tp": chip_lane(step)},
        )

    def sum2_start(use, s):
        for c in range(chips):
            sum1(use, s, c).wait_recv()
        for c in range(chips):
            mine = part[token_rows(s, c, core), :].astype(F32)
            pair[s, c] = (mine + near[pool(use), s, c].astype(F32)).astype(BF16)
        for step in range(1, chips):
            sum2(use, s, step).start()

    def sum_end(use, s):
        for step in range(1, chips):
            sum2(use, s, step).wait_recv()
        total = part[token_rows(s, chip, core), :].astype(F32)
        total += near[pool(use), s, chip].astype(F32)
        for step in range(1, chips):
            total += far[pool(use), s, step - 1].astype(F32)
        for c in range(chips):
            sum1(use, s, c).wait_send()
        for step in range(1, chips):
            sum2(use, s, step).wait_send()
        return total

    def spread1(use, s, step):
        area = hn.at[token_rows(s, chip, core)]
        index = (use, s * max(chips - 1, 1) + step - 1)
        return Copy(area, area, two.spread1, index, {"tp": chip_lane(step)})

    def spread1_start(use, s, value):
        hn[token_rows(s, chip, core), :] = value
        for step in range(1, chips):
            spread1(use, s, step).start()

    def spread2(use, s, c):
        area = hn.at[token_rows(s, c, core)]
        return Copy(area, area, two.spread2, (use, s * chips + c), {"tp": other_core})

    def spread2_start(use, s):
        for step in range(1, chips):
            spread1(use, s, step).wait_recv()
        for c in range(chips):
            spread2(use, s, c).start()

    def spread_end(use, s):
        for c in range(chips):
            spread2(use, s, c).wait_recv()
            spread2(use, s, c).wait_send()
        for step in range(1, chips):
            spread1(use, s, step).wait_send()

    def out_project(s):
        def one(i):
            at = pl.ds(pl.multiple_of(s * local + i * rb, rb), rb)
            inner = pl.ds(aligned(i, rb), rb)
            o_rows = o_t[s, :, inner].astype(F32).T.astype(BF16)
            part[at, :] = dot_nt(o_rows, mat_o[...]).astype(BF16)

        each(local // rb, one)

    small, grad_hidden = r.small, r.grad_hidden
    mid = r.result
    small[...] = jnp.zeros_like(small)

    def share_at(s):
        return pl.ds(s * share, share)

    def keep_of(s):
        code = r.key_code[0, s, pl.ds(aligned(lane, share), share), :]
        return jnp.where(code < PADDING, 1.0, 0.0).astype(F32)

    def middle(s):
        attn = sum_end(0, s)
        value = x[token_rows(s, chip, core), :].astype(F32)
        weight = keep_of(s)[:, 0:1]
        small[4:5, 0:128] += fold_lanes(weight * value * value)
        small[4:5, 128:256] += fold_lanes(weight * attn * attn)
        value = value + attn
        mid[share_at(s), :] = value
        small[4:5, 256:384] += fold_lanes(weight * value * value)
        value = value * lax.rsqrt(mean_square(value) + EPSILON)
        spread1_start(0, s, (value * r.gain_w[1:2, :]).astype(BF16))

    half = qh // 2
    ag_start(3, early=False)
    kv_arrive(0)
    attend(0, 0, qh)
    serve(2)
    ag_end(1)
    out_project(0)
    sum1_start(0, 0)
    serve(3, late=False)
    ag_start(4, late=False)
    kv_arrive(1)
    attend(1, 0, half)
    sum2_start(0, 0)
    ag_start(4, early=False)
    attend(1, half, qh - half)
    out_project(1)
    sum1_start(0, 1)
    middle(0)
    sum2_start(0, 1)
    serve(3)
    spread2_start(0, 0)
    middle(1)
    serve(4, late=False)
    spread_end(0, 0)
    transpose_into(hn, hn_t, 0, local // tb)
    spread2_start(0, 1)
    ag_end(2)

    mat_f, units, acc_m, acc_h = r.mat_f, r.units, r.acc_m, r.acc_h

    def ffn_rows(t, s):
        def one(i):
            at = pl.ds(pl.multiple_of(s * local + i * rb, rb), rb)
            both = dot(hn[at, :], mat_f[t, :, : 2 * ft])
            gate, upward = both[:, :ft], both[:, ft:]
            sigmoid = 1.0 / (1.0 + jnp.exp(-gate))
            grad_inner = dot(dy[at, :], mat_f[t, :, 2 * ft :])
            silu = gate * sigmoid
            grad_up = (grad_inner * silu).astype(BF16)
            grad_gate = (
                grad_inner * upward * sigmoid * (1.0 + gate * (1.0 - sigmoid))
            ).astype(BF16)
            inner = (silu * upward).astype(BF16)
            grads = jnp.concatenate([grad_gate, grad_up], axis=1)
            units[at, : 2 * ft] = grads
            units[at, 2 * ft :] = inner
            back = dot_nt(grads, mat_f[t, :, : 2 * ft])
            ahead = dot_nt(inner, mat_f[t, :, 2 * ft :])
            if t > 0:
                back += acc_h[at, :]
                ahead += acc_m[at, :]
            if t < nt - 1:
                acc_h[at, :] = back
            else:
                part[at, :] = back.astype(BF16)
            acc_m[at, :] = ahead

        each(local // rb, one)

    def ffn_weights(t):
        def one(i):
            at = pl.ds(aligned(i, rb), rb)
            mat_f[t, at, : 2 * ft] = dot(hn_t[at, :], units[:, : 2 * ft]).astype(BF16)
            mat_f[t, at, 2 * ft :] = dot(dr_t[at, :], units[:, 2 * ft :]).astype(BF16)

        each(width // rb, one)

    folds = dp > 2
    grads = [r.grad_q, r.grad_o, None] + [mat_f.at[t] for t in range(1, nt)]
    y_in = [r.y_q, r.y_o, None] + [r.y_f.at[t] for t in range(nt - 1)]
    z_in = [r.z_q, r.z_o, None] + [r.z_f.at[t] for t in range(nt - 1)]
    fold = [None, None, r.fold_a] + [r.fold_f.at[t] for t in range(nt - 1)]
    fin = [r.fin_q, r.fin_o] + [r.fin_f.at[t] for t in range(nt)]

    def fold_of(c):
        return folds and fold[c] is not None

    def send_when(c, step, direct, other, defer):
        if not fold_of(c):
            direct()
            return
        away = []
        if step == dp - 1:
            pl.when(me == 0)(other)
            away.append(me == 0)
        if step == 1:
            pl.when(me == dp - 1)(other)
            away.append(me == dp - 1)
        if step == dp - 2:
            pl.when(me == 1)(defer)
            away.append(me == 1)
        if step == 2:
            pl.when(me == dp - 2)(defer)
            away.append(me == dp - 2)
        if not away:
            direct()
            return
        away = functools.reduce(jnp.logical_or, away)
        pl.when(jnp.logical_not(away))(direct)

    def fold_when(c, body):
        if not fold_of(c):
            return
        if dp == 4:
            pl.when((me == 1) | (me == 2))(lambda: body(2))
        else:
            pl.when(me == 1)(lambda: body(dp - 2))
            pl.when(me == dp - 2)(lambda: body(2))

    def end_when(c, body):
        if fold_of(c):
            pl.when(me == 0)(lambda: body(dp - 1))
            pl.when(me == dp - 1)(lambda: body(1))

    def taken(c, step, body):
        if fold_of(c) and step == dp - 1:
            pl.when(me != dp - 1)(body)
        elif fold_of(c) and step == 1:
            pl.when(me != 0)(body)
        else:
            body()

    def rs_y(c, p):
        return Copy(
            grads[c].at[my_rows(p, peer)], y_in[c].at[p], two.rsy, (c, p), {"ctx": peer}
        )

    def z_out(c, step):
        if c == 2:
            return mat_f.at[0, pl.ds(aligned(dp_at(step), dd), dd)]
        return y_in[c].at[dp_at(step)]

    def z_slot(c, step):
        return r.z_a.at[step - 1] if c == 2 else z_in[c].at[step - 1]

    def rs_z(c, step):
        return Copy(
            z_out(c, step), z_slot(c, step), two.rsz, (c, step - 1), {"dp": dp_at(step)}
        )

    def rs_fold(c, step):
        neighbour = 1 if step == dp - 1 else dp - 2
        return Copy(z_out(c, step), fold[c], two.rsn, c, {"dp": neighbour})

    def rs_f(c):
        area = fin[c].at[pl.ds(aligned(side, hd), hd)]
        return Copy(z_in[c].at[0], area, two.rsf, c, {"ctx": peer})

    def fin_copy(c):
        if c == 2:
            return pltpu.make_async_copy(r.z_a.at[1], fin[c], r.fin_sem.at[c])
        area = fin[c].at[pl.ds(aligned(side, hd), hd)]
        return pltpu.make_async_copy(z_in[c].at[0], area, r.fin_sem.at[c])

    def first_y():
        return Copy(r.z_a.at[0], r.y_a, two.firsty, 0, {"ctx": peer})

    steps = sorted(range(1, dp), key=lambda step: (step not in (1, dp - 1), step))

    def send_piece(c, step):
        send_when(
            c,
            step,
            lambda: rs_z(c, step).start(),
            lambda: rs_fold(c, step).start(),
            lambda: None,
        )

    def rs_start(c):
        if c == 2:
            end_when(c, lambda step: rs_fold(c, step).start())
            if not fold_of(c):
                first_rest()
            return
        for step in steps + [0]:
            rs_y(c, dp_at(step)).start()

    def first_rest():
        for step in steps:
            send_when(
                2, step, lambda: rs_z(2, step).start(), lambda: None, lambda: None
            )

    def rs_mid(c):
        for step in steps + [0]:
            p = dp_at(step)
            rs_y(c, p).wait_recv()
            mine = grads[c][my_rows(p, side), :].astype(F32)
            y_in[c][p] = (mine + y_in[c][p].astype(F32)).astype(BF16)
            if step:
                send_piece(c, step)

    def rs_join(c):
        def one(step):
            rs_fold(c, dp - 1).wait_recv()
            if c == 2:
                for start in range(0, dd, hd):
                    at = pl.ds(pl.multiple_of(dp_at(step) * dd + start, hd), hd)
                    both = mat_f[0, at, :].astype(F32) + fold[c][start : start + hd, :].astype(F32)
                    mat_f[0, at, :] = both.astype(BF16)
            else:
                both = y_in[c][dp_at(step)].astype(F32) + fold[c][...].astype(F32)
                y_in[c][dp_at(step)] = both.astype(BF16)
            rs_z(c, step).start()

        fold_when(c, one)

    def blank(c):
        def zero(step):
            slot = r.z_a if c == 2 else z_in[c]
            slot[step - 1] = jnp.zeros(slot.shape[1:], BF16)

        if fold_of(c):
            pl.when(me == 0)(lambda: zero(1))
            pl.when(me == dp - 1)(lambda: zero(dp - 1))

    def rs_fin(c):
        for step in range(1, dp):
            taken(c, step, lambda: rs_z(c, step).wait_recv())
        blank(c)
        if c == 2:
            for start in range(0, dd, hd):
                at = pl.ds(start, hd)
                mine = pl.ds(pl.multiple_of(me * dd + start, hd), hd)
                total = mat_f[0, mine, :].astype(F32)
                for step in range(1, dp):
                    total += r.z_a[step - 1, at, :].astype(F32)
                r.z_a[0, at, :] = total.astype(BF16)
            first_y().start()
            return
        total = y_in[c][me].astype(F32)
        for step in range(1, dp):
            total += z_in[c][step - 1].astype(F32)
        z_in[c][0] = total.astype(BF16)
        rs_f(c).start()
        fin_copy(c).start()

    def first_sum():
        first_y().wait_recv()
        for start in range(0, dd, hd):
            at = pl.ds(start, hd)
            total = r.z_a[0, at, :].astype(F32) + r.y_a[at, :].astype(F32)
            r.z_a[1, at, :] = total.astype(BF16)
        fin_copy(2).start()

    def rs_end(c):
        for step in range(1, dp):
            wait = lambda: rs_z(c, step).wait_send()
            send_when(c, step, wait, lambda: None, wait)
        end_when(c, lambda step: rs_fold(c, step).wait_send())
        if c == 2:
            first_y().wait_send()
        else:
            for p in range(dp):
                rs_y(c, p).wait_send()
            rs_f(c).wait_recv()
            rs_f(c).wait_send()
        fin_copy(c).wait()

    def acc_low(source, target, s):
        def one(i):
            at = pl.ds(pl.multiple_of(s * local + i * tb, tb), tb)
            target[at, :] = source[at, :].astype(BF16)

        each(local // tb, one)

    for t in range(nt):
        ffn_rows(t, 0)
        if t == 0:
            spread_end(0, 1)
            transpose_into(hn, hn_t, local, local // tb)
        if t == 1 and folds:
            first_rest()
        if t == nt - 1:
            sum1_start(1, 0)
        if t == 2:
            rs_join(2)
        ffn_rows(t, 1)
        if t == 0:
            for c in range(4, nt + 2):
                serve(c)
        if t == nt - 1:
            sum1_start(1, 1)
            sum2_start(1, 0)
        ffn_weights(t)
        rs_start(2 + t)
        if t + 1 < nt:
            ag_end(2 + t + 1)
        if t == 0:
            pass

    def middle_back(s):
        incoming = sum_end(1, s)
        value = mid[share_at(s), :]
        factor = lax.rsqrt(mean_square(value) + EPSILON)
        hat = value * factor
        small[1:2, :] += jnp.sum(incoming * hat, axis=0, keepdims=True)
        grad_hat = incoming * r.gain_w[1:2, :]
        back = factor * (grad_hat - hat * jnp.mean(grad_hat * hat, axis=-1, keepdims=True))
        total = dy[token_rows(s, chip, core), :].astype(F32) + back
        grad_hidden[share_at(s), :] = total
        spread1_start(1, s, total.astype(BF16))

    def again(first, count):
        def one(i):
            at = pl.ds(pl.multiple_of(first + i * tb, tb), tb)
            value = x[at, :].astype(F32)
            value = value * lax.rsqrt(mean_square(value) + EPSILON)
            value = (value * r.gain_w[0:1, :]).astype(BF16).astype(F32)
            hn_t[:, at] = value.T.astype(BF16)

        each(count, one)

    sum2_start(1, 1)
    again(0, rows // tb)
    if nt < 3:
        rs_join(2)
    middle_back(0)
    middle_back(1)
    for s in range(seqs):
        acc_low(acc_m, part, s)
        sum1_start(3, s)
    spread2_start(1, 0)

    spread2_start(1, 1)
    for s in range(seqs):
        sum2_start(3, s)

    g_kv, gq_t = r.g_kv, r.gq_t

    def out_back(s):
        def one(i):
            at = pl.ds(pl.multiple_of(s * local + i * rb, rb), rb)
            value = dot(hn[at, :], mat_o[...])
            for h in range(qh):
                piece = value[:, h * head : (h + 1) * head]
                start = nqkv + h * 2 * head
                units[at, start : start + 2 * head] = jnp.concatenate(
                    [jnp.zeros_like(piece), piece], axis=1
                ).astype(BF16)

        each(local // rb, one)

    def attend_back(s, with_peer):
        for h in range(kh):
            g_kv[s * kh + h] = jnp.zeros_like(g_kv[s * kh + h])

        def one(index):
            for j in range(local // qb):
                parts, head_kv, here = masked(s, j, index, with_peer)
                at = slice(j * qb, (j + 1) * qb)
                token = slice(s * local + j * qb, s * local + (j + 1) * qb)
                lanes = pl.ds(pl.multiple_of(nqkv + index * 2 * head, 128), 2 * head)
                go = units[token, lanes]
                logs = lse[s * qh + index, :, at]
                probs = [jnp.exp(p[0] - logs) for p in parts]
                grad_probs = [dot_nt(kv[head_kv, w, :size, :], go) for _, w, size in parts]
                row_dot = sum(
                    jnp.sum(p * g, axis=0, keepdims=True) for p, g in zip(probs, grad_probs)
                )
                out = jnp.zeros((2 * head, qb), F32)
                for (_, w, size), p, g in zip(parts, probs, grad_probs):
                    gs = (p * (g - row_dot)).astype(BF16)
                    out += dot(kv_t[head_kv, w, :, :size], gs)
                    g_kv[head_kv, w, :size, :] += dot(gs, here) + dot(p.astype(BF16), go)
                spot = pl.ds(pl.multiple_of(index * head, head), head)
                gq_t[s, spot, at] = out[:head, :] * scale

        each(qh, one)

    def back_copy(s):
        return Copy(
            r.g_kv_low.at[pl.ds(s * kh, kh)],
            r.g_kv_in.at[pl.ds(s * kh, kh)],
            two.gkv,
            s,
            {"ctx": peer},
        )

    def attend_back_any(s):
        @pl.when(side == 0)
        def _():
            attend_back(s, False)

        @pl.when(side != 0)
        def _():
            attend_back(s, True)
            for h in range(kh):
                r.g_kv_low[s * kh + h] = g_kv[s * kh + h, 1].astype(BF16)
            back_copy(s).start()

    def kv_back_arrive(s):
        @pl.when(side == 0)
        def _():
            back_copy(s).wait_recv()
            for h in range(kh):
                g_kv[s * kh + h, 0] += r.g_kv_in[s * kh + h].astype(F32)

        @pl.when(side != 0)
        def _():
            back_copy(s).wait_send()

    def project_back(s):
        def one(i):
            at = pl.ds(pl.multiple_of(s * local + i * rb, rb), rb)
            inner = pl.ds(aligned(i, rb), rb)
            gkv = [g_kv[s * kh + h, 0, inner, :] for h in range(kh)]
            if kh == 1:
                g_key, g_value = gkv[0][:, :head], gkv[0][:, head:]
            else:
                keys, values = [], []
                for h in range(0, kh, 2):
                    keys.append(jnp.where(low_half, gkv[h], pltpu.roll(gkv[h + 1], head, 1)))
                    values.append(jnp.where(low_half, pltpu.roll(gkv[h], head, 1), gkv[h + 1]))
                g_key = jnp.concatenate(keys, axis=1)
                g_value = jnp.concatenate(values, axis=1)
            value = jnp.concatenate([gq_t[s, :, inner].T, g_key], axis=1)
            cosine = widen(tab[at, : 2 * head], nqk)
            sine = widen(tab[at, 2 * head :], nqk)
            value = value * cosine - swap_halves(value, head) * sine
            plain = raw[at, :]
            factor = lax.rsqrt(spread_means(plain * plain, head) + EPSILON)
            hat = plain * factor
            small[2:3, :nqk] += jnp.sum(value * hat, axis=0, keepdims=True)
            grad_hat = value * r.gain_h[0:1, :]
            value = factor * (grad_hat - hat * spread_means(grad_hat * hat, head))
            low = jnp.concatenate([value, g_value], axis=1).astype(BF16)
            units[at, :nqkv] = low
            part[at, :] = dot_nt(low, mat_q[...]).astype(BF16)

        each(local // rb, one)

    def out_weights():
        for i in range(width // rb):
            total = sum(
                dot(o_t[s], hn[s * local : (s + 1) * local, i * rb : (i + 1) * rb])
                for s in range(seqs)
            )
            r.grad_o[i * rb : (i + 1) * rb, :] = total.T.astype(BF16)

    def qkv_weights():
        def one(i):
            at = pl.ds(aligned(i, rb), rb)
            r.grad_q[at, :] = dot(hn_t[at, :], units[:, :nqkv]).astype(BF16)

        each(width // rb, one)

    if nt > 1:
        rs_mid(3)
    spread_end(1, 0)
    out_back(0)
    attend_back_any(0)
    spread_end(1, 1)
    out_back(1)
    rs_fin(2)
    attend_back_any(1)
    out_weights()
    rs_start(1)
    if nt > 1:
        rs_join(3)

    def mlp_end(s):
        mlp = sum_end(3, s)
        weight = keep_of(s)[:, 0:1]
        small[4:5, 384:512] += fold_lanes(weight * mlp * mlp)
        small[4:5, 512:640] += jnp.sum(keep_of(s), axis=0, keepdims=True)
        mid[share_at(s), :] += mlp

    for s in range(seqs):
        mlp_end(s)
    if nt > 2:
        rs_mid(4)
    kv_back_arrive(0)
    project_back(0)
    sum1_start(2, 0)
    first_sum()
    kv_back_arrive(1)
    project_back(1)
    sum1_start(2, 1)
    sum2_start(2, 0)
    qkv_weights()
    rs_start(0)
    sum2_start(2, 1)
    if nt > 2:
        rs_join(4)
    if nt > 1:
        rs_fin(3)
    rs_mid(1)

    def first_back(s):
        incoming = sum_end(2, s)
        value = x[token_rows(s, chip, core), :].astype(F32)
        factor = lax.rsqrt(mean_square(value) + EPSILON)
        hat = value * factor
        small[0:1, :] += jnp.sum(incoming * hat, axis=0, keepdims=True)
        grad_hat = incoming * r.gain_w[0:1, :]
        back = factor * (grad_hat - hat * jnp.mean(grad_hat * hat, axis=-1, keepdims=True))
        grad_hidden[share_at(s), :] += back

    first_back(0)
    first_back(1)
    rs_mid(0)

    small_in = r.small_in

    def small_round(start, copies, order):
        for c in copies:
            c.start()
        for c in copies:
            c.wait_recv()
            c.wait_send()
        total = None
        for o in order:
            term = small_in[start + o]
            total = term if total is None else total + term
        small[...] = total

    small_in[pl.ds(core, 1)] = small[...][None]
    small_round(
        0, [Copy(small, small_in.at[core], two.small, 0, {"tp": other_core})], range(2)
    )
    small_in[pl.ds(2 + side, 1)] = small[...][None]
    small_round(2, [Copy(small, small_in.at[2 + side], two.small, 1, {"ctx": peer})], range(2))
    small_in[pl.ds(4 + chip, 1)] = small[...][None]
    small_round(
        4,
        [
            Copy(small, small_in.at[4 + chip], two.small, 1 + s, {"tp": chip_lane(s)})
            for s in range(1, chips)
        ],
        range(chips),
    )
    rs_fin(1)
    if nt > 2:
        rs_fin(4)
    small_in[pl.ds(4 + chips + me, 1)] = small[...][None]
    small_round(
        4 + chips,
        [
            Copy(small, small_in.at[4 + chips + me], two.small, chips + s, {"dp": dp_at(s)})
            for s in range(1, dp)
        ],
        range(dp),
    )
    def mine_of(value, size):
        return sum(
            jnp.where(me == d, value[:, d * size : (d + 1) * size], 0.0) for d in range(dp)
        )

    r.own_attn[...] = mine_of(small[0:1, :], dd)
    r.own_ffn[...] = mine_of(small[1:2, :], dd)
    row = small[2:3, :nqk]
    over_q = sum(row[:, h * head : (h + 1) * head] for h in range(qh))
    over_k = sum(row[:, h * head : (h + 1) * head] for h in range(qh, qh + kh))
    r.own_query[...] = mine_of(over_q, piece)
    r.own_key[...] = mine_of(over_k, piece)
    totals = [
        jnp.sum(small[4:5, i * 128 : (i + 1) * 128], axis=1, keepdims=True) for i in range(4)
    ]
    count = small[4:5, 512:513] * width
    r.own_stat[...] = jnp.sqrt(jnp.concatenate(totals, axis=1) / count)
    rs_fin(0)
    for c in list(range(2, nt + 2)) + [1, 0]:
        rs_end(c)


def per_device(
    sizes,
    hidden_states,
    out_grad,
    w_query,
    w_key,
    w_value,
    w_out,
    w_gate,
    w_up,
    w_down,
    attn_gain,
    ffn_gain,
    query_gain,
    key_gain,
    segment_ids,
    valid_mask,
    positions,
):
    seqs, local, width = hidden_states.shape
    dp, ctx, tp = sizes
    rows = seqs * local
    head = query_gain.shape[0] * dp
    nq, nk, units = w_query.shape[1], w_key.shape[1], w_gate.shape[1]
    nqkv = nq + 2 * nk
    nt = 3 if units % 3 == 0 else 1
    ft = units // nt
    dd = width // dp
    hd = dd // ctx
    share = local // tp
    chips = tp // 2
    qh, kh = nq // head, nk // head
    plain = ft % 128 == 0 and dd % 128 == 0 and nk % 128 == 0
    cfg = types.SimpleNamespace(
        seqs=seqs, local=local, width=width, head=head, dp=dp, ctx=ctx, tp=tp,
        qh=qh, kh=kh, nt=nt, ft=ft, plain=plain,
    )
    gains = jnp.concatenate([attn_gain, ffn_gain, query_gain, key_gain])
    gains = gains.astype(F32).reshape(1, -1)
    half = head // 2
    freq = np.float32(ROPE_BASE) ** (-(np.arange(half, dtype=np.float32) * 2.0) / head)
    freq = jnp.asarray(np.tile(freq.astype(np.float32), 128 // half)[None])
    inputs = dict(
        x=(hidden_states.reshape(rows, width), True),
        dy=(out_grad.reshape(rows, width), True),
        gains=(gains, True),
        segment_ids=(segment_ids, True),
        valid_mask=(valid_mask, True),
        positions=(positions, True),
        freq=(freq, True),
    )
    if plain:
        inputs.update(
            w_query=(w_query, False),
            w_key=(w_key, False),
            w_value=(w_value, False),
            w_out=(w_out, False),
            w_gate=(w_gate, False),
            w_up=(w_up, False),
            w_down=(w_down, False),
        )
    else:
        tiles = []
        for i in range(nt):
            cut = slice(i * ft, (i + 1) * ft)
            tiles.append(jnp.concatenate([w_gate[:, cut], w_up[:, cut], w_down[cut].T], axis=1))
        inputs.update(
            w_qkv=(jnp.concatenate([w_query, w_key, w_value], axis=1), False),
            w_o=(w_out.T, False),
            w_f=(jnp.stack(tiles), False),
        )
    outputs = dict(
        result=((seqs * share, width), F32),
        grad_hidden=((seqs * share, width), F32),
        fin_q=((dd, nqkv), BF16),
        fin_o=((dd, nq), BF16),
        fin_f=((nt, dd, 3 * ft), BF16),
        own_attn=((1, dd), F32),
        own_ffn=((1, dd), F32),
        own_query=((1, head // dp), F32),
        own_key=((1, head // dp), F32),
        own_stat=((1, 4), F32),
    )
    scratch = dict(
        mat_q=((width, nqkv), BF16),
        mat_o=((width, nq), BF16),
        mat_f=((nt, width, 3 * ft), BF16),
        gain_buf=((dp, 1, 2 * dd + 2 * head // dp), F32),
        facts=((seqs, 2, local), F32),
        gain_w=((8, width), F32),
        gain_h=((8, nq + nk), F32),
        code_peer=((seqs, 2, local), F32),
        tab=((rows, 256), F32),
        key_code=((ctx, seqs, local, 128), F32),
        hn=((rows, width), BF16),
        hn_t=((width, rows), BF16),
        dr_t=((width, rows), BF16),
        raw=((rows, nq + nk), F32),
        q_pad=((seqs * qh, local, 2 * head), BF16),
        kv=((seqs * kh, ctx, local, 2 * head), BF16),
        kv_t=((seqs * kh, ctx, 2 * head, local), BF16),
        g_kv=((seqs * kh, ctx, local, 2 * head), F32),
        g_kv_low=((seqs * kh, local, 2 * head), BF16),
        g_kv_in=((seqs * kh, local, 2 * head), BF16),
        o_t=((seqs, nq, local), BF16),
        gq_t=((seqs, nq, local), F32),
        lse=((seqs * qh, 1, local), F32),
        part=((rows, width), BF16),
        near=((2, seqs, chips, share, width), BF16),
        pair=((seqs, chips, share, width), BF16),
        far=((2, seqs, max(chips - 1, 1), share, width), BF16),
        small=((8, width), F32),
        small_in=((4 + chips + dp, 8, width), F32),
        units=((rows, 3 * ft), BF16),
        acc_m=((rows, width), F32),
        acc_h=((rows, width), F32),
        grad_q=((width, nqkv), BF16),
        grad_o=((width, nq), BF16),
        y_q=((dp, hd, nqkv), BF16),
        y_o=((dp, hd, nq), BF16),
        y_f=((nt - 1, dp, hd, 3 * ft), BF16),
        z_q=((dp - 1, hd, nqkv), BF16),
        z_o=((dp - 1, hd, nq), BF16),
        z_f=((nt - 1, dp - 1, hd, 3 * ft), BF16),
    )
    scratch.update(
        y_a=((dd, 3 * ft), BF16),
        z_a=((dp - 1, dd, 3 * ft), BF16),
        fold_a=((dd, 3 * ft), BF16),
        fold_f=((nt - 1, hd, 3 * ft), BF16),
    )
    pairs = dict(
        agz=(nt + 2, dp - 1),
        agy=(nt + 2, dp - 1),
        gain=(dp - 1,),
        code=(1,),
        kv=(seqs,),
        gkv=(seqs,),
        sum1=(4, seqs * chips),
        sum2=(4, seqs * max(chips - 1, 1)),
        spread1=(2, seqs * max(chips - 1, 1)),
        spread2=(2, seqs * chips),
        rsy=(nt + 2, dp),
        rsz=(nt + 2, dp - 1),
        rsf=(nt + 2,),
        small=(chips + dp,),
        rsn=(nt + 2,),
        firsty=(1,),
    )
    singles = dict(own_sem=(nt + 2, 3), agfar=(nt + 2,), fin_sem=(nt + 2,))
    shapes = list(singles.values()) + [v for v in pairs.values() for _ in range(2)]

    def kernel(*refs):
        refs = list(refs)
        r = types.SimpleNamespace()
        for name in list(inputs) + list(outputs) + list(scratch) + list(singles):
            setattr(r, name, refs.pop(0))
        two = types.SimpleNamespace()
        for name in pairs:
            setattr(two, name, (refs.pop(0), refs.pop(0)))
        block_kernel(cfg, r, two)

    vmem = pl.BlockSpec(memory_space=pltpu.VMEM)
    away = pl.BlockSpec(memory_space=pl.ANY)
    out = pl.pallas_call(
        kernel,
        out_shape=[jax.ShapeDtypeStruct(*v) for v in outputs.values()],
        in_specs=[vmem if v else away for _, v in inputs.values()],
        out_specs=[away if n.startswith("fin") else vmem for n in outputs],
        scratch_shapes=[pltpu.VMEM(*v) for v in scratch.values()]
        + [pltpu.SemaphoreType.DMA(v) for v in shapes],
        compiler_params=pltpu.CompilerParams(
            collective_id=0, has_side_effects=True, vmem_limit_bytes=VMEM_LIMIT
        ),
    )(*[v for v, _ in inputs.values()])
    result, grad_hidden, fin_q, fin_o, fin_f = out[:5]

    gates = [fin_f[i, :, :ft] for i in range(nt)]
    ups = [fin_f[i, :, ft : 2 * ft] for i in range(nt)]
    downs = [fin_f[i, :, 2 * ft :] for i in range(nt)]
    return (
        result.reshape(seqs, share, width),
        grad_hidden.reshape(seqs, share, width),
        fin_q[:, :nq].astype(F32),
        fin_q[:, nq : nq + nk].astype(F32),
        fin_q[:, nq + nk :].astype(F32),
        fin_o.T.astype(F32),
        jnp.concatenate(gates, axis=1).astype(F32),
        jnp.concatenate(ups, axis=1).astype(F32),
        jnp.concatenate([d.T for d in downs], axis=0).astype(F32),
        *[value.reshape(-1) for value in out[5:]],
    )


VMEM_LIMIT = 63 * 2**20


def solution(mesh):
    sizes = tuple(mesh.shape[a] for a in ("dp", "ctx", "tp"))
    return jax.shard_map(
        functools.partial(per_device, sizes),
        mesh=mesh,
        in_specs=(
            P("dp", "ctx", None),
            P("dp", "ctx", None),
            P("dp", "tp"),
            P("dp", "tp"),
            P("dp", "tp"),
            P("tp", "dp"),
            P("dp", "tp"),
            P("dp", "tp"),
            P("tp", "dp"),
            P("dp"),
            P("dp"),
            P("dp"),
            P("dp"),
            P("dp", "ctx"),
            P("dp", "ctx"),
            P("dp", "ctx"),
        ),
        out_specs=(
            P("dp", ("ctx", "tp"), None),
            P("dp", ("ctx", "tp"), None),
            P("dp", "tp"),
            P("dp", "tp"),
            P("dp", "tp"),
            P("tp", "dp"),
            P("dp", "tp"),
            P("dp", "tp"),
            P("tp", "dp"),
            P("dp"),
            P("dp"),
            P("dp"),
            P("dp"),
            P(),
        ),
        check_vma=False,
    )
```

```python
import functools
import types

import jax
import jax.numpy as jnp
import numpy as np
from jax import lax
from jax.experimental import pallas as pl
from jax.experimental.pallas import tpu as pltpu
from jax.sharding import PartitionSpec as P

EPSILON = 1e-05
ROPE_BASE = 1000000.0
F32 = jnp.float32
BF16 = jnp.bfloat16
MESH = pl.DeviceIdType.MESH
NEGATIVE = -1e30
PADDING = 50000.0


def dot(left, right):
    return jnp.dot(left, right, preferred_element_type=F32)


def dot_nt(left, right):
    return lax.dot_general(left, right, (((1,), (1,)), ((), ())), preferred_element_type=F32)


def each(count, body):
    def step(i, carry):
        body(i)
        return carry

    lax.fori_loop(0, count, step, 0)


def aligned(index, unit):
    return pl.multiple_of(index * unit, unit)


def mean_square(value):
    return jnp.mean(value * value, axis=-1, keepdims=True)


def swap_halves(value, head):
    half = head // 2
    size = value.shape[1]
    if size % 128 == 0:
        at = lax.broadcasted_iota(jnp.int32, (1, size), 1)
        first = lax.rem(at, head) < half
        return jnp.where(first, pltpu.roll(value, size - half, 1), pltpu.roll(value, half, 1))
    pieces = []
    for start in range(0, size, head):
        pieces += [value[:, start + half : start + head], value[:, start : start + half]]
    return jnp.concatenate(pieces, axis=1)


def spread_means(value, head):
    size = value.shape[1]
    row = lax.div(lax.broadcasted_iota(jnp.int32, (size, size), 0), head)
    column = lax.div(lax.broadcasted_iota(jnp.int32, (size, size), 1), head)
    block = jnp.where(row == column, 1.0 / head, 0.0).astype(BF16)
    high = value.astype(BF16)
    rest = (value - high.astype(F32)).astype(BF16)
    return dot(high, block) + dot(rest, block)


def widen(value, count):
    size = value.shape[1]
    if count <= size:
        return value[:, :count]
    return jnp.concatenate([value] * -(-count // size), axis=1)[:, :count]


def fold_lanes(value):
    total = jnp.sum(value, axis=0, keepdims=True)
    out = total[:, :128]
    for i in range(1, value.shape[1] // 128):
        out += total[:, i * 128 : (i + 1) * 128]
    return out


class Copy:
    def __init__(self, src, dst, sems, index, device, send=None):
        send = sems[0].at[index] if send is None else send
        self.copy = pltpu.make_async_remote_copy(
            src_ref=src,
            dst_ref=dst,
            send_sem=send,
            recv_sem=sems[1].at[index],
            device_id=device,
            device_id_type=MESH,
        )

    def start(self):
        self.copy.start()

    def wait_send(self):
        self.copy.wait_send()

    def wait_recv(self):
        self.copy.wait_recv()


def block_kernel(cfg, r, two):
    seqs, local, width, head = cfg.seqs, cfg.local, cfg.width, cfg.head
    dp, ctx, tp = cfg.dp, cfg.ctx, cfg.tp
    qh, kh, nt, ft = cfg.qh, cfg.kh, cfg.nt, cfg.ft
    nq, nk = qh * head, kh * head
    nqkv = nq + 2 * nk
    group = qh // kh
    chips = tp // 2
    rows = seqs * local
    share = local // tp
    dd = width // dp
    hd = dd // ctx
    me, side, lane = lax.axis_index("dp"), lax.axis_index("ctx"), lax.axis_index("tp")
    core, chip = lax.rem(lane, 2), lax.div(lane, 2)
    other_core = lane + 1 - 2 * core
    peer = 1 - side
    rb = min(256, local)
    qb = min(256, local)
    tb = min(128, local)
    scale = head**-0.5

    def dp_at(step):
        return lax.rem(me + step, dp)

    def chip_lane(step):
        return lax.rem(chip + step, chips) * 2 + core

    barrier = pltpu.get_barrier_semaphore()
    greet = [{"dp": dp_at(s)} for s in range(1, dp)] + [{"ctx": peer}, {"tp": other_core}]
    greet += [{"tp": chip_lane(s)} for s in range(1, chips)]
    for device in greet:
        pl.semaphore_signal(barrier, inc=1, device_id=device, device_id_type=MESH)
    pl.semaphore_wait(barrier, len(greet))

    whole = [r.mat_q, r.mat_o] + [r.mat_f.at[t] for t in range(nt)]

    def my_rows(owner, which):
        return pl.ds(pl.multiple_of(owner * dd + which * hd, hd), hd)

    solo = ()

    def ag_rows(c, owner):
        if c in solo:
            return pl.ds(aligned(owner, dd), dd)
        return my_rows(owner, side)

    def ag_z(c, step):
        return Copy(
            whole[c].at[ag_rows(c, me)],
            whole[c].at[ag_rows(c, me)],
            two.agz,
            (c, step - 1),
            {"dp": dp_at(step)},
        )

    def ag_y(c, step):
        owner = lax.rem(me - step + dp, dp)
        area = whole[c].at[my_rows(owner, side)]
        return Copy(area, area, two.agy, (c, step - 1), {"ctx": peer})

    relayed = (0,) + tuple(range(2, nt + 2)) if dp > 2 else ()
    hops = [dp - 2, 2] if dp > 2 else []
    order = sorted(range(1, dp), key=lambda step: (step not in hops, step))

    def ag_far(c, step):
        owner, target = (0, dp - 1) if step == dp - 2 else (dp - 1, 0)
        if dp == 4:
            owner = jnp.where(me == 1, dp - 1, 0)
            target = jnp.where(me == 1, 0, dp - 1)
        area = whole[c].at[ag_rows(c, owner)]
        index = lax.rem(target - owner + dp, dp) - 1
        send = r.agfar.at[c]
        return Copy(area, area, two.agz, (c, index), {"dp": target}, send)

    def far_when(c, step, body):
        if c not in relayed:
            return
        if dp == 4:
            if step == 2:
                pl.when((me == 1) | (me == 2))(body)
        elif step == dp - 2:
            pl.when(me == dp - 2)(body)
        elif step == 2:
            pl.when(me == 1)(body)

    def near_when(c, step, body):
        if c in relayed and step == dp - 1:
            pl.when(me != 0)(body)
        elif c in relayed and step == 1:
            pl.when(me != dp - 1)(body)
        else:
            body()

    own_rows = pl.ds(aligned(me, dd), dd)

    def stage(c):
        if c == 1:
            return r.units.at[pl.ds(ft, nq), pl.ds(0, dd)]
        return r.units.at[pl.ds(0, ft), pl.ds((c - 2) * dd, dd)]

    def own_moves(c):
        if not cfg.plain:
            source = [r.w_qkv, r.w_o] + [r.w_f.at[t] for t in range(nt)]
            pairs_of = [(source[c], whole[c].at[own_rows])]
        elif c == 0:
            pairs_of, start = [], 0
            for source in (r.w_query, r.w_key, r.w_value):
                size = source.shape[1]
                pairs_of.append((source, r.mat_q.at[own_rows, pl.ds(start, size)]))
                start += size
        elif c == 1:
            pairs_of = [(r.w_out, stage(1))]
        else:
            t = c - 2
            at = pl.ds(t * ft, ft)
            pairs_of = [
                (r.w_gate.at[:, at], r.mat_f.at[t, own_rows, pl.ds(0, ft)]),
                (r.w_up.at[:, at], r.mat_f.at[t, own_rows, pl.ds(ft, ft)]),
                (r.w_down.at[at], stage(c)),
            ]
        return [
            pltpu.make_async_copy(source, target, r.own_sem.at[c, i])
            for i, (source, target) in enumerate(pairs_of)
        ]

    def own_start(c):
        for move in own_moves(c):
            move.start()

    def own_end(c):
        for move in own_moves(c):
            move.wait()
        if cfg.plain and c >= 1:
            block = stage(c)[...].astype(F32).T.astype(BF16)
            if c == 1:
                r.mat_o[own_rows, :] = block
            else:
                r.mat_f[c - 2, own_rows, 2 * ft :] = block

    def ag_start(c, early=True, late=True):
        if c >= nt + 2:
            return
        for step in order:
            if not (early if step in hops else late):
                continue
            near_when(c, step, lambda: ag_z(c, step).start())

    def ag_pass_one(c, step):
        ag_z(c, step).wait_recv()
        far_when(c, step, lambda: ag_far(c, step).start())
        if c not in solo:
            ag_y(c, step).start()

    served = set()

    def serve(c, early=True, late=True):
        for step in order:
            if c < nt + 2 and (c, step) not in served and (early if step in hops else late):
                served.add((c, step))
                ag_pass_one(c, step)

    def ag_end(c):
        serve(c)
        for step in order:
            if c not in solo:
                ag_y(c, step).wait_recv()
                ag_y(c, step).wait_send()
            near_when(c, step, lambda: ag_z(c, step).wait_send())
            far_when(c, step, lambda: ag_far(c, step).wait_send())

    gain_buf = r.gain_buf

    def gain_copy(step):
        return Copy(
            r.gains, gain_buf.at[me], two.gain, step - 1, {"dp": dp_at(step)}
        )

    for s in range(seqs):
        token = lax.broadcasted_iota(jnp.int32, (1, local), 1) + side * local + 100000
        real = r.valid_mask[s : s + 1, :] == 1
        code = jnp.where(real, r.segment_ids[s : s + 1, :], token)
        r.facts[s, 0:1, :] = code.astype(F32)
        r.facts[s, 1:2, :] = r.positions[s : s + 1, :].astype(F32)

    def code_copy():
        return Copy(r.facts, r.code_peer, two.code, 0, {"ctx": peer})

    for c in range(nt + 2):
        own_start(c)
    for step in range(1, dp):
        gain_copy(step).start()
    own_end(0)
    ag_start(0)
    code_copy().start()
    for c in range(1, nt + 2):
        own_end(c)

    x, dy, hn, hn_t, dr_t = r.x, r.dy, r.hn, r.hn_t, r.dr_t

    def transpose_into(source, target, first, count):
        def one(i):
            at = pl.ds(pl.multiple_of(first + i * tb, tb), tb)
            target[:, at] = source[at, :].astype(F32).T.astype(BF16)

        each(count, one)

    def code_columns(source, which):
        for s in range(seqs):
            row = jnp.broadcast_to(source[s, 0:1, :], (128, local))
            r.key_code[which, s] = row.T

    code_columns(r.facts, 0)

    sign = lax.rem(lax.broadcasted_iota(jnp.int32, (1, 128), 1), head) < head // 2
    sign = jnp.where(sign, -1.0, 1.0).astype(F32)
    for s in range(seqs):
        for start in range(0, local, tb):
            place = jnp.broadcast_to(r.facts[s, 1:2, start : start + tb], (128, tb)).T
            angle = place * r.freq[...]
            at = pl.ds(s * local + start, tb)
            r.tab[at, :128] = jnp.cos(angle)
            r.tab[at, 128:] = jnp.sin(angle) * sign

    gain_buf[pl.ds(me, 1)] = r.gains[...][None]
    for step in range(1, dp):
        gain_copy(step).wait_recv()
        gain_copy(step).wait_send()
    piece = head // dp
    for d in range(dp):
        r.gain_w[0:1, d * dd : (d + 1) * dd] = gain_buf[d, :, :dd]
        r.gain_w[1:2, d * dd : (d + 1) * dd] = gain_buf[d, :, dd : 2 * dd]
        for h in range(qh):
            start = h * head + d * piece
            r.gain_h[0:1, start : start + piece] = gain_buf[d, :, 2 * dd : 2 * dd + piece]
        for h in range(kh):
            start = nq + h * head + d * piece
            r.gain_h[0:1, start : start + piece] = gain_buf[d, :, 2 * dd + piece : 2 * dd + 2 * piece]

    def normed_into(target, first, count):
        def one(i):
            at = pl.ds(pl.multiple_of(first + i * tb, tb), tb)
            value = x[at, :].astype(F32)
            value = value * lax.rsqrt(mean_square(value) + EPSILON)
            target[at, :] = (value * r.gain_w[0:1, :]).astype(BF16)

        each(count, one)

    normed_into(hn, 0, rows // tb // 2)
    serve(0, late=False)
    normed_into(hn, rows // 2, rows // tb // 2)
    code_copy().wait_recv()
    code_copy().wait_send()
    code_columns(r.code_peer, 1)
    ag_start(2, late=False)
    serve(0)
    ag_start(1)
    transpose_into(dy, dr_t, 0, rows // tb)
    ag_start(2, early=False)
    ag_end(0)

    mat_q, mat_o, raw, tab = r.mat_q, r.mat_o, r.raw, r.tab
    q_pad, kv, kv_t = r.q_pad, r.kv, r.kv_t

    nqk = nq + nk
    low_half = lax.broadcasted_iota(jnp.int32, (1, 2 * head), 1) < head

    def pairs(value, start, count):
        out = []
        for h in range(0, count, 2):
            if count == 1:
                here = value[:, start : start + head]
                both = jnp.concatenate([here, here], axis=1)
                out.append((both, both))
                continue
            here = value[:, start + h * head : start + (h + 2) * head]
            turned = pltpu.roll(here, head, 1)
            out += [(here, turned), (turned, here)]
        return out

    def project(s):
        def one(i):
            at = pl.ds(pl.multiple_of(s * local + i * rb, rb), rb)
            inner = pl.ds(aligned(i, rb), rb)
            both = dot(hn[at, :], mat_q[...])
            plain = both[:, :nqk]
            raw[at, :] = plain
            cosine = widen(tab[at, : 2 * head], nqk)
            sine = widen(tab[at, 2 * head :], nqk)
            value = plain * lax.rsqrt(spread_means(plain * plain, head) + EPSILON)
            value = value * r.gain_h[0:1, :]
            value = value * cosine + swap_halves(value, head) * sine
            for h, (low, _) in enumerate(pairs(value, 0, qh)):
                q_pad[s * qh + h, inner, :] = jnp.where(low_half, low * scale, 0.0).astype(BF16)
            keys = pairs(value, nq, kh)
            values = pairs(both, nqk, kh)
            for h in range(kh):
                kv[s * kh + h, 0, inner, :] = jnp.where(
                    low_half, keys[h][0], values[h][1]
                ).astype(BF16)

        each(local // rb, one)

    def kv_copy(s):
        return Copy(
            kv.at[pl.ds(s * kh, kh), 0],
            kv.at[pl.ds(s * kh, kh), 1],
            two.kv,
            s,
            {"ctx": peer},
        )

    def kv_transpose(s, which):
        for h in range(kh):
            kv_t[s * kh + h, which] = kv[s * kh + h, which].astype(F32).T.astype(BF16)

    for s in range(seqs):
        project(s)

        @pl.when(side == 0)
        def _():
            kv_copy(s).start()

        kv_transpose(s, 0)
        if s == 0:
            serve(2, late=False)
            serve(1)
            ag_start(3, late=False)

    o_t, lse = r.o_t, r.lse

    def masked(s, j, index, with_peer):
        last = (j + 1) * qb
        head_kv = s * kh + index // group
        here = q_pad[s * qh + index, j * qb : last, :]
        query = r.facts[s, 0:1, j * qb : last]

        def spread(code):
            return jnp.concatenate([code] * (qb // 128), axis=1)

        own = dot_nt(kv[head_kv, 0, :last, :], here)
        key_at = lax.broadcasted_iota(jnp.int32, (last, qb), 0)
        query_at = lax.broadcasted_iota(jnp.int32, (last, qb), 1) + j * qb
        allowed = (spread(r.key_code[0, s, :last, :]) == query) & (key_at <= query_at)
        own = jnp.where(allowed, own, NEGATIVE)
        parts = [(own, 0, last)]
        if with_peer:
            far = dot_nt(kv[head_kv, 1], here)
            far = jnp.where(spread(r.key_code[1, s]) == query, far, NEGATIVE)
            parts.append((far, 1, local))
        return parts, head_kv, here

    def attend_one(s, index, with_peer):
        for j in range(local // qb):
            parts, head_kv, _ = masked(s, j, index, with_peer)
            highest = functools.reduce(
                jnp.maximum, [jnp.max(p[0], axis=0, keepdims=True) for p in parts]
            )
            expo = [jnp.exp(p[0] - highest) for p in parts]
            total = sum(jnp.sum(e, axis=0, keepdims=True) for e in expo)
            factor = 1.0 / total
            out = jnp.zeros((2 * head, qb), F32)
            for (_, which, size), e in zip(parts, expo):
                out += dot(kv_t[head_kv, which, :, :size], (e * factor).astype(BF16))
            at = pl.ds(pl.multiple_of(index * head, head), head)
            o_t[s, at, j * qb : (j + 1) * qb] = out[head:, :].astype(BF16)
            lse[s * qh + index, :, j * qb : (j + 1) * qb] = highest + jnp.log(total)

    def attend(s, first, count):
        def one(i):
            @pl.when(side == 0)
            def _():
                attend_one(s, first + i, False)

            @pl.when(side != 0)
            def _():
                attend_one(s, first + i, True)

        each(count, one)

    def kv_arrive(s):
        @pl.when(side == 0)
        def _():
            kv_copy(s).wait_send()

        @pl.when(side != 0)
        def _():
            kv_copy(s).wait_recv()
            kv_transpose(s, 1)

    part, near, pair, far = r.part, r.near, r.pair, r.far

    def pool(use):
        return 1 if use == 3 else 0

    def token_rows(s, which_chip, which_core):
        start = s * local + (which_chip * 2 + which_core) * share
        return pl.ds(pl.multiple_of(start, share), share)

    def sum1(use, s, c):
        return Copy(
            part.at[token_rows(s, c, 1 - core)],
            near.at[pool(use), s, c],
            two.sum1,
            (use, s * chips + c),
            {"tp": other_core},
        )

    def sum1_start(use, s):
        for c in range(chips):
            sum1(use, s, c).start()

    def sum2(use, s, step):
        return Copy(
            pair.at[s, lax.rem(chip + step, chips)],
            far.at[pool(use), s, step - 1],
            two.sum2,
            (use, s * max(chips - 1, 1) + step - 1),
            {"tp": chip_lane(step)},
        )

    def sum2_start(use, s):
        for c in range(chips):
            sum1(use, s, c).wait_recv()
        for c in range(chips):
            mine = part[token_rows(s, c, core), :].astype(F32)
            pair[s, c] = (mine + near[pool(use), s, c].astype(F32)).astype(BF16)
        for step in range(1, chips):
            sum2(use, s, step).start()

    def sum_end(use, s):
        for step in range(1, chips):
            sum2(use, s, step).wait_recv()
        total = part[token_rows(s, chip, core), :].astype(F32)
        total += near[pool(use), s, chip].astype(F32)
        for step in range(1, chips):
            total += far[pool(use), s, step - 1].astype(F32)
        for c in range(chips):
            sum1(use, s, c).wait_send()
        for step in range(1, chips):
            sum2(use, s, step).wait_send()
        return total

    def spread1(use, s, step):
        area = hn.at[token_rows(s, chip, core)]
        index = (use, s * max(chips - 1, 1) + step - 1)
        return Copy(area, area, two.spread1, index, {"tp": chip_lane(step)})

    def spread1_start(use, s, value):
        hn[token_rows(s, chip, core), :] = value
        for step in range(1, chips):
            spread1(use, s, step).start()

    def spread2(use, s, c):
        area = hn.at[token_rows(s, c, core)]
        return Copy(area, area, two.spread2, (use, s * chips + c), {"tp": other_core})

    def spread2_start(use, s):
        for step in range(1, chips):
            spread1(use, s, step).wait_recv()
        for c in range(chips):
            spread2(use, s, c).start()

    def spread_end(use, s):
        for c in range(chips):
            spread2(use, s, c).wait_recv()
            spread2(use, s, c).wait_send()
        for step in range(1, chips):
            spread1(use, s, step).wait_send()

    def out_project(s):
        def one(i):
            at = pl.ds(pl.multiple_of(s * local + i * rb, rb), rb)
            inner = pl.ds(aligned(i, rb), rb)
            o_rows = o_t[s, :, inner].astype(F32).T.astype(BF16)
            part[at, :] = dot_nt(o_rows, mat_o[...]).astype(BF16)

        each(local // rb, one)

    small, grad_hidden = r.small, r.grad_hidden
    mid = r.result
    small[...] = jnp.zeros_like(small)

    def share_at(s):
        return pl.ds(s * share, share)

    def keep_of(s):
        code = r.key_code[0, s, pl.ds(aligned(lane, share), share), :]
        return jnp.where(code < PADDING, 1.0, 0.0).astype(F32)

    def middle(s):
        attn = sum_end(0, s)
        value = x[token_rows(s, chip, core), :].astype(F32)
        weight = keep_of(s)[:, 0:1]
        small[4:5, 0:128] += fold_lanes(weight * value * value)
        small[4:5, 128:256] += fold_lanes(weight * attn * attn)
        value = value + attn
        mid[share_at(s), :] = value
        small[4:5, 256:384] += fold_lanes(weight * value * value)
        value = value * lax.rsqrt(mean_square(value) + EPSILON)
        spread1_start(0, s, (value * r.gain_w[1:2, :]).astype(BF16))

    half = qh // 2
    ag_start(3, early=False)
    kv_arrive(0)
    attend(0, 0, qh)
    serve(2)
    ag_end(1)
    out_project(0)
    sum1_start(0, 0)
    kv_arrive(1)
    attend(1, 0, half)
    sum2_start(0, 0)
    serve(3, late=False)
    ag_start(4, late=False)
    ag_start(4, early=False)
    attend(1, half, qh - half)
    out_project(1)
    sum1_start(0, 1)
    middle(0)
    sum2_start(0, 1)
    serve(3)
    spread2_start(0, 0)
    middle(1)
    serve(4, late=False)
    spread_end(0, 0)
    transpose_into(hn, hn_t, 0, local // tb)
    spread2_start(0, 1)
    ag_end(2)

    mat_f, units, acc_m, acc_h = r.mat_f, r.units, r.acc_m, r.acc_h

    def ffn_rows(t, s):
        def one(i):
            at = pl.ds(pl.multiple_of(s * local + i * rb, rb), rb)
            both = dot(hn[at, :], mat_f[t, :, : 2 * ft])
            gate, upward = both[:, :ft], both[:, ft:]
            sigmoid = 1.0 / (1.0 + jnp.exp(-gate))
            grad_inner = dot(dy[at, :], mat_f[t, :, 2 * ft :])
            silu = gate * sigmoid
            grad_up = (grad_inner * silu).astype(BF16)
            grad_gate = (
                grad_inner * upward * sigmoid * (1.0 + gate * (1.0 - sigmoid))
            ).astype(BF16)
            inner = (silu * upward).astype(BF16)
            grads = jnp.concatenate([grad_gate, grad_up], axis=1)
            units[at, : 2 * ft] = grads
            units[at, 2 * ft :] = inner
            back = dot_nt(grads, mat_f[t, :, : 2 * ft])
            ahead = dot_nt(inner, mat_f[t, :, 2 * ft :])
            if t > 0:
                back += acc_h[at, :]
                ahead += acc_m[at, :]
            if t < nt - 1:
                acc_h[at, :] = back
            else:
                part[at, :] = back.astype(BF16)
            acc_m[at, :] = ahead

        each(local // rb, one)

    def ffn_weights(t):
        def one(i):
            at = pl.ds(aligned(i, rb), rb)
            mat_f[t, at, : 2 * ft] = dot(hn_t[at, :], units[:, : 2 * ft]).astype(BF16)
            mat_f[t, at, 2 * ft :] = dot(dr_t[at, :], units[:, 2 * ft :]).astype(BF16)

        each(width // rb, one)

    folds = dp > 2
    parts = {}

    def add_part(c, grad, fin, first, size, direct, fold):
        half_size = size if direct else size // ctx
        parts[c] = types.SimpleNamespace(
            grad=grad, fin=fin, first=first, size=size, half=half_size, direct=direct,
            fold=fold, y_in=getattr(r, f"y{c}"), z_in=getattr(r, f"z{c}"),
        )

    add_part(0, r.grad_q, r.fin_q, 0, dd, False, None)
    add_part(1, r.grad_o, r.fin_o, 0, dd, False, None)
    for t in range(nt):
        cut = cfg.cuts[t]
        if cut < dd:
            c = 2 + t
            add_part(c, mat_f.at[t], r.fin_f.at[t], cut, dd - cut, False, getattr(r, f"fold{c}"))
        if cut:
            c = 2 + nt + t
            add_part(c, mat_f.at[t], r.fin_f.at[t], 0, cut, True, getattr(r, f"fold{c}"))

    def fold_of(c):
        return folds and parts[c].fold is not None

    def window(c, owner, which=0):
        part_c = parts[c]
        start = owner * dd + part_c.first + which * part_c.half
        return pl.ds(pl.multiple_of(start, 16), part_c.half)

    def fin_rows(c, which=0):
        part_c = parts[c]
        return pl.ds(pl.multiple_of(part_c.first + which * part_c.half, 16), part_c.half)

    def send_when(c, step, direct, other, defer):
        if not fold_of(c):
            direct()
            return
        away = []
        if step == dp - 1:
            pl.when(me == 0)(other)
            away.append(me == 0)
        if step == 1:
            pl.when(me == dp - 1)(other)
            away.append(me == dp - 1)
        if step == dp - 2:
            pl.when(me == 1)(defer)
            away.append(me == 1)
        if step == 2:
            pl.when(me == dp - 2)(defer)
            away.append(me == dp - 2)
        if not away:
            direct()
            return
        away = functools.reduce(jnp.logical_or, away)
        pl.when(jnp.logical_not(away))(direct)

    def fold_when(c, body):
        if not fold_of(c):
            return
        if dp == 4:
            pl.when((me == 1) | (me == 2))(lambda: body(2))
        else:
            pl.when(me == 1)(lambda: body(dp - 2))
            pl.when(me == dp - 2)(lambda: body(2))

    def end_when(c, body):
        if fold_of(c):
            pl.when(me == 0)(lambda: body(dp - 1))
            pl.when(me == dp - 1)(lambda: body(1))

    def taken(c, step, body):
        if fold_of(c) and step == dp - 1:
            pl.when(me != dp - 1)(body)
        elif fold_of(c) and step == 1:
            pl.when(me != 0)(body)
        else:
            body()

    def rs_y(c, p):
        part_c = parts[c]
        area = part_c.grad.at[window(c, p, peer)]
        return Copy(area, part_c.y_in.at[p], two.rsy, (c, p), {"ctx": peer})

    def z_out(c, step):
        if parts[c].direct:
            return parts[c].grad.at[window(c, dp_at(step))]
        return parts[c].y_in.at[dp_at(step)]

    def rs_z(c, step):
        slot = parts[c].z_in.at[step - 1]
        return Copy(z_out(c, step), slot, two.rsz, (c, step - 1), {"dp": dp_at(step)})

    def rs_fold(c, step):
        neighbour = 1 if step == dp - 1 else dp - 2
        return Copy(z_out(c, step), parts[c].fold, two.rsn, c, {"dp": neighbour})

    def rs_f(c):
        part_c = parts[c]
        if part_c.direct:
            return Copy(part_c.z_in.at[0], part_c.y_in, two.rsf, c, {"ctx": peer})
        area = part_c.fin.at[fin_rows(c, side)]
        return Copy(part_c.z_in.at[0], area, two.rsf, c, {"ctx": peer})

    def fin_copy(c):
        part_c = parts[c]
        if part_c.direct:
            area = part_c.fin.at[fin_rows(c)]
            return pltpu.make_async_copy(part_c.z_in.at[1], area, r.fin_sem.at[c])
        area = part_c.fin.at[fin_rows(c, side)]
        return pltpu.make_async_copy(part_c.z_in.at[0], area, r.fin_sem.at[c])

    steps = sorted(range(1, dp), key=lambda step: (step not in (1, dp - 1), step))

    def send_piece(c, step):
        send_when(
            c,
            step,
            lambda: rs_z(c, step).start(),
            lambda: rs_fold(c, step).start(),
            lambda: None,
        )

    def rs_start(c):
        if c not in parts:
            return
        if parts[c].direct:
            end_when(c, lambda step: rs_fold(c, step).start())
            if not fold_of(c) or c != 2 + nt:
                first_rest(c)
            return
        for step in steps + [0]:
            rs_y(c, dp_at(step)).start()

    def first_rest(c):
        for step in steps:
            send_when(c, step, lambda: rs_z(c, step).start(), lambda: None, lambda: None)

    def rs_mid(c):
        if c not in parts:
            return
        part_c = parts[c]
        for step in steps + [0]:
            p = dp_at(step)
            rs_y(c, p).wait_recv()
            mine = part_c.grad[window(c, p, side), :].astype(F32)
            part_c.y_in[p] = (mine + part_c.y_in[p].astype(F32)).astype(BF16)
            if step:
                send_piece(c, step)

    def rs_join(c):
        if c not in parts:
            return
        part_c = parts[c]

        def one(step):
            rs_fold(c, dp - 1).wait_recv()
            extra = part_c.fold[...].astype(F32)
            p = dp_at(step)
            if part_c.direct:
                at = window(c, p)
                part_c.grad[at, :] = (part_c.grad[at, :].astype(F32) + extra).astype(BF16)
            else:
                part_c.y_in[p] = (part_c.y_in[p].astype(F32) + extra).astype(BF16)
            rs_z(c, step).start()

        fold_when(c, one)

    def blank(c):
        def zero(step):
            slot = parts[c].z_in
            slot[step - 1] = jnp.zeros(slot.shape[1:], BF16)

        if fold_of(c):
            pl.when(me == 0)(lambda: zero(1))
            pl.when(me == dp - 1)(lambda: zero(dp - 1))

    def rs_fin(c):
        if c not in parts:
            return
        part_c = parts[c]
        for step in range(1, dp):
            taken(c, step, lambda: rs_z(c, step).wait_recv())
        blank(c)
        if part_c.direct:
            total = part_c.grad[window(c, me), :].astype(F32)
        else:
            total = part_c.y_in[me].astype(F32)
        for step in range(1, dp):
            total += part_c.z_in[step - 1].astype(F32)
        part_c.z_in[0] = total.astype(BF16)
        rs_f(c).start()
        if not part_c.direct:
            fin_copy(c).start()

    def rs_last(c):
        if c not in parts:
            return
        part_c = parts[c]
        rs_f(c).wait_recv()
        total = part_c.z_in[0].astype(F32) + part_c.y_in[...].astype(F32)
        part_c.z_in[1] = total.astype(BF16)
        fin_copy(c).start()

    def rs_end(c):
        part_c = parts[c]
        for step in range(1, dp):
            wait = lambda: rs_z(c, step).wait_send()
            send_when(c, step, wait, lambda: None, wait)
        end_when(c, lambda step: rs_fold(c, step).wait_send())
        if not part_c.direct:
            for p in range(dp):
                rs_y(c, p).wait_send()
            rs_f(c).wait_recv()
        rs_f(c).wait_send()
        fin_copy(c).wait()

    def acc_low(source, target, s):
        def one(i):
            at = pl.ds(pl.multiple_of(s * local + i * tb, tb), tb)
            target[at, :] = source[at, :].astype(BF16)

        each(local // tb, one)

    for t in range(nt):
        ffn_rows(t, 0)
        if t == 0:
            spread_end(0, 1)
            transpose_into(hn, hn_t, local, local // tb)
            for c in range(4, nt + 2):
                serve(c)
        if t == 1 and fold_of(2 + nt):
            first_rest(2 + nt)
        if t == nt - 1:
            sum1_start(1, 0)
        if t == 2:
            rs_join(2 + nt)
        ffn_rows(t, 1)
        if t == nt - 1:
            sum1_start(1, 1)
            sum2_start(1, 0)
        ffn_weights(t)
        rs_start(2 + nt + t)
        rs_start(2 + t)
        if t + 1 < nt:
            ag_end(2 + t + 1)
        if t == 0:
            pass

    def middle_back(s):
        incoming = sum_end(1, s)
        value = mid[share_at(s), :]
        factor = lax.rsqrt(mean_square(value) + EPSILON)
        hat = value * factor
        small[1:2, :] += jnp.sum(incoming * hat, axis=0, keepdims=True)
        grad_hat = incoming * r.gain_w[1:2, :]
        back = factor * (grad_hat - hat * jnp.mean(grad_hat * hat, axis=-1, keepdims=True))
        total = dy[token_rows(s, chip, core), :].astype(F32) + back
        grad_hidden[share_at(s), :] = total
        spread1_start(1, s, total.astype(BF16))

    def again(first, count):
        def one(i):
            at = pl.ds(pl.multiple_of(first + i * tb, tb), tb)
            value = x[at, :].astype(F32)
            value = value * lax.rsqrt(mean_square(value) + EPSILON)
            value = (value * r.gain_w[0:1, :]).astype(BF16).astype(F32)
            hn_t[:, at] = value.T.astype(BF16)

        each(count, one)

    sum2_start(1, 1)
    again(0, rows // tb)
    if nt < 3:
        rs_join(2 + nt)
    rs_mid(2)
    middle_back(0)
    middle_back(1)
    for s in range(seqs):
        acc_low(acc_m, part, s)
        sum1_start(3, s)
    spread2_start(1, 0)

    spread2_start(1, 1)
    for s in range(seqs):
        sum2_start(3, s)

    g_kv, gq_t = r.g_kv, r.gq_t

    def out_back(s):
        def one(i):
            at = pl.ds(pl.multiple_of(s * local + i * rb, rb), rb)
            value = dot(hn[at, :], mat_o[...])
            for h in range(qh):
                piece = value[:, h * head : (h + 1) * head]
                start = nqkv + h * 2 * head
                units[at, start : start + 2 * head] = jnp.concatenate(
                    [jnp.zeros_like(piece), piece], axis=1
                ).astype(BF16)

        each(local // rb, one)

    def attend_back(s, with_peer):
        for h in range(kh):
            g_kv[s * kh + h] = jnp.zeros_like(g_kv[s * kh + h])

        def one(index):
            for j in range(local // qb):
                parts, head_kv, here = masked(s, j, index, with_peer)
                at = slice(j * qb, (j + 1) * qb)
                token = slice(s * local + j * qb, s * local + (j + 1) * qb)
                lanes = pl.ds(pl.multiple_of(nqkv + index * 2 * head, 128), 2 * head)
                go = units[token, lanes]
                logs = lse[s * qh + index, :, at]
                probs = [jnp.exp(p[0] - logs) for p in parts]
                grad_probs = [dot_nt(kv[head_kv, w, :size, :], go) for _, w, size in parts]
                row_dot = sum(
                    jnp.sum(p * g, axis=0, keepdims=True) for p, g in zip(probs, grad_probs)
                )
                out = jnp.zeros((2 * head, qb), F32)
                for (_, w, size), p, g in zip(parts, probs, grad_probs):
                    gs = (p * (g - row_dot)).astype(BF16)
                    out += dot(kv_t[head_kv, w, :, :size], gs)
                    g_kv[head_kv, w, :size, :] += dot(gs, here) + dot(p.astype(BF16), go)
                spot = pl.ds(pl.multiple_of(index * head, head), head)
                gq_t[s, spot, at] = out[:head, :] * scale

        each(qh, one)

    def back_copy(s):
        return Copy(
            r.g_kv_low.at[pl.ds(s * kh, kh)],
            r.g_kv_in.at[pl.ds(s * kh, kh)],
            two.gkv,
            s,
            {"ctx": peer},
        )

    def attend_back_any(s):
        @pl.when(side == 0)
        def _():
            attend_back(s, False)

        @pl.when(side != 0)
        def _():
            attend_back(s, True)
            for h in range(kh):
                r.g_kv_low[s * kh + h] = g_kv[s * kh + h, 1].astype(BF16)
            back_copy(s).start()

    def kv_back_arrive(s):
        @pl.when(side == 0)
        def _():
            back_copy(s).wait_recv()
            for h in range(kh):
                g_kv[s * kh + h, 0] += r.g_kv_in[s * kh + h].astype(F32)

        @pl.when(side != 0)
        def _():
            back_copy(s).wait_send()

    def project_back(s):
        def one(i):
            at = pl.ds(pl.multiple_of(s * local + i * rb, rb), rb)
            inner = pl.ds(aligned(i, rb), rb)
            gkv = [g_kv[s * kh + h, 0, inner, :] for h in range(kh)]
            if kh == 1:
                g_key, g_value = gkv[0][:, :head], gkv[0][:, head:]
            else:
                keys, values = [], []
                for h in range(0, kh, 2):
                    keys.append(jnp.where(low_half, gkv[h], pltpu.roll(gkv[h + 1], head, 1)))
                    values.append(jnp.where(low_half, pltpu.roll(gkv[h], head, 1), gkv[h + 1]))
                g_key = jnp.concatenate(keys, axis=1)
                g_value = jnp.concatenate(values, axis=1)
            value = jnp.concatenate([gq_t[s, :, inner].T, g_key], axis=1)
            cosine = widen(tab[at, : 2 * head], nqk)
            sine = widen(tab[at, 2 * head :], nqk)
            value = value * cosine - swap_halves(value, head) * sine
            plain = raw[at, :]
            factor = lax.rsqrt(spread_means(plain * plain, head) + EPSILON)
            hat = plain * factor
            small[2:3, :nqk] += jnp.sum(value * hat, axis=0, keepdims=True)
            grad_hat = value * r.gain_h[0:1, :]
            value = factor * (grad_hat - hat * spread_means(grad_hat * hat, head))
            low = jnp.concatenate([value, g_value], axis=1).astype(BF16)
            units[at, :nqkv] = low
            part[at, :] = dot_nt(low, mat_q[...]).astype(BF16)

        each(local // rb, one)

    def out_weights():
        for i in range(width // rb):
            total = sum(
                dot(o_t[s], hn[s * local : (s + 1) * local, i * rb : (i + 1) * rb])
                for s in range(seqs)
            )
            r.grad_o[i * rb : (i + 1) * rb, :] = total.T.astype(BF16)

    def qkv_weights():
        def one(i):
            at = pl.ds(aligned(i, rb), rb)
            r.grad_q[at, :] = dot(hn_t[at, :], units[:, :nqkv]).astype(BF16)

        each(width // rb, one)

    if nt > 1:
        rs_mid(3)
    rs_join(2)
    spread_end(1, 0)
    out_back(0)
    attend_back_any(0)
    spread_end(1, 1)
    out_back(1)
    rs_fin(2 + nt)
    rs_fin(2)
    if nt > 1:
        rs_join(3 + nt)
    attend_back_any(1)
    out_weights()
    rs_start(1)
    if nt > 1:
        rs_join(3)

    def mlp_end(s):
        mlp = sum_end(3, s)
        weight = keep_of(s)[:, 0:1]
        small[4:5, 384:512] += fold_lanes(weight * mlp * mlp)
        small[4:5, 512:640] += jnp.sum(keep_of(s), axis=0, keepdims=True)
        mid[share_at(s), :] += mlp

    if nt > 2:
        rs_mid(4)
        rs_join(4 + nt)
    for s in range(seqs):
        mlp_end(s)
    kv_back_arrive(0)
    project_back(0)
    sum1_start(2, 0)
    rs_last(2 + nt)
    if nt > 1:
        rs_fin(3 + nt)
    kv_back_arrive(1)
    project_back(1)
    sum1_start(2, 1)
    sum2_start(2, 0)
    qkv_weights()
    rs_start(0)
    sum2_start(2, 1)
    if nt > 2:
        rs_join(4)
    if nt > 1:
        rs_fin(3)
    if nt > 2:
        rs_fin(4 + nt)
    rs_mid(1)

    def first_back(s):
        incoming = sum_end(2, s)
        value = x[token_rows(s, chip, core), :].astype(F32)
        factor = lax.rsqrt(mean_square(value) + EPSILON)
        hat = value * factor
        small[0:1, :] += jnp.sum(incoming * hat, axis=0, keepdims=True)
        grad_hat = incoming * r.gain_w[0:1, :]
        back = factor * (grad_hat - hat * jnp.mean(grad_hat * hat, axis=-1, keepdims=True))
        grad_hidden[share_at(s), :] += back

    first_back(0)
    first_back(1)
    rs_mid(0)

    small_in = r.small_in

    def small_round(start, copies, order):
        for c in copies:
            c.start()
        for c in copies:
            c.wait_recv()
            c.wait_send()
        total = None
        for o in order:
            term = small_in[start + o]
            total = term if total is None else total + term
        small[...] = total

    small_in[pl.ds(core, 1)] = small[...][None]
    small_round(
        0, [Copy(small, small_in.at[core], two.small, 0, {"tp": other_core})], range(2)
    )
    small_in[pl.ds(2 + side, 1)] = small[...][None]
    small_round(2, [Copy(small, small_in.at[2 + side], two.small, 1, {"ctx": peer})], range(2))
    small_in[pl.ds(4 + chip, 1)] = small[...][None]
    small_round(
        4,
        [
            Copy(small, small_in.at[4 + chip], two.small, 1 + s, {"tp": chip_lane(s)})
            for s in range(1, chips)
        ],
        range(chips),
    )
    rs_fin(1)
    if nt > 2:
        rs_fin(4)
        rs_last(4 + nt)
    small_in[pl.ds(4 + chips + me, 1)] = small[...][None]
    small_round(
        4 + chips,
        [
            Copy(small, small_in.at[4 + chips + me], two.small, chips + s, {"dp": dp_at(s)})
            for s in range(1, dp)
        ],
        range(dp),
    )
    def mine_of(value, size):
        return sum(
            jnp.where(me == d, value[:, d * size : (d + 1) * size], 0.0) for d in range(dp)
        )

    r.own_attn[...] = mine_of(small[0:1, :], dd)
    r.own_ffn[...] = mine_of(small[1:2, :], dd)
    row = small[2:3, :nqk]
    over_q = sum(row[:, h * head : (h + 1) * head] for h in range(qh))
    over_k = sum(row[:, h * head : (h + 1) * head] for h in range(qh, qh + kh))
    r.own_query[...] = mine_of(over_q, piece)
    r.own_key[...] = mine_of(over_k, piece)
    totals = [
        jnp.sum(small[4:5, i * 128 : (i + 1) * 128], axis=1, keepdims=True) for i in range(4)
    ]
    count = small[4:5, 512:513] * width
    r.own_stat[...] = jnp.sqrt(jnp.concatenate(totals, axis=1) / count)
    if nt > 1:
        rs_last(3 + nt)
    rs_fin(0)
    for c in sorted(parts, reverse=True):
        rs_end(c)


def per_device(
    sizes,
    hidden_states,
    out_grad,
    w_query,
    w_key,
    w_value,
    w_out,
    w_gate,
    w_up,
    w_down,
    attn_gain,
    ffn_gain,
    query_gain,
    key_gain,
    segment_ids,
    valid_mask,
    positions,
):
    seqs, local, width = hidden_states.shape
    dp, ctx, tp = sizes
    rows = seqs * local
    head = query_gain.shape[0] * dp
    nq, nk, units = w_query.shape[1], w_key.shape[1], w_gate.shape[1]
    nqkv = nq + 2 * nk
    nt = 3 if units % 3 == 0 else 1
    ft = units // nt
    dd = width // dp
    hd = dd // ctx
    share = local // tp
    chips = tp // 2
    qh, kh = nq // head, nk // head
    plain = ft % 128 == 0 and dd % 128 == 0 and nk % 128 == 0
    cuts = [dd if t < 1 else dd // 2 if t < 2 else 0 for t in range(nt)]
    cfg = types.SimpleNamespace(
        seqs=seqs, local=local, width=width, head=head, dp=dp, ctx=ctx, tp=tp,
        qh=qh, kh=kh, nt=nt, ft=ft, plain=plain, cuts=cuts,
    )
    gains = jnp.concatenate([attn_gain, ffn_gain, query_gain, key_gain])
    gains = gains.astype(F32).reshape(1, -1)
    half = head // 2
    freq = np.float32(ROPE_BASE) ** (-(np.arange(half, dtype=np.float32) * 2.0) / head)
    freq = jnp.asarray(np.tile(freq.astype(np.float32), 128 // half)[None])
    inputs = dict(
        x=(hidden_states.reshape(rows, width), True),
        dy=(out_grad.reshape(rows, width), True),
        gains=(gains, True),
        segment_ids=(segment_ids, True),
        valid_mask=(valid_mask, True),
        positions=(positions, True),
        freq=(freq, True),
    )
    if plain:
        inputs.update(
            w_query=(w_query, False),
            w_key=(w_key, False),
            w_value=(w_value, False),
            w_out=(w_out, False),
            w_gate=(w_gate, False),
            w_up=(w_up, False),
            w_down=(w_down, False),
        )
    else:
        tiles = []
        for i in range(nt):
            cut = slice(i * ft, (i + 1) * ft)
            tiles.append(jnp.concatenate([w_gate[:, cut], w_up[:, cut], w_down[cut].T], axis=1))
        inputs.update(
            w_qkv=(jnp.concatenate([w_query, w_key, w_value], axis=1), False),
            w_o=(w_out.T, False),
            w_f=(jnp.stack(tiles), False),
        )
    outputs = dict(
        result=((seqs * share, width), F32),
        grad_hidden=((seqs * share, width), F32),
        fin_q=((dd, nqkv), BF16),
        fin_o=((dd, nq), BF16),
        fin_f=((nt, dd, 3 * ft), BF16),
        own_attn=((1, dd), F32),
        own_ffn=((1, dd), F32),
        own_query=((1, head // dp), F32),
        own_key=((1, head // dp), F32),
        own_stat=((1, 4), F32),
    )
    scratch = dict(
        mat_q=((width, nqkv), BF16),
        mat_o=((width, nq), BF16),
        mat_f=((nt, width, 3 * ft), BF16),
        gain_buf=((dp, 1, 2 * dd + 2 * head // dp), F32),
        facts=((seqs, 2, local), F32),
        gain_w=((8, width), F32),
        gain_h=((8, nq + nk), F32),
        code_peer=((seqs, 2, local), F32),
        tab=((rows, 256), F32),
        key_code=((ctx, seqs, local, 128), F32),
        hn=((rows, width), BF16),
        hn_t=((width, rows), BF16),
        dr_t=((width, rows), BF16),
        raw=((rows, nq + nk), F32),
        q_pad=((seqs * qh, local, 2 * head), BF16),
        kv=((seqs * kh, ctx, local, 2 * head), BF16),
        kv_t=((seqs * kh, ctx, 2 * head, local), BF16),
        g_kv=((seqs * kh, ctx, local, 2 * head), F32),
        g_kv_low=((seqs * kh, local, 2 * head), BF16),
        g_kv_in=((seqs * kh, local, 2 * head), BF16),
        o_t=((seqs, nq, local), BF16),
        gq_t=((seqs, nq, local), F32),
        lse=((seqs * qh, 1, local), F32),
        part=((rows, width), BF16),
        near=((2, seqs, chips, share, width), BF16),
        pair=((seqs, chips, share, width), BF16),
        far=((2, seqs, max(chips - 1, 1), share, width), BF16),
        small=((8, width), F32),
        small_in=((4 + chips + dp, 8, width), F32),
        units=((rows, 3 * ft), BF16),
        acc_m=((rows, width), F32),
        acc_h=((rows, width), F32),
        grad_q=((width, nqkv), BF16),
        grad_o=((width, nq), BF16),
        y0=((dp, hd, nqkv), BF16),
        y1=((dp, hd, nq), BF16),
        z0=((dp - 1, hd, nqkv), BF16),
        z1=((dp - 1, hd, nq), BF16),
    )
    for t in range(nt):
        cut = cfg.cuts[t]
        if cut < dd:
            size = (dd - cut) // ctx
            scratch[f"y{2 + t}"] = ((dp, size, 3 * ft), BF16)
            scratch[f"z{2 + t}"] = ((dp - 1, size, 3 * ft), BF16)
            scratch[f"fold{2 + t}"] = ((size, 3 * ft), BF16)
        if cut:
            scratch[f"y{2 + nt + t}"] = ((cut, 3 * ft), BF16)
            scratch[f"z{2 + nt + t}"] = ((dp - 1, cut, 3 * ft), BF16)
            scratch[f"fold{2 + nt + t}"] = ((cut, 3 * ft), BF16)
    pairs = dict(
        agz=(nt + 2, dp - 1),
        agy=(nt + 2, dp - 1),
        gain=(dp - 1,),
        code=(1,),
        kv=(seqs,),
        gkv=(seqs,),
        sum1=(4, seqs * chips),
        sum2=(4, seqs * max(chips - 1, 1)),
        spread1=(2, seqs * max(chips - 1, 1)),
        spread2=(2, seqs * chips),
        rsy=(2 * nt + 2, dp),
        rsz=(2 * nt + 2, dp - 1),
        rsf=(2 * nt + 2,),
        small=(chips + dp,),
        rsn=(2 * nt + 2,),
    )
    singles = dict(own_sem=(nt + 2, 3), agfar=(nt + 2,), fin_sem=(2 * nt + 2,))
    shapes = list(singles.values()) + [v for v in pairs.values() for _ in range(2)]

    def kernel(*refs):
        refs = list(refs)
        r = types.SimpleNamespace()
        for name in list(inputs) + list(outputs) + list(scratch) + list(singles):
            setattr(r, name, refs.pop(0))
        two = types.SimpleNamespace()
        for name in pairs:
            setattr(two, name, (refs.pop(0), refs.pop(0)))
        block_kernel(cfg, r, two)

    vmem = pl.BlockSpec(memory_space=pltpu.VMEM)
    away = pl.BlockSpec(memory_space=pl.ANY)
    out = pl.pallas_call(
        kernel,
        out_shape=[jax.ShapeDtypeStruct(*v) for v in outputs.values()],
        in_specs=[vmem if v else away for _, v in inputs.values()],
        out_specs=[away if n.startswith("fin") else vmem for n in outputs],
        scratch_shapes=[pltpu.VMEM(*v) for v in scratch.values()]
        + [pltpu.SemaphoreType.DMA(v) for v in shapes],
        compiler_params=pltpu.CompilerParams(
            collective_id=0, has_side_effects=True, vmem_limit_bytes=VMEM_LIMIT
        ),
    )(*[v for v, _ in inputs.values()])
    result, grad_hidden, fin_q, fin_o, fin_f = out[:5]

    gates = [fin_f[i, :, :ft] for i in range(nt)]
    ups = [fin_f[i, :, ft : 2 * ft] for i in range(nt)]
    downs = [fin_f[i, :, 2 * ft :] for i in range(nt)]
    return (
        result.reshape(seqs, share, width),
        grad_hidden.reshape(seqs, share, width),
        fin_q[:, :nq].astype(F32),
        fin_q[:, nq : nq + nk].astype(F32),
        fin_q[:, nq + nk :].astype(F32),
        fin_o.T.astype(F32),
        jnp.concatenate(gates, axis=1).astype(F32),
        jnp.concatenate(ups, axis=1).astype(F32),
        jnp.concatenate([d.T for d in downs], axis=0).astype(F32),
        *[value.reshape(-1) for value in out[5:]],
    )


VMEM_LIMIT = 63 * 2**20


def solution(mesh):
    sizes = tuple(mesh.shape[a] for a in ("dp", "ctx", "tp"))
    return jax.shard_map(
        functools.partial(per_device, sizes),
        mesh=mesh,
        in_specs=(
            P("dp", "ctx", None),
            P("dp", "ctx", None),
            P("dp", "tp"),
            P("dp", "tp"),
            P("dp", "tp"),
            P("tp", "dp"),
            P("dp", "tp"),
            P("dp", "tp"),
            P("tp", "dp"),
            P("dp"),
            P("dp"),
            P("dp"),
            P("dp"),
            P("dp", "ctx"),
            P("dp", "ctx"),
            P("dp", "ctx"),
        ),
        out_specs=(
            P("dp", ("ctx", "tp"), None),
            P("dp", ("ctx", "tp"), None),
            P("dp", "tp"),
            P("dp", "tp"),
            P("dp", "tp"),
            P("tp", "dp"),
            P("dp", "tp"),
            P("dp", "tp"),
            P("tp", "dp"),
            P("dp"),
            P("dp"),
            P("dp"),
            P("dp"),
            P(),
        ),
        check_vma=False,
    )
```

```python
import functools
import types

import jax
import jax.numpy as jnp
import numpy as np
from jax import lax
from jax.experimental import pallas as pl
from jax.experimental.pallas import tpu as pltpu
from jax.sharding import PartitionSpec as P

EPSILON = 1e-05
ROPE_BASE = 1000000.0
F32 = jnp.float32
BF16 = jnp.bfloat16
MESH = pl.DeviceIdType.MESH
NEGATIVE = -1e30
PADDING = 50000.0


def dot(left, right):
    return jnp.dot(left, right, preferred_element_type=F32)


def dot_nt(left, right):
    return lax.dot_general(left, right, (((1,), (1,)), ((), ())), preferred_element_type=F32)


def each(count, body):
    def step(i, carry):
        body(i)
        return carry

    lax.fori_loop(0, count, step, 0)


def aligned(index, unit):
    return pl.multiple_of(index * unit, unit)


def mean_square(value):
    return jnp.mean(value * value, axis=-1, keepdims=True)


def swap_halves(value, head):
    half = head // 2
    size = value.shape[1]
    if size % 128 == 0:
        at = lax.broadcasted_iota(jnp.int32, (1, size), 1)
        first = lax.rem(at, head) < half
        return jnp.where(first, pltpu.roll(value, size - half, 1), pltpu.roll(value, half, 1))
    pieces = []
    for start in range(0, size, head):
        pieces += [value[:, start + half : start + head], value[:, start : start + half]]
    return jnp.concatenate(pieces, axis=1)


def spread_means(value, head):
    size = value.shape[1]
    row = lax.div(lax.broadcasted_iota(jnp.int32, (size, size), 0), head)
    column = lax.div(lax.broadcasted_iota(jnp.int32, (size, size), 1), head)
    block = jnp.where(row == column, 1.0 / head, 0.0).astype(BF16)
    high = value.astype(BF16)
    rest = (value - high.astype(F32)).astype(BF16)
    return dot(high, block) + dot(rest, block)


def widen(value, count):
    size = value.shape[1]
    if count <= size:
        return value[:, :count]
    return jnp.concatenate([value] * -(-count // size), axis=1)[:, :count]


def fold_lanes(value):
    total = jnp.sum(value, axis=0, keepdims=True)
    out = total[:, :128]
    for i in range(1, value.shape[1] // 128):
        out += total[:, i * 128 : (i + 1) * 128]
    return out


class Copy:
    def __init__(self, src, dst, sems, index, device, send=None):
        send = sems[0].at[index] if send is None else send
        self.copy = pltpu.make_async_remote_copy(
            src_ref=src,
            dst_ref=dst,
            send_sem=send,
            recv_sem=sems[1].at[index],
            device_id=device,
            device_id_type=MESH,
        )

    def start(self):
        self.copy.start()

    def wait_send(self):
        self.copy.wait_send()

    def wait_recv(self):
        self.copy.wait_recv()


def block_kernel(cfg, r, two):
    seqs, local, width, head = cfg.seqs, cfg.local, cfg.width, cfg.head
    dp, ctx, tp = cfg.dp, cfg.ctx, cfg.tp
    qh, kh, nt, ft = cfg.qh, cfg.kh, cfg.nt, cfg.ft
    nq, nk = qh * head, kh * head
    nqkv = nq + 2 * nk
    group = qh // kh
    chips = tp // 2
    rows = seqs * local
    share = local // tp
    dd = width // dp
    hd = dd // ctx
    me, side, lane = lax.axis_index("dp"), lax.axis_index("ctx"), lax.axis_index("tp")
    core, chip = lax.rem(lane, 2), lax.div(lane, 2)
    other_core = lane + 1 - 2 * core
    peer = 1 - side
    rb = min(256, local)
    qb = min(256, local)
    tb = min(128, local)
    scale = head**-0.5

    def dp_at(step):
        return lax.rem(me + step, dp)

    def chip_lane(step):
        return lax.rem(chip + step, chips) * 2 + core

    barrier = pltpu.get_barrier_semaphore()
    greet = [{"dp": dp_at(s)} for s in range(1, dp)] + [{"ctx": peer}, {"tp": other_core}]
    greet += [{"tp": chip_lane(s)} for s in range(1, chips)]
    for device in greet:
        pl.semaphore_signal(barrier, inc=1, device_id=device, device_id_type=MESH)
    pl.semaphore_wait(barrier, len(greet))

    whole = [r.mat_q, r.mat_o] + [r.mat_f.at[t] for t in range(nt)]

    def my_rows(owner, which):
        return pl.ds(pl.multiple_of(owner * dd + which * hd, hd), hd)

    solo = ()

    def ag_rows(c, owner):
        if c in solo:
            return pl.ds(aligned(owner, dd), dd)
        return my_rows(owner, side)

    def ag_z(c, step):
        return Copy(
            whole[c].at[ag_rows(c, me)],
            whole[c].at[ag_rows(c, me)],
            two.agz,
            (c, step - 1),
            {"dp": dp_at(step)},
        )

    def ag_y(c, step):
        owner = lax.rem(me - step + dp, dp)
        area = whole[c].at[my_rows(owner, side)]
        return Copy(area, area, two.agy, (c, step - 1), {"ctx": peer})

    relayed = (0,) + tuple(range(2, nt + 2)) if dp > 2 else ()
    hops = [dp - 2, 2] if dp > 2 else []
    order = sorted(range(1, dp), key=lambda step: (step not in hops, step))

    def ag_far(c, step):
        owner, target = (0, dp - 1) if step == dp - 2 else (dp - 1, 0)
        if dp == 4:
            owner = jnp.where(me == 1, dp - 1, 0)
            target = jnp.where(me == 1, 0, dp - 1)
        area = whole[c].at[ag_rows(c, owner)]
        index = lax.rem(target - owner + dp, dp) - 1
        send = r.agfar.at[c]
        return Copy(area, area, two.agz, (c, index), {"dp": target}, send)

    def far_when(c, step, body):
        if c not in relayed:
            return
        if dp == 4:
            if step == 2:
                pl.when((me == 1) | (me == 2))(body)
        elif step == dp - 2:
            pl.when(me == dp - 2)(body)
        elif step == 2:
            pl.when(me == 1)(body)

    def near_when(c, step, body):
        if c in relayed and step == dp - 1:
            pl.when(me != 0)(body)
        elif c in relayed and step == 1:
            pl.when(me != dp - 1)(body)
        else:
            body()

    own_rows = pl.ds(aligned(me, dd), dd)

    def stage(c):
        if c == 1:
            return r.units.at[pl.ds(ft, nq), pl.ds(0, dd)]
        return r.units.at[pl.ds(0, ft), pl.ds((c - 2) * dd, dd)]

    def own_moves(c):
        if not cfg.plain:
            source = [r.w_qkv, r.w_o] + [r.w_f.at[t] for t in range(nt)]
            pairs_of = [(source[c], whole[c].at[own_rows])]
        elif c == 0:
            pairs_of, start = [], 0
            for source in (r.w_query, r.w_key, r.w_value):
                size = source.shape[1]
                pairs_of.append((source, r.mat_q.at[own_rows, pl.ds(start, size)]))
                start += size
        elif c == 1:
            pairs_of = [(r.w_out, stage(1))]
        else:
            t = c - 2
            at = pl.ds(t * ft, ft)
            pairs_of = [
                (r.w_gate.at[:, at], r.mat_f.at[t, own_rows, pl.ds(0, ft)]),
                (r.w_up.at[:, at], r.mat_f.at[t, own_rows, pl.ds(ft, ft)]),
                (r.w_down.at[at], stage(c)),
            ]
        return [
            pltpu.make_async_copy(source, target, r.own_sem.at[c, i])
            for i, (source, target) in enumerate(pairs_of)
        ]

    def own_start(c):
        for move in own_moves(c):
            move.start()

    def own_end(c):
        for move in own_moves(c):
            move.wait()
        if cfg.plain and c >= 1:
            block = stage(c)[...].astype(F32).T.astype(BF16)
            if c == 1:
                r.mat_o[own_rows, :] = block
            else:
                r.mat_f[c - 2, own_rows, 2 * ft :] = block

    def ag_start(c, early=True, late=True):
        if c >= nt + 2:
            return
        for step in order:
            if not (early if step in hops else late):
                continue
            near_when(c, step, lambda: ag_z(c, step).start())

    def ag_pass_one(c, step):
        ag_z(c, step).wait_recv()
        far_when(c, step, lambda: ag_far(c, step).start())
        if c not in solo:
            ag_y(c, step).start()

    served = set()

    def serve(c, early=True, late=True):
        for step in order:
            if c < nt + 2 and (c, step) not in served and (early if step in hops else late):
                served.add((c, step))
                ag_pass_one(c, step)

    def ag_end(c):
        serve(c)
        for step in order:
            if c not in solo:
                ag_y(c, step).wait_recv()
                ag_y(c, step).wait_send()
            near_when(c, step, lambda: ag_z(c, step).wait_send())
            far_when(c, step, lambda: ag_far(c, step).wait_send())

    gain_buf = r.gain_buf

    def gain_copy(step):
        return Copy(
            r.gains, gain_buf.at[me], two.gain, step - 1, {"dp": dp_at(step)}
        )

    for s in range(seqs):
        token = lax.broadcasted_iota(jnp.int32, (1, local), 1) + side * local + 100000
        real = r.valid_mask[s : s + 1, :] == 1
        code = jnp.where(real, r.segment_ids[s : s + 1, :], token)
        r.facts[s, 0:1, :] = code.astype(F32)
        r.facts[s, 1:2, :] = r.positions[s : s + 1, :].astype(F32)

    def code_copy():
        return Copy(r.facts, r.code_peer, two.code, 0, {"ctx": peer})

    for c in range(nt + 2):
        own_start(c)
    for step in range(1, dp):
        gain_copy(step).start()
    own_end(0)
    ag_start(0)
    code_copy().start()
    for c in range(1, nt + 2):
        own_end(c)

    x, dy, hn, hn_t, dr_t = r.x, r.dy, r.hn, r.hn_t, r.dr_t

    def transpose_into(source, target, first, count):
        def one(i):
            at = pl.ds(pl.multiple_of(first + i * tb, tb), tb)
            target[:, at] = source[at, :].astype(F32).T.astype(BF16)

        each(count, one)

    def code_columns(source, which):
        for s in range(seqs):
            row = jnp.broadcast_to(source[s, 0:1, :], (128, local))
            r.key_code[which, s] = row.T

    code_columns(r.facts, 0)

    sign = lax.rem(lax.broadcasted_iota(jnp.int32, (1, 128), 1), head) < head // 2
    sign = jnp.where(sign, -1.0, 1.0).astype(F32)
    for s in range(seqs):
        for start in range(0, local, tb):
            place = jnp.broadcast_to(r.facts[s, 1:2, start : start + tb], (128, tb)).T
            angle = place * r.freq[...]
            at = pl.ds(s * local + start, tb)
            r.tab[at, :128] = jnp.cos(angle)
            r.tab[at, 128:] = jnp.sin(angle) * sign

    gain_buf[pl.ds(me, 1)] = r.gains[...][None]
    for step in range(1, dp):
        gain_copy(step).wait_recv()
        gain_copy(step).wait_send()
    piece = head // dp
    for d in range(dp):
        r.gain_w[0:1, d * dd : (d + 1) * dd] = gain_buf[d, :, :dd]
        r.gain_w[1:2, d * dd : (d + 1) * dd] = gain_buf[d, :, dd : 2 * dd]
        for h in range(qh):
            start = h * head + d * piece
            r.gain_h[0:1, start : start + piece] = gain_buf[d, :, 2 * dd : 2 * dd + piece]
        for h in range(kh):
            start = nq + h * head + d * piece
            r.gain_h[0:1, start : start + piece] = gain_buf[d, :, 2 * dd + piece : 2 * dd + 2 * piece]

    def normed_into(target, first, count):
        def one(i):
            at = pl.ds(pl.multiple_of(first + i * tb, tb), tb)
            value = x[at, :].astype(F32)
            value = value * lax.rsqrt(mean_square(value) + EPSILON)
            target[at, :] = (value * r.gain_w[0:1, :]).astype(BF16)

        each(count, one)

    normed_into(hn, 0, rows // tb // 2)
    serve(0, late=False)
    normed_into(hn, rows // 2, rows // tb // 2)
    code_copy().wait_recv()
    code_copy().wait_send()
    code_columns(r.code_peer, 1)
    ag_start(2, late=False)
    serve(0)
    ag_start(1)
    transpose_into(dy, dr_t, 0, rows // tb)
    ag_start(2, early=False)
    ag_end(0)

    mat_q, mat_o, raw, tab = r.mat_q, r.mat_o, r.raw, r.tab
    q_pad, kv, kv_t = r.q_pad, r.kv, r.kv_t

    nqk = nq + nk
    low_half = lax.broadcasted_iota(jnp.int32, (1, 2 * head), 1) < head

    def pairs(value, start, count):
        out = []
        for h in range(0, count, 2):
            if count == 1:
                here = value[:, start : start + head]
                both = jnp.concatenate([here, here], axis=1)
                out.append((both, both))
                continue
            here = value[:, start + h * head : start + (h + 2) * head]
            turned = pltpu.roll(here, head, 1)
            out += [(here, turned), (turned, here)]
        return out

    def project(s):
        def one(i):
            at = pl.ds(pl.multiple_of(s * local + i * rb, rb), rb)
            inner = pl.ds(aligned(i, rb), rb)
            both = dot(hn[at, :], mat_q[...])
            plain = both[:, :nqk]
            raw[at, :] = plain
            cosine = widen(tab[at, : 2 * head], nqk)
            sine = widen(tab[at, 2 * head :], nqk)
            value = plain * lax.rsqrt(spread_means(plain * plain, head) + EPSILON)
            value = value * r.gain_h[0:1, :]
            value = value * cosine + swap_halves(value, head) * sine
            for h, (low, _) in enumerate(pairs(value, 0, qh)):
                q_pad[s * qh + h, inner, :] = jnp.where(low_half, low * scale, 0.0).astype(BF16)
            keys = pairs(value, nq, kh)
            values = pairs(both, nqk, kh)
            for h in range(kh):
                kv[s * kh + h, 0, inner, :] = jnp.where(
                    low_half, keys[h][0], values[h][1]
                ).astype(BF16)

        each(local // rb, one)

    def kv_copy(s):
        return Copy(
            kv.at[pl.ds(s * kh, kh), 0],
            kv.at[pl.ds(s * kh, kh), 1],
            two.kv,
            s,
            {"ctx": peer},
        )

    def kv_transpose(s, which):
        for h in range(kh):
            kv_t[s * kh + h, which] = kv[s * kh + h, which].astype(F32).T.astype(BF16)

    for s in range(seqs):
        project(s)

        @pl.when(side == 0)
        def _():
            kv_copy(s).start()

        kv_transpose(s, 0)
        if s == 0:
            serve(2, late=False)
            serve(1)
            ag_start(3, late=False)

    o_t, lse = r.o_t, r.lse

    def masked(s, j, index, with_peer):
        last = (j + 1) * qb
        head_kv = s * kh + index // group
        here = q_pad[s * qh + index, j * qb : last, :]
        query = r.facts[s, 0:1, j * qb : last]

        def spread(code):
            return jnp.concatenate([code] * (qb // 128), axis=1)

        own = dot_nt(kv[head_kv, 0, :last, :], here)
        key_at = lax.broadcasted_iota(jnp.int32, (last, qb), 0)
        query_at = lax.broadcasted_iota(jnp.int32, (last, qb), 1) + j * qb
        allowed = (spread(r.key_code[0, s, :last, :]) == query) & (key_at <= query_at)
        own = jnp.where(allowed, own, NEGATIVE)
        parts = [(own, 0, last)]
        if with_peer:
            far = dot_nt(kv[head_kv, 1], here)
            far = jnp.where(spread(r.key_code[1, s]) == query, far, NEGATIVE)
            parts.append((far, 1, local))
        return parts, head_kv, here

    def attend_one(s, index, with_peer):
        for j in range(local // qb):
            parts, head_kv, _ = masked(s, j, index, with_peer)
            highest = functools.reduce(
                jnp.maximum, [jnp.max(p[0], axis=0, keepdims=True) for p in parts]
            )
            expo = [jnp.exp(p[0] - highest) for p in parts]
            total = sum(jnp.sum(e, axis=0, keepdims=True) for e in expo)
            factor = 1.0 / total
            out = jnp.zeros((2 * head, qb), F32)
            for (_, which, size), e in zip(parts, expo):
                out += dot(kv_t[head_kv, which, :, :size], (e * factor).astype(BF16))
            at = pl.ds(pl.multiple_of(index * head, head), head)
            o_t[s, at, j * qb : (j + 1) * qb] = out[head:, :].astype(BF16)
            lse[s * qh + index, :, j * qb : (j + 1) * qb] = highest + jnp.log(total)

    def attend(s, first, count):
        def one(i):
            @pl.when(side == 0)
            def _():
                attend_one(s, first + i, False)

            @pl.when(side != 0)
            def _():
                attend_one(s, first + i, True)

        each(count, one)

    def kv_arrive(s):
        @pl.when(side == 0)
        def _():
            kv_copy(s).wait_send()

        @pl.when(side != 0)
        def _():
            kv_copy(s).wait_recv()
            kv_transpose(s, 1)

    part, near, pair, far = r.part, r.near, r.pair, r.far

    def pool(use):
        return 1 if use == 3 else 0

    def token_rows(s, which_chip, which_core):
        start = s * local + (which_chip * 2 + which_core) * share
        return pl.ds(pl.multiple_of(start, share), share)

    def sum1(use, s, c):
        return Copy(
            part.at[token_rows(s, c, 1 - core)],
            near.at[pool(use), s, c],
            two.sum1,
            (use, s * chips + c),
            {"tp": other_core},
        )

    def sum1_start(use, s):
        for c in range(chips):
            sum1(use, s, c).start()

    def sum2(use, s, step):
        return Copy(
            pair.at[s, lax.rem(chip + step, chips)],
            far.at[pool(use), s, step - 1],
            two.sum2,
            (use, s * max(chips - 1, 1) + step - 1),
            {"tp": chip_lane(step)},
        )

    def sum2_start(use, s):
        for c in range(chips):
            sum1(use, s, c).wait_recv()
        for c in range(chips):
            mine = part[token_rows(s, c, core), :].astype(F32)
            pair[s, c] = (mine + near[pool(use), s, c].astype(F32)).astype(BF16)
        for step in range(1, chips):
            sum2(use, s, step).start()

    def sum_end(use, s):
        for step in range(1, chips):
            sum2(use, s, step).wait_recv()
        total = part[token_rows(s, chip, core), :].astype(F32)
        total += near[pool(use), s, chip].astype(F32)
        for step in range(1, chips):
            total += far[pool(use), s, step - 1].astype(F32)
        for c in range(chips):
            sum1(use, s, c).wait_send()
        for step in range(1, chips):
            sum2(use, s, step).wait_send()
        return total

    def spread1(use, s, step):
        area = hn.at[token_rows(s, chip, core)]
        index = (use, s * max(chips - 1, 1) + step - 1)
        return Copy(area, area, two.spread1, index, {"tp": chip_lane(step)})

    def spread1_start(use, s, value):
        hn[token_rows(s, chip, core), :] = value
        for step in range(1, chips):
            spread1(use, s, step).start()

    def spread2(use, s, c):
        area = hn.at[token_rows(s, c, core)]
        return Copy(area, area, two.spread2, (use, s * chips + c), {"tp": other_core})

    def spread2_start(use, s):
        for step in range(1, chips):
            spread1(use, s, step).wait_recv()
        for c in range(chips):
            spread2(use, s, c).start()

    def spread_end(use, s):
        for c in range(chips):
            spread2(use, s, c).wait_recv()
            spread2(use, s, c).wait_send()
        for step in range(1, chips):
            spread1(use, s, step).wait_send()

    def out_project(s):
        def one(i):
            at = pl.ds(pl.multiple_of(s * local + i * rb, rb), rb)
            inner = pl.ds(aligned(i, rb), rb)
            o_rows = o_t[s, :, inner].astype(F32).T.astype(BF16)
            part[at, :] = dot_nt(o_rows, mat_o[...]).astype(BF16)

        each(local // rb, one)

    small, grad_hidden = r.small, r.grad_hidden
    mid = r.result
    small[...] = jnp.zeros_like(small)

    def share_at(s):
        return pl.ds(s * share, share)

    def keep_of(s):
        code = r.key_code[0, s, pl.ds(aligned(lane, share), share), :]
        return jnp.where(code < PADDING, 1.0, 0.0).astype(F32)

    def middle(s):
        attn = sum_end(0, s)
        value = x[token_rows(s, chip, core), :].astype(F32)
        weight = keep_of(s)[:, 0:1]
        small[4:5, 0:128] += fold_lanes(weight * value * value)
        small[4:5, 128:256] += fold_lanes(weight * attn * attn)
        value = value + attn
        mid[share_at(s), :] = value
        small[4:5, 256:384] += fold_lanes(weight * value * value)
        value = value * lax.rsqrt(mean_square(value) + EPSILON)
        spread1_start(0, s, (value * r.gain_w[1:2, :]).astype(BF16))

    half = qh // 2
    ag_start(3, early=False)
    kv_arrive(0)
    attend(0, 0, qh)
    serve(2)
    ag_end(1)
    out_project(0)
    sum1_start(0, 0)
    kv_arrive(1)
    attend(1, 0, half)
    sum2_start(0, 0)
    serve(3, late=False)
    ag_start(4, late=False)
    ag_start(4, early=False)
    attend(1, half, qh - half)
    out_project(1)
    sum1_start(0, 1)
    middle(0)
    sum2_start(0, 1)
    serve(3)
    spread2_start(0, 0)
    middle(1)
    serve(4, late=False)
    spread_end(0, 0)
    transpose_into(hn, hn_t, 0, local // tb)
    spread2_start(0, 1)
    ag_end(2)

    mat_f, units, acc_m, acc_h = r.mat_f, r.units, r.acc_m, r.acc_h

    def ffn_rows(t, s):
        def one(i):
            at = pl.ds(pl.multiple_of(s * local + i * rb, rb), rb)
            both = dot(hn[at, :], mat_f[t, :, : 2 * ft])
            gate, upward = both[:, :ft], both[:, ft:]
            sigmoid = 1.0 / (1.0 + jnp.exp(-gate))
            grad_inner = dot(dy[at, :], mat_f[t, :, 2 * ft :])
            silu = gate * sigmoid
            grad_up = (grad_inner * silu).astype(BF16)
            grad_gate = (
                grad_inner * upward * sigmoid * (1.0 + gate * (1.0 - sigmoid))
            ).astype(BF16)
            inner = (silu * upward).astype(BF16)
            grads = jnp.concatenate([grad_gate, grad_up], axis=1)
            units[at, : 2 * ft] = grads
            units[at, 2 * ft :] = inner
            back = dot_nt(grads, mat_f[t, :, : 2 * ft])
            ahead = dot_nt(inner, mat_f[t, :, 2 * ft :])
            if t > 0:
                back += acc_h[at, :]
                ahead += acc_m[at, :]
            if t < nt - 1:
                acc_h[at, :] = back
            else:
                part[at, :] = back.astype(BF16)
            acc_m[at, :] = ahead

        each(local // rb, one)

    def ffn_weights(t):
        def one(i):
            at = pl.ds(aligned(i, rb), rb)
            mat_f[t, at, : 2 * ft] = dot(hn_t[at, :], units[:, : 2 * ft]).astype(BF16)
            mat_f[t, at, 2 * ft :] = dot(dr_t[at, :], units[:, 2 * ft :]).astype(BF16)
            rows_done(2 + t, i)

        each(width // rb, one)

    folds = dp > 2
    parts = {}

    def add_part(c, grad, fin, first, size, direct, fold):
        half_size = size if direct else size // ctx
        parts[c] = types.SimpleNamespace(
            grad=grad, fin=fin, first=first, size=size, half=half_size, direct=direct,
            fold=fold, y_in=getattr(r, f"y{c}"), z_in=getattr(r, f"z{c}"),
        )

    add_part(0, r.grad_q, r.fin_q, 0, dd, False, None)
    add_part(1, r.grad_o, r.fin_o, 0, dd, False, None)
    for t in range(nt):
        cut = cfg.cuts[t]
        if cut < dd:
            c = 2 + t
            add_part(c, mat_f.at[t], r.fin_f.at[t], cut, dd - cut, False, getattr(r, f"fold{c}"))
        if cut:
            c = 2 + nt + t
            add_part(c, mat_f.at[t], r.fin_f.at[t], 0, cut, True, getattr(r, f"fold{c}"))

    def fold_of(c):
        return folds and parts[c].fold is not None

    def window(c, owner, which=0):
        part_c = parts[c]
        start = owner * dd + part_c.first + which * part_c.half
        return pl.ds(pl.multiple_of(start, 16), part_c.half)

    def fin_rows(c, which=0):
        part_c = parts[c]
        return pl.ds(pl.multiple_of(part_c.first + which * part_c.half, 16), part_c.half)

    def send_when(c, step, direct, other, defer):
        if not fold_of(c):
            direct()
            return
        away = []
        if step == dp - 1:
            pl.when(me == 0)(other)
            away.append(me == 0)
        if step == 1:
            pl.when(me == dp - 1)(other)
            away.append(me == dp - 1)
        if step == dp - 2:
            pl.when(me == 1)(defer)
            away.append(me == 1)
        if step == 2:
            pl.when(me == dp - 2)(defer)
            away.append(me == dp - 2)
        if not away:
            direct()
            return
        away = functools.reduce(jnp.logical_or, away)
        pl.when(jnp.logical_not(away))(direct)

    def fold_when(c, body):
        if not fold_of(c):
            return
        if dp == 4:
            pl.when((me == 1) | (me == 2))(lambda: body(2))
        else:
            pl.when(me == 1)(lambda: body(dp - 2))
            pl.when(me == dp - 2)(lambda: body(2))

    def end_when(c, body):
        if fold_of(c):
            pl.when(me == 0)(lambda: body(dp - 1))
            pl.when(me == dp - 1)(lambda: body(1))

    def taken(c, step, body):
        if fold_of(c) and step == dp - 1:
            pl.when(me != dp - 1)(body)
        elif fold_of(c) and step == 1:
            pl.when(me != 0)(body)
        else:
            body()

    def rs_y(c, p):
        part_c = parts[c]
        area = part_c.grad.at[window(c, p, peer)]
        return Copy(area, part_c.y_in.at[p], two.rsy, (c, p), {"ctx": peer})

    def z_out(c, step):
        if parts[c].direct:
            return parts[c].grad.at[window(c, dp_at(step))]
        return parts[c].y_in.at[dp_at(step)]

    def rs_z(c, step):
        slot = parts[c].z_in.at[step - 1]
        return Copy(z_out(c, step), slot, two.rsz, (c, step - 1), {"dp": dp_at(step)})

    def rs_fold(c, step):
        neighbour = 1 if step == dp - 1 else dp - 2
        return Copy(z_out(c, step), parts[c].fold, two.rsn, c, {"dp": neighbour})

    def rs_f(c):
        part_c = parts[c]
        if part_c.direct:
            return Copy(part_c.z_in.at[0], part_c.y_in, two.rsf, c, {"ctx": peer})
        area = part_c.fin.at[fin_rows(c, side)]
        return Copy(part_c.z_in.at[0], area, two.rsf, c, {"ctx": peer})

    def fin_copy(c):
        part_c = parts[c]
        if part_c.direct:
            area = part_c.fin.at[fin_rows(c)]
            return pltpu.make_async_copy(part_c.z_in.at[1], area, r.fin_sem.at[c])
        area = part_c.fin.at[fin_rows(c, side)]
        return pltpu.make_async_copy(part_c.z_in.at[0], area, r.fin_sem.at[c])

    steps = sorted(range(1, dp), key=lambda step: (step not in (1, dp - 1), step))

    def send_piece(c, step):
        send_when(
            c,
            step,
            lambda: rs_z(c, step).start(),
            lambda: rs_fold(c, step).start(),
            lambda: None,
        )

    def rs_start(c):
        if c not in parts:
            return
        if parts[c].direct:
            end_when(c, lambda step: rs_fold(c, step).start())
            if not fold_of(c) or c != 2 + nt:
                first_rest(c)
            return
        for step in steps + [0]:
            rs_y(c, dp_at(step)).start()

    def first_rest(c):
        for step in steps:
            send_when(c, step, lambda: rs_z(c, step).start(), lambda: None, lambda: None)

    def rows_done(c, i):
        if c in parts and rb % dd == 0:
            for k in range(rb // dd):
                rs_y(c, i * (rb // dd) + k).start()

    def rs_mid(c):
        if c not in parts:
            return
        part_c = parts[c]
        for step in steps + [0]:
            p = dp_at(step)
            rs_y(c, p).wait_recv()
            mine = part_c.grad[window(c, p, side), :].astype(F32)
            part_c.y_in[p] = (mine + part_c.y_in[p].astype(F32)).astype(BF16)
            if step:
                send_piece(c, step)

    def rs_join(c):
        if c not in parts:
            return
        part_c = parts[c]

        def one(step):
            rs_fold(c, dp - 1).wait_recv()
            extra = part_c.fold[...].astype(F32)
            p = dp_at(step)
            if part_c.direct:
                at = window(c, p)
                part_c.grad[at, :] = (part_c.grad[at, :].astype(F32) + extra).astype(BF16)
            else:
                part_c.y_in[p] = (part_c.y_in[p].astype(F32) + extra).astype(BF16)
            rs_z(c, step).start()

        fold_when(c, one)

    def blank(c):
        def zero(step):
            slot = parts[c].z_in
            slot[step - 1] = jnp.zeros(slot.shape[1:], BF16)

        if fold_of(c):
            pl.when(me == 0)(lambda: zero(1))
            pl.when(me == dp - 1)(lambda: zero(dp - 1))

    def rs_fin(c):
        if c not in parts:
            return
        part_c = parts[c]
        for step in range(1, dp):
            taken(c, step, lambda: rs_z(c, step).wait_recv())
        blank(c)
        if part_c.direct:
            total = part_c.grad[window(c, me), :].astype(F32)
        else:
            total = part_c.y_in[me].astype(F32)
        for step in range(1, dp):
            total += part_c.z_in[step - 1].astype(F32)
        part_c.z_in[0] = total.astype(BF16)
        rs_f(c).start()
        if not part_c.direct:
            fin_copy(c).start()

    def rs_last(c):
        if c not in parts:
            return
        part_c = parts[c]
        rs_f(c).wait_recv()
        total = part_c.z_in[0].astype(F32) + part_c.y_in[...].astype(F32)
        part_c.z_in[1] = total.astype(BF16)
        fin_copy(c).start()

    def rs_end(c):
        part_c = parts[c]
        for step in range(1, dp):
            wait = lambda: rs_z(c, step).wait_send()
            send_when(c, step, wait, lambda: None, wait)
        end_when(c, lambda step: rs_fold(c, step).wait_send())
        if not part_c.direct:
            for p in range(dp):
                rs_y(c, p).wait_send()
            rs_f(c).wait_recv()
        rs_f(c).wait_send()
        fin_copy(c).wait()

    def acc_low(source, target, s):
        def one(i):
            at = pl.ds(pl.multiple_of(s * local + i * tb, tb), tb)
            target[at, :] = source[at, :].astype(BF16)

        each(local // tb, one)

    for t in range(nt):
        ffn_rows(t, 0)
        if t == 0:
            spread_end(0, 1)
            transpose_into(hn, hn_t, local, local // tb)
            for c in range(4, nt + 2):
                serve(c)
        if t == 1 and fold_of(2 + nt):
            first_rest(2 + nt)
        if t == nt - 1:
            sum1_start(1, 0)
        if t == 2:
            rs_join(2 + nt)
        ffn_rows(t, 1)
        if t == nt - 1:
            sum1_start(1, 1)
            sum2_start(1, 0)
        ffn_weights(t)
        rs_start(2 + nt + t)
        if rb % dd:
            rs_start(2 + t)
        if t + 1 < nt:
            ag_end(2 + t + 1)
        if t == 0:
            pass

    def middle_back(s):
        incoming = sum_end(1, s)
        value = mid[share_at(s), :]
        factor = lax.rsqrt(mean_square(value) + EPSILON)
        hat = value * factor
        small[1:2, :] += jnp.sum(incoming * hat, axis=0, keepdims=True)
        grad_hat = incoming * r.gain_w[1:2, :]
        back = factor * (grad_hat - hat * jnp.mean(grad_hat * hat, axis=-1, keepdims=True))
        total = dy[token_rows(s, chip, core), :].astype(F32) + back
        grad_hidden[share_at(s), :] = total
        spread1_start(1, s, total.astype(BF16))

    def again(first, count):
        def one(i):
            at = pl.ds(pl.multiple_of(first + i * tb, tb), tb)
            value = x[at, :].astype(F32)
            value = value * lax.rsqrt(mean_square(value) + EPSILON)
            value = (value * r.gain_w[0:1, :]).astype(BF16).astype(F32)
            hn_t[:, at] = value.T.astype(BF16)

        each(count, one)

    sum2_start(1, 1)
    again(0, rows // tb)
    if nt < 3:
        rs_join(2 + nt)
    rs_mid(2)
    middle_back(0)
    middle_back(1)
    for s in range(seqs):
        acc_low(acc_m, part, s)
        sum1_start(3, s)
    spread2_start(1, 0)

    spread2_start(1, 1)
    for s in range(seqs):
        sum2_start(3, s)

    g_kv, gq_t = r.g_kv, r.gq_t

    def out_back(s):
        def one(i):
            at = pl.ds(pl.multiple_of(s * local + i * rb, rb), rb)
            value = dot(hn[at, :], mat_o[...])
            for h in range(qh):
                piece = value[:, h * head : (h + 1) * head]
                start = nqkv + h * 2 * head
                units[at, start : start + 2 * head] = jnp.concatenate(
                    [jnp.zeros_like(piece), piece], axis=1
                ).astype(BF16)

        each(local // rb, one)

    def attend_back(s, with_peer):
        for h in range(kh):
            g_kv[s * kh + h] = jnp.zeros_like(g_kv[s * kh + h])

        def one(index):
            for j in range(local // qb):
                parts, head_kv, here = masked(s, j, index, with_peer)
                at = slice(j * qb, (j + 1) * qb)
                token = slice(s * local + j * qb, s * local + (j + 1) * qb)
                lanes = pl.ds(pl.multiple_of(nqkv + index * 2 * head, 128), 2 * head)
                go = units[token, lanes]
                logs = lse[s * qh + index, :, at]
                probs = [jnp.exp(p[0] - logs) for p in parts]
                grad_probs = [dot_nt(kv[head_kv, w, :size, :], go) for _, w, size in parts]
                row_dot = sum(
                    jnp.sum(p * g, axis=0, keepdims=True) for p, g in zip(probs, grad_probs)
                )
                out = jnp.zeros((2 * head, qb), F32)
                for (_, w, size), p, g in zip(parts, probs, grad_probs):
                    gs = (p * (g - row_dot)).astype(BF16)
                    out += dot(kv_t[head_kv, w, :, :size], gs)
                    g_kv[head_kv, w, :size, :] += dot(gs, here) + dot(p.astype(BF16), go)
                spot = pl.ds(pl.multiple_of(index * head, head), head)
                gq_t[s, spot, at] = out[:head, :] * scale

        each(qh, one)

    def back_copy(s):
        return Copy(
            r.g_kv_low.at[pl.ds(s * kh, kh)],
            r.g_kv_in.at[pl.ds(s * kh, kh)],
            two.gkv,
            s,
            {"ctx": peer},
        )

    def attend_back_any(s):
        @pl.when(side == 0)
        def _():
            attend_back(s, False)

        @pl.when(side != 0)
        def _():
            attend_back(s, True)
            for h in range(kh):
                r.g_kv_low[s * kh + h] = g_kv[s * kh + h, 1].astype(BF16)
            back_copy(s).start()

    def kv_back_arrive(s):
        @pl.when(side == 0)
        def _():
            back_copy(s).wait_recv()
            for h in range(kh):
                g_kv[s * kh + h, 0] += r.g_kv_in[s * kh + h].astype(F32)

        @pl.when(side != 0)
        def _():
            back_copy(s).wait_send()

    def project_back(s):
        def one(i):
            at = pl.ds(pl.multiple_of(s * local + i * rb, rb), rb)
            inner = pl.ds(aligned(i, rb), rb)
            gkv = [g_kv[s * kh + h, 0, inner, :] for h in range(kh)]
            if kh == 1:
                g_key, g_value = gkv[0][:, :head], gkv[0][:, head:]
            else:
                keys, values = [], []
                for h in range(0, kh, 2):
                    keys.append(jnp.where(low_half, gkv[h], pltpu.roll(gkv[h + 1], head, 1)))
                    values.append(jnp.where(low_half, pltpu.roll(gkv[h], head, 1), gkv[h + 1]))
                g_key = jnp.concatenate(keys, axis=1)
                g_value = jnp.concatenate(values, axis=1)
            value = jnp.concatenate([gq_t[s, :, inner].T, g_key], axis=1)
            cosine = widen(tab[at, : 2 * head], nqk)
            sine = widen(tab[at, 2 * head :], nqk)
            value = value * cosine - swap_halves(value, head) * sine
            plain = raw[at, :]
            factor = lax.rsqrt(spread_means(plain * plain, head) + EPSILON)
            hat = plain * factor
            small[2:3, :nqk] += jnp.sum(value * hat, axis=0, keepdims=True)
            grad_hat = value * r.gain_h[0:1, :]
            value = factor * (grad_hat - hat * spread_means(grad_hat * hat, head))
            low = jnp.concatenate([value, g_value], axis=1).astype(BF16)
            units[at, :nqkv] = low
            part[at, :] = dot_nt(low, mat_q[...]).astype(BF16)

        each(local // rb, one)

    def out_weights():
        for i in range(width // rb):
            total = sum(
                dot(o_t[s], hn[s * local : (s + 1) * local, i * rb : (i + 1) * rb])
                for s in range(seqs)
            )
            r.grad_o[i * rb : (i + 1) * rb, :] = total.T.astype(BF16)

    def qkv_weights():
        def one(i):
            at = pl.ds(aligned(i, rb), rb)
            r.grad_q[at, :] = dot(hn_t[at, :], units[:, :nqkv]).astype(BF16)
            rows_done(0, i)

        each(width // rb, one)

    if nt > 1:
        rs_mid(3)
    rs_join(2)
    spread_end(1, 0)
    out_back(0)
    attend_back_any(0)
    spread_end(1, 1)
    out_back(1)
    rs_fin(2 + nt)
    rs_fin(2)
    if nt > 1:
        rs_join(3 + nt)
    attend_back_any(1)
    out_weights()
    rs_start(1)
    if nt > 1:
        rs_join(3)

    def mlp_end(s):
        mlp = sum_end(3, s)
        weight = keep_of(s)[:, 0:1]
        small[4:5, 384:512] += fold_lanes(weight * mlp * mlp)
        small[4:5, 512:640] += jnp.sum(keep_of(s), axis=0, keepdims=True)
        mid[share_at(s), :] += mlp

    if nt > 2:
        rs_mid(4)
        rs_join(4 + nt)
    for s in range(seqs):
        mlp_end(s)
    kv_back_arrive(0)
    project_back(0)
    sum1_start(2, 0)
    rs_last(2 + nt)
    if nt > 1:
        rs_fin(3 + nt)
    kv_back_arrive(1)
    project_back(1)
    sum1_start(2, 1)
    sum2_start(2, 0)
    qkv_weights()
    if rb % dd:
        rs_start(0)
    sum2_start(2, 1)
    if nt > 2:
        rs_join(4)
    if nt > 1:
        rs_fin(3)
    if nt > 2:
        rs_fin(4 + nt)
    rs_mid(1)

    def first_back(s):
        incoming = sum_end(2, s)
        value = x[token_rows(s, chip, core), :].astype(F32)
        factor = lax.rsqrt(mean_square(value) + EPSILON)
        hat = value * factor
        small[0:1, :] += jnp.sum(incoming * hat, axis=0, keepdims=True)
        grad_hat = incoming * r.gain_w[0:1, :]
        back = factor * (grad_hat - hat * jnp.mean(grad_hat * hat, axis=-1, keepdims=True))
        grad_hidden[share_at(s), :] += back

    first_back(0)
    first_back(1)
    rs_mid(0)

    small_in = r.small_in

    def small_round(start, copies, order):
        for c in copies:
            c.start()
        for c in copies:
            c.wait_recv()
            c.wait_send()
        total = None
        for o in order:
            term = small_in[start + o]
            total = term if total is None else total + term
        small[...] = total

    small_in[pl.ds(core, 1)] = small[...][None]
    small_round(
        0, [Copy(small, small_in.at[core], two.small, 0, {"tp": other_core})], range(2)
    )
    small_in[pl.ds(2 + side, 1)] = small[...][None]
    small_round(2, [Copy(small, small_in.at[2 + side], two.small, 1, {"ctx": peer})], range(2))
    small_in[pl.ds(4 + chip, 1)] = small[...][None]
    small_round(
        4,
        [
            Copy(small, small_in.at[4 + chip], two.small, 1 + s, {"tp": chip_lane(s)})
            for s in range(1, chips)
        ],
        range(chips),
    )
    rs_fin(1)
    if nt > 2:
        rs_fin(4)
        rs_last(4 + nt)
    small_in[pl.ds(4 + chips + me, 1)] = small[...][None]
    small_round(
        4 + chips,
        [
            Copy(small, small_in.at[4 + chips + me], two.small, chips + s, {"dp": dp_at(s)})
            for s in range(1, dp)
        ],
        range(dp),
    )
    def mine_of(value, size):
        return sum(
            jnp.where(me == d, value[:, d * size : (d + 1) * size], 0.0) for d in range(dp)
        )

    r.own_attn[...] = mine_of(small[0:1, :], dd)
    r.own_ffn[...] = mine_of(small[1:2, :], dd)
    row = small[2:3, :nqk]
    over_q = sum(row[:, h * head : (h + 1) * head] for h in range(qh))
    over_k = sum(row[:, h * head : (h + 1) * head] for h in range(qh, qh + kh))
    r.own_query[...] = mine_of(over_q, piece)
    r.own_key[...] = mine_of(over_k, piece)
    totals = [
        jnp.sum(small[4:5, i * 128 : (i + 1) * 128], axis=1, keepdims=True) for i in range(4)
    ]
    count = small[4:5, 512:513] * width
    r.own_stat[...] = jnp.sqrt(jnp.concatenate(totals, axis=1) / count)
    if nt > 1:
        rs_last(3 + nt)
    rs_fin(0)
    for c in sorted(parts, reverse=True):
        rs_end(c)


def per_device(
    sizes,
    hidden_states,
    out_grad,
    w_query,
    w_key,
    w_value,
    w_out,
    w_gate,
    w_up,
    w_down,
    attn_gain,
    ffn_gain,
    query_gain,
    key_gain,
    segment_ids,
    valid_mask,
    positions,
):
    seqs, local, width = hidden_states.shape
    dp, ctx, tp = sizes
    rows = seqs * local
    head = query_gain.shape[0] * dp
    nq, nk, units = w_query.shape[1], w_key.shape[1], w_gate.shape[1]
    nqkv = nq + 2 * nk
    nt = 3 if units % 3 == 0 else 1
    ft = units // nt
    dd = width // dp
    hd = dd // ctx
    share = local // tp
    chips = tp // 2
    qh, kh = nq // head, nk // head
    plain = ft % 128 == 0 and dd % 128 == 0 and nk % 128 == 0
    cuts = [dd if t < 1 else dd // 2 if t < 2 else 0 for t in range(nt)]
    cfg = types.SimpleNamespace(
        seqs=seqs, local=local, width=width, head=head, dp=dp, ctx=ctx, tp=tp,
        qh=qh, kh=kh, nt=nt, ft=ft, plain=plain, cuts=cuts,
    )
    gains = jnp.concatenate([attn_gain, ffn_gain, query_gain, key_gain])
    gains = gains.astype(F32).reshape(1, -1)
    half = head // 2
    freq = np.float32(ROPE_BASE) ** (-(np.arange(half, dtype=np.float32) * 2.0) / head)
    freq = jnp.asarray(np.tile(freq.astype(np.float32), 128 // half)[None])
    inputs = dict(
        x=(hidden_states.reshape(rows, width), True),
        dy=(out_grad.reshape(rows, width), True),
        gains=(gains, True),
        segment_ids=(segment_ids, True),
        valid_mask=(valid_mask, True),
        positions=(positions, True),
        freq=(freq, True),
    )
    if plain:
        inputs.update(
            w_query=(w_query, False),
            w_key=(w_key, False),
            w_value=(w_value, False),
            w_out=(w_out, False),
            w_gate=(w_gate, False),
            w_up=(w_up, False),
            w_down=(w_down, False),
        )
    else:
        tiles = []
        for i in range(nt):
            cut = slice(i * ft, (i + 1) * ft)
            tiles.append(jnp.concatenate([w_gate[:, cut], w_up[:, cut], w_down[cut].T], axis=1))
        inputs.update(
            w_qkv=(jnp.concatenate([w_query, w_key, w_value], axis=1), False),
            w_o=(w_out.T, False),
            w_f=(jnp.stack(tiles), False),
        )
    outputs = dict(
        result=((seqs * share, width), F32),
        grad_hidden=((seqs * share, width), F32),
        fin_q=((dd, nqkv), BF16),
        fin_o=((dd, nq), BF16),
        fin_f=((nt, dd, 3 * ft), BF16),
        own_attn=((1, dd), F32),
        own_ffn=((1, dd), F32),
        own_query=((1, head // dp), F32),
        own_key=((1, head // dp), F32),
        own_stat=((1, 4), F32),
    )
    scratch = dict(
        mat_q=((width, nqkv), BF16),
        mat_o=((width, nq), BF16),
        mat_f=((nt, width, 3 * ft), BF16),
        gain_buf=((dp, 1, 2 * dd + 2 * head // dp), F32),
        facts=((seqs, 2, local), F32),
        gain_w=((8, width), F32),
        gain_h=((8, nq + nk), F32),
        code_peer=((seqs, 2, local), F32),
        tab=((rows, 256), F32),
        key_code=((ctx, seqs, local, 128), F32),
        hn=((rows, width), BF16),
        hn_t=((width, rows), BF16),
        dr_t=((width, rows), BF16),
        raw=((rows, nq + nk), F32),
        q_pad=((seqs * qh, local, 2 * head), BF16),
        kv=((seqs * kh, ctx, local, 2 * head), BF16),
        kv_t=((seqs * kh, ctx, 2 * head, local), BF16),
        g_kv=((seqs * kh, ctx, local, 2 * head), F32),
        g_kv_low=((seqs * kh, local, 2 * head), BF16),
        g_kv_in=((seqs * kh, local, 2 * head), BF16),
        o_t=((seqs, nq, local), BF16),
        gq_t=((seqs, nq, local), F32),
        lse=((seqs * qh, 1, local), F32),
        part=((rows, width), BF16),
        near=((2, seqs, chips, share, width), BF16),
        pair=((seqs, chips, share, width), BF16),
        far=((2, seqs, max(chips - 1, 1), share, width), BF16),
        small=((8, width), F32),
        small_in=((4 + chips + dp, 8, width), F32),
        units=((rows, 3 * ft), BF16),
        acc_m=((rows, width), F32),
        acc_h=((rows, width), F32),
        grad_q=((width, nqkv), BF16),
        grad_o=((width, nq), BF16),
        y0=((dp, hd, nqkv), BF16),
        y1=((dp, hd, nq), BF16),
        z0=((dp - 1, hd, nqkv), BF16),
        z1=((dp - 1, hd, nq), BF16),
    )
    for t in range(nt):
        cut = cfg.cuts[t]
        if cut < dd:
            size = (dd - cut) // ctx
            scratch[f"y{2 + t}"] = ((dp, size, 3 * ft), BF16)
            scratch[f"z{2 + t}"] = ((dp - 1, size, 3 * ft), BF16)
            scratch[f"fold{2 + t}"] = ((size, 3 * ft), BF16)
        if cut:
            scratch[f"y{2 + nt + t}"] = ((cut, 3 * ft), BF16)
            scratch[f"z{2 + nt + t}"] = ((dp - 1, cut, 3 * ft), BF16)
            scratch[f"fold{2 + nt + t}"] = ((cut, 3 * ft), BF16)
    pairs = dict(
        agz=(nt + 2, dp - 1),
        agy=(nt + 2, dp - 1),
        gain=(dp - 1,),
        code=(1,),
        kv=(seqs,),
        gkv=(seqs,),
        sum1=(4, seqs * chips),
        sum2=(4, seqs * max(chips - 1, 1)),
        spread1=(2, seqs * max(chips - 1, 1)),
        spread2=(2, seqs * chips),
        rsy=(2 * nt + 2, dp),
        rsz=(2 * nt + 2, dp - 1),
        rsf=(2 * nt + 2,),
        small=(chips + dp,),
        rsn=(2 * nt + 2,),
    )
    singles = dict(own_sem=(nt + 2, 3), agfar=(nt + 2,), fin_sem=(2 * nt + 2,))
    shapes = list(singles.values()) + [v for v in pairs.values() for _ in range(2)]

    def kernel(*refs):
        refs = list(refs)
        r = types.SimpleNamespace()
        for name in list(inputs) + list(outputs) + list(scratch) + list(singles):
            setattr(r, name, refs.pop(0))
        two = types.SimpleNamespace()
        for name in pairs:
            setattr(two, name, (refs.pop(0), refs.pop(0)))
        block_kernel(cfg, r, two)

    vmem = pl.BlockSpec(memory_space=pltpu.VMEM)
    away = pl.BlockSpec(memory_space=pl.ANY)
    out = pl.pallas_call(
        kernel,
        out_shape=[jax.ShapeDtypeStruct(*v) for v in outputs.values()],
        in_specs=[vmem if v else away for _, v in inputs.values()],
        out_specs=[away if n.startswith("fin") else vmem for n in outputs],
        scratch_shapes=[pltpu.VMEM(*v) for v in scratch.values()]
        + [pltpu.SemaphoreType.DMA(v) for v in shapes],
        compiler_params=pltpu.CompilerParams(
            collective_id=0, has_side_effects=True, vmem_limit_bytes=VMEM_LIMIT
        ),
    )(*[v for v, _ in inputs.values()])
    result, grad_hidden, fin_q, fin_o, fin_f = out[:5]

    gates = [fin_f[i, :, :ft] for i in range(nt)]
    ups = [fin_f[i, :, ft : 2 * ft] for i in range(nt)]
    downs = [fin_f[i, :, 2 * ft :] for i in range(nt)]
    return (
        result.reshape(seqs, share, width),
        grad_hidden.reshape(seqs, share, width),
        fin_q[:, :nq].astype(F32),
        fin_q[:, nq : nq + nk].astype(F32),
        fin_q[:, nq + nk :].astype(F32),
        fin_o.T.astype(F32),
        jnp.concatenate(gates, axis=1).astype(F32),
        jnp.concatenate(ups, axis=1).astype(F32),
        jnp.concatenate([d.T for d in downs], axis=0).astype(F32),
        *[value.reshape(-1) for value in out[5:]],
    )


VMEM_LIMIT = 63 * 2**20


def solution(mesh):
    sizes = tuple(mesh.shape[a] for a in ("dp", "ctx", "tp"))
    return jax.shard_map(
        functools.partial(per_device, sizes),
        mesh=mesh,
        in_specs=(
            P("dp", "ctx", None),
            P("dp", "ctx", None),
            P("dp", "tp"),
            P("dp", "tp"),
            P("dp", "tp"),
            P("tp", "dp"),
            P("dp", "tp"),
            P("dp", "tp"),
            P("tp", "dp"),
            P("dp"),
            P("dp"),
            P("dp"),
            P("dp"),
            P("dp", "ctx"),
            P("dp", "ctx"),
            P("dp", "ctx"),
        ),
        out_specs=(
            P("dp", ("ctx", "tp"), None),
            P("dp", ("ctx", "tp"), None),
            P("dp", "tp"),
            P("dp", "tp"),
            P("dp", "tp"),
            P("tp", "dp"),
            P("dp", "tp"),
            P("dp", "tp"),
            P("tp", "dp"),
            P("dp"),
            P("dp"),
            P("dp"),
            P("dp"),
            P(),
        ),
        check_vma=False,
    )
```
